128 devices in a mesh: row: 16 (over x, y_lo, core), col: 8 (over y_hi, z).
Axes of the slice: x: 4, y: 4 (y_hi: 2, y_lo: 2; y = y_hi * 2 + y_lo), z: 4, core: 2. Of those that a mesh axis runs over, the one named last changes fastest.
Arguments:
- features: bfloat16 [128, 1024, 3072], P('row', 'col'), may hold values from -6 to 6
- enc_weight: bfloat16 [3072, 64], replicated, may hold values from -0.4375 to 0.4375
- dec_weight: bfloat16 [3072, 64], replicated, may hold values from -0.75 to 0.75
- disc_weight: float32 [64, 64], replicated, may hold values from -0.75 to 0.75
- send_order: int32 [16, 8, 1024], P('row', 'col'), may hold values from 0 to 1023, each once within a row
- recv_order: int32 [16, 8, 1024], P('row', 'col'), may hold values from 0 to 1023, each once within a row
Outputs:
- enc_out: float32 [3072, 64], P(('row', 'col'))
- dec_out: float32 [3072, 64], P(('row', 'col'))
- disc_out: float32 [64, 64], replicated
- embedded_out: float32 [64, 128, 1024], P(None, 'row', 'col')
- logits: float32 [4, 128, 1024], P(None, 'row', 'col')
- proj_grad: bfloat16 [2, 64, 128, 1024], P(None, None, 'row', 'col')
The draws below stay inside these ranges and needn't reach their ends.
Inputs may be any that keep to these rules, and one draw needn't show every extreme that they name: `send_order`: each device's row of 1024 entries holds every local bin number exactly once. `recv_order`: each device's row of 1024 entries holds every position exactly once.
All inputs are finite; a program needn't handle non-finite values.
Results may differ from the reference program's by a relative error of at most 0.0055.
Values may be sent and summed in bfloat16 or wider, within the bound.
A program may use at most 128 MiB of HBM per device.

```python
import math
import jax
import jax.numpy as jnp
from jax import lax

G = 3072
LAT = 64
TR = 8
TC = 128
RADIUS = 3
BINS = 1024
NR = 128
NC = 1024
N_ROW = 16
N_COL = 8
DEVICES = 128


def strengthened(values, stream_key, source, target, parts, factor):
    def block_of(position):
        return (jnp.arange(values.shape[position]) // (values.shape[position] // parts)).reshape((-1,) + (1,) * (values.ndim - 1 - position))

    near = jax.random.permutation(stream_key, parts)[block_of(target)]
    other_side = (block_of(target) + parts // 2) % parts
    return jnp.where((block_of(source) == near) | (block_of(source) == other_side), factor * values, values)


def steps_of(key, dims, cuts, smallest, high):
    factor_of, own = 1.0, jax.random.fold_in(key, 6)
    for dim, blocks in cuts:
        draws = jnp.exp(jax.random.uniform(jax.random.fold_in(own, dim), (blocks,), jnp.float32, smallest / len(cuts), high / len(cuts)))
        factor_of = factor_of * jnp.repeat(draws, dims[dim] // blocks).reshape([-1 if axis == dim else 1 for axis in range(len(dims))])
    return factor_of


def scatter_about(own_key, extent, scale, bound, pieces=(), held_as=jnp.bfloat16):
    values = jax.random.normal(own_key, extent, jnp.float32) * scale
    if len(pieces) > 0:
        values = steps_of(own_key, extent, pieces, -0.22, 0.18) * values
    return jnp.clip(values, min=-bound, max=bound).astype(held_as)


def heavy_noise(rng, dims, scale, most, pieces, heavy, kind=jnp.bfloat16):
    entries = scale * jax.random.normal(rng, dims, jnp.float32)
    if pieces:
        entries = entries * steps_of(rng, dims, pieces, -0.22, 0.18)
    return jnp.clip(strengthened(entries, jax.random.fold_in(rng, 3), *heavy), -most, most).astype(kind)


def setup_inputs(seed: int = 0) -> dict:
    arg_keys = jax.random.split(jax.random.key(seed), 7)
    features = heavy_noise(arg_keys[0], (NR, NC, G), 1.0, 6.0, ((0, 16), (1, 8)), (0, 2, 16, 2.0))
    enc_weight = scatter_about(arg_keys[1], (G, LAT), (G // 16) ** -0.5, 0.4375)
    dec_weight = scatter_about(arg_keys[2], (G, LAT), LAT ** -0.5, 0.75)
    disc_weight = scatter_about(arg_keys[3], (LAT, LAT), LAT ** -0.5, 0.75, (), jnp.float32)
    send_order = jax.vmap(lambda own: jax.random.permutation(own, BINS))(jax.random.split(arg_keys[4], N_ROW * N_COL)).reshape((N_ROW, N_COL, BINS)).astype(jnp.int32)
    recv_order = jax.vmap(lambda own: jax.random.permutation(own, BINS))(jax.random.split(arg_keys[5], N_ROW * N_COL)).reshape((N_ROW, N_COL, BINS)).astype(jnp.int32)
    return dict(features=features, enc_weight=enc_weight, dec_weight=dec_weight, disc_weight=disc_weight, send_order=send_order, recv_order=recv_order)


RECON_WEIGHT = 10.0

def stencil_taps():
    raw_taps = [math.exp(-offset * offset / 12.0) for offset in range(-RADIUS, RADIUS + 1)]
    tap_total = sum(raw_taps)
    return [raw_value / tap_total for raw_value in raw_taps]

def smooth_padded(padded, height_count, width_count):
    tap_list = stencil_taps()
    across = tap_list[0] * padded[..., 0:height_count, :]
    for offset in range(1, 2 * RADIUS + 1):
        across = across + tap_list[offset] * padded[..., offset:offset + height_count, :]
    result = tap_list[0] * across[..., :, 0:width_count]
    for offset in range(1, 2 * RADIUS + 1):
        result = result + tap_list[offset] * across[..., :, offset:offset + width_count]
    return result

def smooth_whole(grid_field):
    widths = [(0, 0)] * (grid_field.ndim - 2) + [(RADIUS, RADIUS), (RADIUS, RADIUS)]
    return smooth_padded(jnp.pad(grid_field, widths), NR, NC)

def to_devices(grid_field):
    leading = grid_field.shape[0]
    grid_view = grid_field.reshape(leading, N_ROW, TR, N_COL, TC)
    return grid_view.transpose(0, 1, 3, 2, 4).reshape(leading, DEVICES * TR * TC)

def from_devices(flat_field):
    leading = flat_field.shape[0]
    grid_view = flat_field.reshape(leading, N_ROW, N_COL, TR, TC)
    return grid_view.transpose(0, 1, 3, 2, 4).reshape(leading, NR, NC)

def source_map_of(send_order, recv_order):
    portion = TR * TC // DEVICES
    sending = send_order.reshape(DEVICES, TR * TC)
    receiving = recv_order.reshape(DEVICES, TR * TC)
    target = jnp.arange(DEVICES, dtype=jnp.int32)[:, None]
    source = receiving // portion
    within = receiving % portion
    anchor = sending[source, target * portion + within]
    return (source * (TR * TC) + anchor).reshape(-1).astype(jnp.int32)

def elu_slope(grid_field):
    return jnp.where(grid_field > 0, jnp.ones_like(grid_field), jnp.exp(jnp.minimum(grid_field, 0.0)))

def reference(features, enc_weight, dec_weight, disc_weight, send_order, recv_order):
    flat_all = features.reshape(NR * NC, G)
    projected = jnp.dot(flat_all, enc_weight, preferred_element_type=jnp.float32).astype(jnp.bfloat16)
    projected = projected.T.reshape(LAT, NR, NC)
    source_map = source_map_of(send_order, recv_order)
    scrambled = from_devices(to_devices(projected)[:, source_map])
    stacked = jnp.stack([projected, scrambled]).astype(jnp.float32)
    latent = smooth_whole(stacked)
    embedded = jax.nn.elu(latent)
    spread = smooth_whole(embedded)
    summary = jax.nn.sigmoid(spread)
    spread_low = spread[0].astype(jnp.bfloat16)
    strips = jnp.arange(N_ROW, dtype=jnp.int32)

    def recon_strip(strip_index):
        first_row = strip_index * TR
        segment_x = lax.dynamic_slice_in_dim(features, first_row, TR, 0).reshape(TR * NC, G)
        segment_f = lax.dynamic_slice_in_dim(spread_low, first_row, TR, 1).reshape(LAT, TR * NC)
        rebuilt = jnp.dot(segment_f.T, dec_weight.T, preferred_element_type=jnp.float32)
        residual = rebuilt - segment_x.astype(jnp.float32)
        rec_slope = (2.0 * RECON_WEIGHT / G * residual).astype(jnp.bfloat16)
        rec_back = jnp.dot(dec_weight.T, rec_slope.T, preferred_element_type=jnp.float32)
        dec_part = jnp.dot(rec_slope.T, segment_f.T, preferred_element_type=jnp.float32)
        return (rec_back.reshape(LAT, TR, NC), dec_part)
    back_parts, dec_parts = lax.map(recon_strip, strips)
    rec_back = back_parts.transpose(1, 0, 2, 3).reshape(LAT, NR, NC)
    dec_grad = lax.optimization_barrier(jnp.sum(dec_parts, axis=0))
    highest = lax.Precision.HIGHEST
    queries = jnp.einsum('kl,blrc->bkrc', disc_weight, summary, precision=highest)
    logit_pos = lax.optimization_barrier(jnp.sum(embedded[0] * queries[0], axis=0))
    logit_neg = lax.optimization_barrier(jnp.sum(embedded[1] * queries[0], axis=0))
    logit_cpos = lax.optimization_barrier(jnp.sum(embedded[1] * queries[1], axis=0))
    logit_cneg = lax.optimization_barrier(jnp.sum(embedded[0] * queries[1], axis=0))
    logits = jnp.stack([logit_pos, logit_neg, logit_cpos, logit_cneg])
    grad_pos = -jax.nn.sigmoid(-logit_pos)
    grad_neg = jax.nn.sigmoid(logit_neg)
    grad_cpos = -jax.nn.sigmoid(-logit_cpos)
    grad_cneg = jax.nn.sigmoid(logit_cneg)
    embed_grad = jnp.stack([grad_pos * queries[0] + grad_cneg * queries[1], grad_neg * queries[0] + grad_cpos * queries[1]])
    query_grad = jnp.stack([grad_pos * embedded[0] + grad_neg * embedded[1], grad_cpos * embedded[1] + grad_cneg * embedded[0]])
    disc_grad = jnp.einsum('bkrc,blrc->kl', query_grad, summary, precision=highest)
    summary_grad = jnp.einsum('kl,bkrc->blrc', disc_weight, query_grad, precision=highest)
    spread_grad = summary_grad * summary * (1.0 - summary)
    spread_grad = spread_grad.at[0].add(rec_back)
    embed_total = embed_grad + smooth_whole(spread_grad)
    latent_grad = embed_total * elu_slope(latent)
    proj_grad = smooth_whole(latent_grad).astype(jnp.bfloat16)
    restored = jnp.zeros((LAT, DEVICES * TR * TC), jnp.bfloat16).at[:, source_map].set(to_devices(proj_grad[1]))
    restored = from_devices(restored)

    def enc_strip(strip_index):
        first_row = strip_index * TR
        segment_x = lax.dynamic_slice_in_dim(features, first_row, TR, 0).reshape(TR * NC, G)
        own_part = lax.dynamic_slice_in_dim(proj_grad[0], first_row, TR, 1).reshape(LAT, TR * NC)
        moved_part = lax.dynamic_slice_in_dim(restored, first_row, TR, 1).reshape(LAT, TR * NC)
        combined = jnp.concatenate([own_part, moved_part], axis=0)
        product_term = jnp.dot(combined, segment_x, preferred_element_type=jnp.float32)
        return product_term[:LAT] + product_term[LAT:]
    enc_grad = lax.optimization_barrier(jnp.sum(lax.map(enc_strip, strips), axis=0)).T
    enc_out = enc_grad * lax.rsqrt(jnp.mean(enc_grad * enc_grad) + 1e-06)
    dec_out = dec_grad * lax.rsqrt(jnp.mean(dec_grad * dec_grad) + 1e-06)
    disc_out = disc_grad * lax.rsqrt(jnp.mean(disc_grad * disc_grad) + 1e-06)
    return (enc_out, dec_out, disc_out, embedded[0], logits, proj_grad)
```

```python
import functools
import math

import jax
import jax.numpy as jnp
from jax import lax
from jax.experimental import pallas as pl
from jax.experimental.pallas import tpu as pltpu
from jax.sharding import PartitionSpec as P

RADIUS = 3
RECON_WEIGHT = 10.0
LANES = 128
EDGE = 16
SIDE = 8
MESH = pl.DeviceIdType.MESH
F32 = jnp.float32
BF16 = jnp.bfloat16
DIRECTIONS = ((-1, 0), (1, 0), (0, -1), (0, 1), (-1, -1), (-1, 1), (1, -1), (1, 1))
OPPOSITE = (1, 0, 3, 2, 7, 6, 5, 4)
ROUNDS = 5
PACKED = {0: 0, 2: 1}
CHUNKS = 4


def stencil_taps():
    raw_taps = [math.exp(-offset * offset / 12.0) for offset in range(-RADIUS, RADIUS + 1)]
    tap_total = sum(raw_taps)
    return [raw_value / tap_total for raw_value in raw_taps]


def dot(a, b, ca=1, cb=0):
    return lax.dot_general(a, b, (((ca,), (cb,)), ((), ())), preferred_element_type=F32)


def split_2(value):
    high = value.astype(BF16)
    low = (value - high.astype(F32)).astype(BF16)
    return jnp.concatenate([high, low], axis=1)


def kernel(
    n_row,
    n_col,
    feat_hbm,
    enc_hbm,
    dec_hbm,
    disc_hbm,
    send_hbm,
    recv_hbm,
    enc_hbm_out,
    dec_hbm_out,
    disc_hbm_out,
    emb_hbm_out,
    log_hbm_out,
    pg_hbm_out,
    enc_out,
    dec_out,
    disc_out,
    emb_out,
    log_out,
    pg_out,
    x,
    discw,
    orders,
    wcat,
    wtwice,
    gram2,
    bd_nt,
    bd_nn,
    send_pick,
    recv_pick,
    recv_pick_t,
    xp,
    xp_low,
    ex_src,
    ex_dst,
    pads,
    tmp,
    hsrc,
    h_row,
    h_col,
    h_corner,
    pack_src,
    h_pack,
    lat,
    emb,
    spread,
    summ,
    s_low,
    back,
    grads_2,
    summ_2,
    mix,
    eg,
    pg_low,
    lt,
    own,
    rs1_src,
    rs1_dst,
    rs2_src,
    rs2_dst,
    disc_src,
    disc_a,
    disc_bsrc,
    disc_b,
    disc_full,
    norm_src,
    norm_a,
    norm_bsrc,
    norm_b,
    stage,
    dec_sum,
    load_sem,
    feat_sem,
    hs_sem,
    hr_sem,
    as_sem,
    ar_sem,
    r1s_sem,
    r1r_sem,
    r2s_sem,
    r2r_sem,
    ds_sem,
    dr_sem,
    ns_sem,
    nr_sem,
    meet_sem,
    out_sem,
):
    n_dev = n_row * n_col
    bins, genes = x.shape
    rows = bins // LANES
    lats = discw.shape[1]
    portion = bins // n_dev
    n_group = n_row // 2
    n_pair = n_group // 2
    per_dev = genes // n_dev
    span = genes // n_group
    per_group = 2 * n_col
    part = lats // n_col
    slope_scale = 2.0 * RECON_WEIGHT / genes
    tap = stencil_taps()
    chunk = bins // CHUNKS

    r = lax.axis_index("row")
    c = lax.axis_index("col")
    me = r * n_col + c
    my_group = r // 2
    lane = lax.broadcasted_iota(jnp.int32, (1, LANES), 1)
    first = lane < lats

    outs = [
        pltpu.make_async_copy(a, b, out_sem.at[i])
        for i, (a, b) in enumerate(
            [
                (enc_out, enc_hbm_out),
                (dec_out, dec_hbm_out),
                (disc_out, disc_hbm_out),
                (emb_out, emb_hbm_out),
                (log_out, log_hbm_out),
                (pg_out, pg_hbm_out),
            ]
        )
    ]

    def swap(value):
        return pltpu.roll(value, lats, value.ndim - 1)

    def halo_buffer(turn, way):
        if way < 2:
            return h_row.at[turn, way]
        if way < 4:
            return h_col.at[turn, way - 2]
        return h_corner.at[turn, way - 4]

    def halo_copy(turn, way):
        dr, dc = DIRECTIONS[way]
        row_part = pl.ds(0, RADIUS) if dr < 0 else pl.ds(rows - RADIUS, RADIUS) if dr else pl.ds(0, rows)
        col_part = pl.ds(0, EDGE) if dc < 0 else pl.ds(LANES - EDGE, EDGE) if dc else pl.ds(0, LANES)
        if way < 2 and turn in PACKED:
            source = pack_src.at[PACKED[turn], way]
            target = h_pack.at[PACKED[turn], OPPOSITE[way]]
        else:
            source = hsrc.at[turn, row_part, col_part]
            target = halo_buffer(turn, OPPOSITE[way])
        return pltpu.make_async_remote_copy(
            src_ref=source,
            dst_ref=target,
            send_sem=hs_sem.at[turn, way],
            recv_sem=hr_sem.at[turn, OPPOSITE[way]],
            device_id=(r + dr, c + dc),
            device_id_type=MESH,
        )

    def present(way):
        dr, dc = DIRECTIONS[way]
        tests = []
        if dr < 0:
            tests.append(r > 0)
        if dr > 0:
            tests.append(r < n_row - 1)
        if dc < 0:
            tests.append(c > 0)
        if dc > 0:
            tests.append(c < n_col - 1)
        return functools.reduce(jnp.logical_and, tests)

    def halo_start(turn):
        for way in range(8):

            @pl.when(present(way))
            def _():
                halo_copy(turn, way).start()

    def halo_take(turn):
        pad = pads.at[turn % 2]
        for way in range(8):

            @pl.when(present(way))
            def _():
                halo_copy(turn, OPPOSITE[way]).wait_recv()

        left, right = slice(0, SIDE), slice(SIDE + LANES, LANES + 2 * SIDE)
        top, bottom = slice(0, RADIUS), slice(RADIUS + rows, rows + 2 * RADIUS)
        for way, part in ((0, top), (1, bottom)):
            if turn in PACKED:
                packed = h_pack[PACKED[turn], way].astype(F32)
                halves = (packed, swap(packed)) if turn == 0 else (swap(packed), packed)
                pad[part, SIDE : SIDE + LANES // 2, :] = halves[0]
                pad[part, SIDE + LANES // 2 : SIDE + LANES, :] = halves[1]
            else:
                pad[part, SIDE : SIDE + LANES, :] = h_row[turn, way].astype(F32)
            pad[part, left, :] = h_corner[turn, 2 * way].astype(F32)[:, EDGE - SIDE :, :]
            pad[part, right, :] = h_corner[turn, 2 * way + 1].astype(F32)[:, :SIDE, :]
        own_rows = slice(RADIUS, RADIUS + rows)
        pad[own_rows, left, :] = h_col[turn, 0].astype(F32)[:, EDGE - SIDE :, :]
        pad[own_rows, right, :] = h_col[turn, 1].astype(F32)[:, :SIDE, :]

    def halo_finish(turn):
        for way in range(8):

            @pl.when(present(way))
            def _():
                halo_copy(turn, way).wait_send()

    def stencil(turn, then):
        pad = pads.at[turn % 2]
        for t in range(0, LANES + 2 * SIDE, SIDE):
            block = pad[:, t : t + SIDE, :]
            across = tap[RADIUS] * block[RADIUS : RADIUS + rows]
            for k in range(1, RADIUS + 1):
                across += tap[RADIUS + k] * (
                    block[RADIUS - k : RADIUS - k + rows] + block[RADIUS + k : RADIUS + k + rows]
                )
            tmp[:, t : t + SIDE, :] = across
        for i in range(rows):
            total = tap[RADIUS] * tmp[i, SIDE : SIDE + LANES, :]
            for k in range(1, RADIUS + 1):
                total += tap[RADIUS + k] * (
                    tmp[i, SIDE - k : SIDE - k + LANES, :] + tmp[i, SIDE + k : SIDE + k + LANES, :]
                )
            then(i, total)

    def put(turn, i, value):
        pads[turn % 2, i + RADIUS, SIDE : SIDE + LANES, :] = value
        low = value.astype(BF16)
        if turn not in PACKED:
            hsrc[turn, i] = low
            return
        hsrc[turn, i, 0:EDGE, :] = low[0:EDGE, :]
        hsrc[turn, i, LANES - EDGE :, :] = low[LANES - EDGE :, :]
        front, rear = value[: LANES // 2, :], value[LANES // 2 :, :]
        if turn == 0:
            packed = jnp.where(first, front, swap(rear)).astype(BF16)
        else:
            packed = jnp.where(first, swap(front), rear).astype(BF16)
        if i < RADIUS:
            pack_src[PACKED[turn], 0, i] = packed
        if i >= rows - RADIUS:
            pack_src[PACKED[turn], 1, i - (rows - RADIUS)] = packed

    loads = [
        pltpu.make_async_copy(a, b, load_sem.at[i])
        for i, (a, b) in enumerate(
            [
                (send_hbm, orders.at[0]),
                (recv_hbm, orders.at[1]),
                (dec_hbm, wcat.at[pl.ds(0, lats)]),
                (enc_hbm, wcat.at[pl.ds(lats, lats)]),
                (dec_hbm, wtwice.at[pl.ds(0, lats)]),
                (dec_hbm, wtwice.at[pl.ds(lats, lats)]),
                (disc_hbm, discw),
            ]
        )
    ]
    for load in loads[:4]:
        load.start()
    feats = []
    for i in range(rows):
        piece = pl.ds(i * LANES, LANES)
        copy = pltpu.make_async_copy(feat_hbm.at[piece], x.at[piece], feat_sem.at[i])
        copy.start()
        feats.append(copy)
    for load in loads[4:]:
        load.start()

    barrier = pltpu.get_barrier_semaphore()

    def greet_row(k, carry):
        other = lax.rem(r + k, n_row)
        pl.semaphore_signal(barrier, inc=1, device_id=(other, c), device_id_type=MESH)
        return carry

    def greet_col(k, carry):
        other = lax.rem(c + k, n_col)
        pl.semaphore_signal(barrier, inc=1, device_id=(r, other), device_id_type=MESH)
        return carry

    lax.fori_loop(1, n_row, greet_row, 0)
    lax.fori_loop(1, n_col, greet_col, 0)

    def build_send():
        for a in range(rows):
            line = orders[0, a : a + 1, :].astype(F32)
            column = jnp.broadcast_to(line, (LANES, LANES)).T
            for t in range(rows):
                index = (lane + t * LANES).astype(F32)
                send_pick[a * LANES : (a + 1) * LANES, t * LANES : (t + 1) * LANES] = jnp.where(
                    column == index, 1.0, 0.0
                ).astype(BF16)

    def build_recv():
        def body(a, carry):
            line = orders[1, pl.ds(a, 1), :].astype(F32)
            column = jnp.broadcast_to(line, (LANES, LANES)).T
            for t in range(rows):
                index = (lane + t * LANES).astype(F32)
                recv_pick[
                    pl.ds(pl.multiple_of(a * LANES, LANES), LANES), t * LANES : (t + 1) * LANES
                ] = jnp.where(column == index, 1.0, 0.0).astype(BF16)
            return carry

        lax.fori_loop(0, rows, body, 0)

    def build_recv_t():
        def body(t, carry):
            index = (lax.broadcasted_iota(jnp.int32, (LANES, 1), 0) + t * LANES).astype(F32)
            for a in range(rows):
                line = orders[1, a : a + 1, :].astype(F32)
                recv_pick_t[
                    pl.ds(pl.multiple_of(t * LANES, LANES), LANES), a * LANES : (a + 1) * LANES
                ] = jnp.where(line == index, 1.0, 0.0).astype(BF16)
            return carry

        lax.fori_loop(0, rows, body, 0)

    def ex_copy(which, k):
        other = lax.rem(me + k, n_dev)
        return pltpu.make_async_remote_copy(
            src_ref=ex_src.at[which, other],
            dst_ref=ex_dst.at[which, me],
            send_sem=as_sem.at[which],
            recv_sem=ar_sem.at[which],
            device_id=(other // n_col, lax.rem(other, n_col)),
            device_id_type=MESH,
        )

    def peers(count, make):
        def body(k, carry):
            make(k).start()
            return carry

        lax.fori_loop(1, count, body, 0)

    def drain(ref, count, send_sem, recv_sem):
        most = ref.at[pl.ds(0, count - 1)]
        pltpu.make_async_copy(most, most, recv_sem).wait()
        pltpu.make_async_copy(most, most, send_sem).wait()

    def ex_start(which):
        peers(n_dev, functools.partial(ex_copy, which))
        ex_dst[which, me] = ex_src[which, me]

    def ex_wait(which):
        drain(ex_dst.at[which], n_dev, as_sem.at[which], ar_sem.at[which])
        return ex_dst[which].reshape(bins, LANES)

    rs2_src[...] = jnp.zeros_like(rs2_src)
    loads[0].wait()
    loads[1].wait()
    build_send()
    for way in range(8):

        @pl.when(jnp.logical_not(present(way)))
        def _():
            for turn in range(ROUNDS):
                if way < 2 and turn in PACKED:
                    empty = h_pack.at[PACKED[turn], way]
                else:
                    empty = halo_buffer(turn, way)
                empty[...] = jnp.zeros_like(empty)

    loads[2].wait()
    loads[3].wait()

    for i in range(2):
        for k in range(rows // 2):
            feats[i * (rows // 2) + k].wait()
        piece = slice(i * (bins // 2), (i + 1) * (bins // 2))
        acc = dot(x[piece, :], wcat[...], 1, 1)
        xp[piece, :] = acc
        xp_low[piece, :] = acc.astype(BF16)
    outgoing = dot(send_pick[...], xp_low[...])
    ex_src[0] = outgoing.astype(BF16).reshape(n_dev, portion, LANES)

    pl.semaphore_wait(barrier, n_row + n_col - 2)

    def greet_meet(k, carry):
        other = lax.rem(c + k, n_col)
        pl.semaphore_signal(meet_sem, inc=1, device_id=(r, other), device_id_type=MESH)
        return carry

    lax.fori_loop(1, n_col, greet_meet, 0)
    pl.semaphore_wait(meet_sem, n_col - 1)

    ex_start(0)

    for i in range(rows):
        piece = slice(i * LANES, (i + 1) * LANES)
        put(0, i, swap(xp_low[piece, :].astype(F32)))
    halo_start(0)
    build_recv()
    def elu(value):
        return jnp.where(value > 0, value, jnp.exp(jnp.minimum(value, 0.0)) - 1.0)

    def first_latent(i, value):
        lat[i] = value
        emb[i] = elu(value)

    halo_take(0)
    stencil(0, first_latent)

    scrambled = dot(recv_pick[...], ex_wait(0))
    for i in range(rows):
        put(1, i, jnp.where(first, emb[i], scrambled[i * LANES : (i + 1) * LANES, :]))
    halo_start(1)
    build_recv_t()
    gram = dot(wcat[0:lats, :], wcat[0:lats, :], 1, 1)
    gram_high = gram.astype(BF16)
    gram_low = (gram - gram_high.astype(F32)).astype(BF16)
    gram2[...] = jnp.zeros_like(gram2)
    gram2[0:lats, 0:lats] = gram_high
    gram2[lats:, 0:lats] = gram_low

    def first_spread(i, value):
        out = elu(value)
        lat[i] = jnp.where(first, lat[i], value)
        emb[i] = jnp.where(first, emb[i], out)
        put(2, i, out)
        spread[i] = value

    halo_take(1)
    stencil(1, first_spread)
    halo_start(2)
    for i in range(rows):
        value = spread[i]
        here = slice(i * LANES, (i + 1) * LANES)
        low = value.astype(BF16).astype(F32)
        summ[i] = jax.nn.sigmoid(value)
        s_low[here, :] = jnp.where(first, low, swap(low)).astype(BF16)
        lt[0:lats, here] = low.T[0:lats, :].astype(BF16)

    back[...] = slope_scale * (
        dot(s_low[...], gram2[...]) - jnp.where(first, xp[...], 0.0)
    )

    def rs1_copy(which, group):
        return pltpu.make_async_remote_copy(
            src_ref=rs1_src.at[which, group],
            dst_ref=rs1_dst.at[which, my_group],
            send_sem=r1s_sem.at[which],
            recv_sem=r1r_sem.at[which],
            device_id=(2 * group + lax.rem(r, 2), c),
            device_id_type=MESH,
        )

    def rs1_run(which, product):
        for k in range(n_pair):
            pair = lax.rem(my_group // 2 + 1 + k, n_pair)
            where = pl.ds(pl.multiple_of(pair * (2 * span), LANES), 2 * span)
            value = product(where).astype(BF16)
            for j in range(2):
                rs1_src[which, 2 * pair + j] = value[:, j * span : (j + 1) * span]
            if k < n_pair - 1:
                for j in range(2):
                    rs1_copy(which, 2 * pair + j).start()
            else:
                rs1_copy(which, my_group + 1 - 2 * lax.rem(my_group, 2)).start()

    def rs1_finish(which):
        seven = rs1_dst.at[which, pl.ds(0, n_group - 1)]
        pltpu.make_async_copy(seven, seven, r1r_sem.at[which]).wait()
        pltpu.make_async_copy(seven, seven, r1s_sem.at[which]).wait()
        rs1_dst[which, my_group] = rs1_src[which, my_group]
        total = rs1_dst[which, 0].astype(F32)
        for group in range(1, n_group):
            total += rs1_dst[which, group].astype(F32)
        for k in range(span // LANES):
            rs2_src[which, k * LANES : (k + 1) * LANES, 0:lats] = total[
                :, k * LANES : (k + 1) * LANES
            ].T

    mine = lax.rem(r, 2) * n_col + c

    def gene_part(index):
        return pl.ds(pl.multiple_of(index * per_dev, 8), per_dev)

    def rs2_start(which):
        def body(k, carry):
            other = lax.rem(mine + k, per_group)
            pltpu.make_async_remote_copy(
                src_ref=rs2_src.at[which, gene_part(other)],
                dst_ref=rs2_dst.at[which, mine],
                send_sem=r2s_sem.at[which],
                recv_sem=r2r_sem.at[which],
                device_id=((r // 2) * 2 + other // n_col, lax.rem(other, n_col)),
                device_id_type=MESH,
            ).start()
            return carry

        rs2_dst[which, mine] = rs2_src[which, gene_part(mine), :]
        lax.fori_loop(1, per_group, body, 0)

    def rs2_finish(which):
        most = rs2_dst.at[which, pl.ds(0, per_group - 1)]
        pltpu.make_async_copy(most, most, r2r_sem.at[which]).wait()
        pltpu.make_async_copy(most, most, r2s_sem.at[which]).wait()
        total = rs2_dst[which, 0]
        for k in range(1, per_group):
            total += rs2_dst[which, k]
        return jnp.where(first, total, 0.0)

    loads[4].wait()
    loads[5].wait()
    square = dot(lt[0:lats, :], s_low[...])
    square_high = square.astype(BF16).astype(F32)
    square2 = jnp.where(first, square_high, square - square_high).astype(BF16)
    rs1_run(
        0,
        lambda where: slope_scale
        * (dot(square2, wtwice[:, where]) - dot(lt[0:lats, :], x[:, where])),
    )

    loads[6].wait()
    wide = jnp.concatenate([discw[...], jnp.zeros_like(discw)], axis=1)
    block = jnp.concatenate([wide, pltpu.roll(wide, lats, 1)], axis=0)
    block_high = block.astype(BF16)
    block_low = (block - block_high.astype(F32)).astype(BF16)
    for u in range(2):
        one = slice(u * LANES, (u + 1) * LANES)
        bd_nt[0:LANES, one] = block_high
        bd_nt[LANES:, one] = block_low
        bd_nn[one, 0:LANES] = block_high
        bd_nn[one, LANES:] = block_low
    for i in range(rows):
        stage[:, i, :] = emb[i].T
    emb_out[...] = stage[0:lats]
    outs[3].start()
    halo_take(2)

    def to_summary(i, value):
        summ[i] = jnp.where(first, summ[i], jax.nn.sigmoid(value))

    stencil(2, to_summary)

    half_sum = jnp.where(
        (lax.broadcasted_iota(jnp.int32, (LANES, LANES), 0) < lats)
        == (lax.broadcasted_iota(jnp.int32, (LANES, LANES), 1) < lats),
        1.0,
        0.0,
    ).astype(BF16)
    half_sum2 = jnp.concatenate([half_sum, half_sum], axis=0)

    step = rows // CHUNKS
    for i in range(CHUNKS):
        piece = slice(i * step, (i + 1) * step)
        summary = summ[piece].reshape(chunk, LANES)
        embedded = emb[piece].reshape(chunk, LANES)
        swapped = swap(embedded)
        summary_2 = split_2(summary)
        wide_q = dot(summary_2, bd_nt[...], 1, 1)
        queries = wide_q[:, :LANES] + wide_q[:, LANES:]
        logit_same = dot(split_2(embedded * queries), half_sum2)
        logit_other = dot(split_2(swapped * queries), half_sum2)
        grad_same = -jax.nn.sigmoid(-logit_same)
        grad_other = jax.nn.sigmoid(logit_other)
        embed_grad = grad_same * queries + swap(grad_other * queries)
        query_grad = grad_same * embedded + grad_other * swapped
        query_grad_2 = split_2(query_grad)
        here = slice(i * chunk, (i + 1) * chunk)
        grads_2[here, :] = query_grad_2
        summ_2[here, :] = summary_2
        wide_s = dot(query_grad_2, bd_nn[...])
        summary_grad = wide_s[:, :LANES] + wide_s[:, LANES:]
        spread_grad = summary_grad * summary * (1.0 - summary)
        spread_grad += back[i * chunk : (i + 1) * chunk, :]
        eg[piece] = embed_grad.reshape(step, LANES, LANES)
        mix[here, :] = jnp.where(lax.rem(lane, lats) < lats // 2, logit_same, logit_other)
        for j in range(step):
            put(3, i * step + j, spread_grad[j * LANES : (j + 1) * LANES, :])
    halo_start(3)

    disc_total = jnp.zeros((2 * LANES, 2 * LANES), F32)
    for i in range(CHUNKS):
        here = slice(i * chunk, (i + 1) * chunk)
        disc_total += dot(grads_2[here, :], summ_2[here, :], 0, 0)
    quarter = (disc_total[:LANES, :LANES] + disc_total[LANES:, :LANES]) + (
        disc_total[:LANES, LANES:] + disc_total[LANES:, LANES:]
    )
    disc_src[...] = quarter[:lats, :] + swap(quarter[lats:, :])

    def part_of(index):
        return pl.ds(pl.multiple_of(index * part, 8), part)

    def disc_1(k):
        other = lax.rem(c + k, n_col)
        return pltpu.make_async_remote_copy(
            src_ref=disc_src.at[part_of(other)],
            dst_ref=disc_a.at[c],
            send_sem=ds_sem.at[0],
            recv_sem=dr_sem.at[0],
            device_id=(r, other),
            device_id_type=MESH,
        )

    disc_a[c] = disc_src[part_of(c), :]
    peers(n_col, disc_1)

    for i in range(rows):
        flipped = mix[i * LANES : (i + 1) * LANES, :].T
        for k in range(4):
            at = k * (lats // 2)
            log_out[k, i : i + 1, :] = flipped[at : at + 1, :]
    outs[4].start()
    rs1_finish(0)
    rs2_start(0)

    halo_take(3)

    def to_latent_grad(i, value):
        z = lat[i]
        slope = jnp.where(z > 0, 1.0, jnp.exp(jnp.minimum(z, 0.0)))
        put(4, i, (eg[i] + value) * slope)

    stencil(3, to_latent_grad)
    halo_start(4)

    drain(disc_a, n_col, ds_sem.at[0], dr_sem.at[0])
    disc_bsrc[...] = jnp.sum(disc_a[...], axis=0)

    def disc_2(k):
        other = lax.rem(r + k, n_row)
        return pltpu.make_async_remote_copy(
            src_ref=disc_bsrc,
            dst_ref=disc_b.at[r],
            send_sem=ds_sem.at[1],
            recv_sem=dr_sem.at[1],
            device_id=(other, c),
            device_id_type=MESH,
        )

    disc_b[r] = disc_bsrc[...]
    peers(n_row, disc_2)
    dec_sum[...] = rs2_finish(0)

    halo_take(4)

    def to_proj_grad(i, value):
        pg_low[i * LANES : (i + 1) * LANES, :] = value.astype(BF16)

    stencil(4, to_proj_grad)

    returned = dot(recv_pick_t[...], pg_low[...])
    ex_src[1] = returned.astype(BF16).reshape(n_dev, portion, LANES)
    ex_start(1)
    for i in range(rows):
        here = slice(i * LANES, (i + 1) * LANES)
        flipped = pg_low[here, :].astype(F32).T
        stage[:, i, :] = flipped
        own[:, here] = flipped[:lats, :].astype(BF16)
    pg_out[...] = stage[...].astype(BF16)
    outs[5].start()

    drain(disc_b, n_row, ds_sem.at[1], dr_sem.at[1])
    disc_full[c] = jnp.sum(disc_b[...], axis=0)

    def disc_3(k):
        other = lax.rem(c + k, n_col)
        return pltpu.make_async_remote_copy(
            src_ref=disc_full.at[c],
            dst_ref=disc_full.at[c],
            send_sem=ds_sem.at[2],
            recv_sem=dr_sem.at[2],
            device_id=(r, other),
            device_id_type=MESH,
        )

    peers(n_col, disc_3)

    for turn in range(ROUNDS):
        halo_finish(turn)

    lt[0:lats, :] = own[...]
    home = ex_wait(1)
    flipped = jnp.concatenate(
        [home[i * LANES : (i + 1) * LANES, :].astype(F32).T[lats:, :] for i in range(rows)], axis=1
    ).astype(BF16)
    lt[lats:, :] = dot(flipped, send_pick[...]).astype(BF16)

    def encoder_part(where):
        value = dot(lt[...], x[:, where])
        return value[:lats, :] + value[lats:, :]

    rs1_run(1, encoder_part)

    drain(disc_full, n_col, ds_sem.at[2], dr_sem.at[2])
    disc_grad = disc_full[...].reshape(lats, LANES)[:, :lats]
    disc_mean = jnp.sum(disc_grad * disc_grad) / (lats * lats)
    disc_out[...] = disc_grad * lax.rsqrt(disc_mean + 1e-06)
    outs[2].start()

    rs1_finish(1)
    rs2_start(1)
    enc_sum = rs2_finish(1)

    def squares(value):
        return jnp.broadcast_to(jnp.sum(value * value), (8, LANES))

    norm_src[0] = squares(enc_sum)
    norm_src[1] = squares(dec_sum[...])

    def norm_1(k):
        other = lax.rem(r + k, n_row)
        return pltpu.make_async_remote_copy(
            src_ref=norm_src,
            dst_ref=norm_a.at[r],
            send_sem=ns_sem.at[0],
            recv_sem=nr_sem.at[0],
            device_id=(other, c),
            device_id_type=MESH,
        )

    norm_a[r] = norm_src[...]
    peers(n_row, norm_1)
    drain(norm_a, n_row, ns_sem.at[0], nr_sem.at[0])
    norm_bsrc[...] = jnp.sum(norm_a[...], axis=0)

    def norm_2(k):
        other = lax.rem(c + k, n_col)
        return pltpu.make_async_remote_copy(
            src_ref=norm_bsrc,
            dst_ref=norm_b.at[c],
            send_sem=ns_sem.at[1],
            recv_sem=nr_sem.at[1],
            device_id=(r, other),
            device_id_type=MESH,
        )

    norm_b[c] = norm_bsrc[...]
    peers(n_col, norm_2)
    drain(norm_b, n_col, ns_sem.at[1], nr_sem.at[1])
    totals = jnp.sum(norm_b[...], axis=0)
    entries = genes * lats
    enc_out[...] = enc_sum[:, :lats] * lax.rsqrt(totals[0, 0:1, 0:1] / entries + 1e-06)
    dec_out[...] = dec_sum[:, :lats] * lax.rsqrt(totals[1, 0:1, 0:1] / entries + 1e-06)
    outs[0].start()
    outs[1].start()
    for out in outs:
        out.wait()


def hand_on(*refs):
    count = (len(refs) - 2) // 3
    sources, targets, held = (refs[k * count : (k + 1) * count] for k in range(3))
    come, go = refs[3 * count :]
    ins = [pltpu.make_async_copy(sources[i], held[i], come.at[i]) for i in range(count)]
    outs = [pltpu.make_async_copy(held[i], targets[i], go.at[i]) for i in range(count)]
    for copy in ins:
        copy.start()
    for i in range(count):
        ins[i].wait()
        outs[i].start()
    for copy in outs:
        copy.wait()


def per_device(features, enc_weight, dec_weight, disc_weight, send_order, recv_order):
    tile_rows, tile_cols, genes = features.shape
    lats = enc_weight.shape[1]
    bins = tile_rows * tile_cols
    n_row = lax.axis_size("row")
    n_col = lax.axis_size("col")
    n_dev = n_row * n_col
    n_group = n_row // 2
    per_dev = genes // n_dev
    span = genes // n_group
    part = lats // n_col
    portion = bins // n_dev
    field = (tile_rows, LANES, LANES)
    dma = pltpu.SemaphoreType.DMA
    vmem = pltpu.VMEM
    shape = jax.ShapeDtypeStruct
    out_shape = [
        shape((per_dev, lats), F32),
        shape((per_dev, lats), F32),
        shape((lats, lats), F32),
        shape((lats, tile_rows, tile_cols), F32),
        shape((4, tile_rows, tile_cols), F32),
        shape((2 * lats, tile_rows, tile_cols), BF16),
    ]
    scratch = [
        *(vmem(one.shape, one.dtype) for one in out_shape),
        vmem((bins, genes), BF16),
        vmem((lats, lats), F32),
        vmem((2, tile_rows, LANES), jnp.int32),
        vmem((2 * lats, genes), BF16),
        vmem((2 * lats, genes), BF16),
        vmem((LANES, LANES), BF16),
        vmem((2 * LANES, 2 * LANES), BF16),
        vmem((2 * LANES, 2 * LANES), BF16),
        vmem((bins, bins), BF16),
        vmem((bins, bins), BF16),
        vmem((bins, bins), BF16),
        vmem((bins, LANES), F32),
        vmem((bins, LANES), BF16),
        vmem((2, n_dev, portion, LANES), BF16),
        vmem((2, n_dev, portion, LANES), BF16),
        vmem((2, tile_rows + 2 * RADIUS, LANES + 2 * SIDE, LANES), F32),
        vmem((tile_rows, LANES + 2 * SIDE, LANES), F32),
        vmem((ROUNDS,) + field, BF16),
        vmem((ROUNDS, 2, RADIUS, LANES, LANES), BF16),
        vmem((ROUNDS, 2, tile_rows, EDGE, LANES), BF16),
        vmem((ROUNDS, 4, RADIUS, EDGE, LANES), BF16),
        vmem((len(PACKED), 2, RADIUS, LANES // 2, LANES), BF16),
        vmem((len(PACKED), 2, RADIUS, LANES // 2, LANES), BF16),
        vmem(field, F32),
        vmem(field, F32),
        vmem(field, F32),
        vmem(field, F32),
        vmem((bins, LANES), BF16),
        vmem((bins, LANES), F32),
        vmem((bins, 2 * LANES), BF16),
        vmem((bins, 2 * LANES), BF16),
        vmem((bins, LANES), F32),
        vmem(field, F32),
        vmem((bins, LANES), BF16),
        vmem((LANES, bins), BF16),
        vmem((lats, bins), BF16),
        vmem((2, n_group, lats, span), BF16),
        vmem((2, n_group, lats, span), BF16),
        vmem((2, span, LANES), F32),
        vmem((2, 2 * n_col, per_dev, LANES), F32),
        vmem((lats, LANES), F32),
        vmem((n_col, part, LANES), F32),
        vmem((part, LANES), F32),
        vmem((n_row, part, LANES), F32),
        vmem((n_col, part, LANES), F32),
        vmem((2, 8, LANES), F32),
        vmem((n_row, 2, 8, LANES), F32),
        vmem((2, 8, LANES), F32),
        vmem((n_col, 2, 8, LANES), F32),
        vmem((LANES, tile_rows, LANES), F32),
        vmem((per_dev, LANES), F32),
        dma((7,)),
        dma((tile_rows,)),
        dma((ROUNDS, 8)),
        dma((ROUNDS, 8)),
        dma((2,)),
        dma((2,)),
        dma((2,)),
        dma((2,)),
        dma((2,)),
        dma((2,)),
        dma((3,)),
        dma((3,)),
        dma((2,)),
        dma((2,)),
        pltpu.SemaphoreType.REGULAR,
        dma((6,)),
    ]
    anywhere = [pl.BlockSpec(memory_space=pl.ANY)] * 6
    results = pl.pallas_call(
        functools.partial(kernel, n_row, n_col),
        out_shape=out_shape,
        in_specs=anywhere,
        out_specs=anywhere,
        scratch_shapes=scratch,
        compiler_params=pltpu.CompilerParams(
            collective_id=0, has_side_effects=True, vmem_limit_bytes=56 * 1024 * 1024
        ),
    )(
        features.reshape(bins, genes),
        enc_weight.T,
        dec_weight.T,
        disc_weight,
        send_order.reshape(tile_rows, LANES),
        recv_order.reshape(tile_rows, LANES),
    )
    *others, grads = pl.pallas_call(
        hand_on,
        out_shape=out_shape,
        in_specs=anywhere,
        out_specs=anywhere,
        scratch_shapes=[*(vmem(one.shape, one.dtype) for one in out_shape), dma((6,)), dma((6,))],
    )(*results)
    return (*others, grads.reshape(2, lats, tile_rows, tile_cols))


def solution(mesh):
    in_specs = (P("row", "col", None), P(), P(), P(), P("row", "col", None), P("row", "col", None))
    out_specs = (
        P(("row", "col"), None),
        P(("row", "col"), None),
        P(),
        P(None, "row", "col"),
        P(None, "row", "col"),
        P(None, None, "row", "col"),
    )
    return jax.shard_map(
        per_device, mesh=mesh, in_specs=in_specs, out_specs=out_specs, check_vma=False
    )
```

```python
import functools
import math

import jax
import jax.numpy as jnp
from jax import lax
from jax.experimental import pallas as pl
from jax.experimental.pallas import tpu as pltpu
from jax.sharding import PartitionSpec as P

RADIUS = 3
RECON_WEIGHT = 10.0
LANES = 128
EDGE = 16
SIDE = 8
MESH = pl.DeviceIdType.MESH
F32 = jnp.float32
BF16 = jnp.bfloat16
DIRECTIONS = ((-1, 0), (1, 0), (0, -1), (0, 1), (-1, -1), (-1, 1), (1, -1), (1, 1))
OPPOSITE = (1, 0, 3, 2, 7, 6, 5, 4)
ROUNDS = 5
PACKED = {0: 0, 2: 1}
CHUNKS = 4


def stencil_taps():
    raw_taps = [math.exp(-offset * offset / 12.0) for offset in range(-RADIUS, RADIUS + 1)]
    tap_total = sum(raw_taps)
    return [raw_value / tap_total for raw_value in raw_taps]


def dot(a, b, ca=1, cb=0):
    return lax.dot_general(a, b, (((ca,), (cb,)), ((), ())), preferred_element_type=F32)


def each(count, body):
    def step(i, carry):
        body(i)
        return carry

    lax.fori_loop(0, count, step, 0)


def split_2(value):
    high = value.astype(BF16)
    low = (value - high.astype(F32)).astype(BF16)
    return jnp.concatenate([high, low], axis=1)


def kernel(
    n_row,
    n_col,
    feat_hbm,
    enc_hbm,
    dec_hbm,
    disc_hbm,
    send_hbm,
    recv_hbm,
    enc_hbm_out,
    dec_hbm_out,
    disc_hbm_out,
    emb_hbm_out,
    log_hbm_out,
    pg_hbm_out,
    enc_out,
    dec_out,
    disc_out,
    emb_out,
    log_out,
    pg_out,
    x,
    discw,
    orders,
    wcat,
    wtwice,
    gram2,
    bd_nt,
    bd_nn,
    send_pick,
    recv_pick,
    recv_pick_t,
    xp,
    xp_low,
    ex_src,
    ex_dst,
    low_in,
    pads,
    tmp,
    hsrc,
    h_row,
    h_col,
    h_corner,
    pack_src,
    h_pack,
    lat,
    emb,
    spread,
    summ,
    s_low,
    back,
    grads_2,
    summ_2,
    mix,
    eg,
    pg_low,
    lt,
    own,
    rs1_src,
    rs1_dst,
    rs2_src,
    rs2_dst,
    disc_src,
    disc_a,
    disc_bsrc,
    disc_b,
    disc_full,
    norm_src,
    norm_a,
    by_gene,
    stage,
    dec_sum,
    load_sem,
    feat_sem,
    hs_sem,
    hr_sem,
    as_sem,
    ar_sem,
    r1s_sem,
    r1r_sem,
    r2s_sem,
    r2r_sem,
    ds_sem,
    dr_sem,
    ns_sem,
    nr_sem,
    meet_sem,
    out_sem,
):
    n_dev = n_row * n_col
    bins, genes = x.shape
    rows = bins // LANES
    lats = discw.shape[1]
    portion = bins // n_dev
    n_group = n_row // 2
    n_pair = n_group // 2
    width = 2 * LANES
    per_dev = genes // n_dev
    span = genes // n_group
    part = lats // n_col
    slope_scale = 2.0 * RECON_WEIGHT / genes
    tap = stencil_taps()
    chunk = bins // CHUNKS

    r = lax.axis_index("row")
    c = lax.axis_index("col")
    me = r * n_col + c
    my_group = r // 2
    lane = lax.broadcasted_iota(jnp.int32, (1, LANES), 1)
    first = lane < lats

    outs = [
        pltpu.make_async_copy(a, b, out_sem.at[i])
        for i, (a, b) in enumerate(
            [
                (enc_out, enc_hbm_out),
                (dec_out, dec_hbm_out),
                (disc_out, disc_hbm_out),
                (emb_out, emb_hbm_out),
                (log_out, log_hbm_out),
                (pg_out, pg_hbm_out),
            ]
        )
    ]

    def swap(value):
        return pltpu.roll(value, lats, value.ndim - 1)

    def halo_buffer(turn, way):
        if way < 2:
            return h_row.at[turn, way]
        if way < 4:
            return h_col.at[turn, way - 2]
        return h_corner.at[turn, way - 4]

    def halo_copy(turn, way):
        dr, dc = DIRECTIONS[way]
        row_part = pl.ds(0, RADIUS) if dr < 0 else pl.ds(rows - RADIUS, RADIUS) if dr else pl.ds(0, rows)
        col_part = pl.ds(0, EDGE) if dc < 0 else pl.ds(LANES - EDGE, EDGE) if dc else pl.ds(0, LANES)
        if way < 2 and turn in PACKED:
            source = pack_src.at[PACKED[turn], way]
            target = h_pack.at[PACKED[turn], OPPOSITE[way]]
        else:
            source = hsrc.at[turn, row_part, col_part]
            target = halo_buffer(turn, OPPOSITE[way])
        return pltpu.make_async_remote_copy(
            src_ref=source,
            dst_ref=target,
            send_sem=hs_sem.at[turn, way],
            recv_sem=hr_sem.at[turn, OPPOSITE[way]],
            device_id=(r + dr, c + dc),
            device_id_type=MESH,
        )

    def present(way):
        dr, dc = DIRECTIONS[way]
        tests = []
        if dr < 0:
            tests.append(r > 0)
        if dr > 0:
            tests.append(r < n_row - 1)
        if dc < 0:
            tests.append(c > 0)
        if dc > 0:
            tests.append(c < n_col - 1)
        return functools.reduce(jnp.logical_and, tests)

    def halo_start(turn):
        for way in range(8):

            @pl.when(present(way))
            def _():
                halo_copy(turn, way).start()

    def halo_take(turn):
        pad = pads.at[turn % 2]
        for way in range(8):

            @pl.when(present(way))
            def _():
                halo_copy(turn, OPPOSITE[way]).wait_recv()

        left, right = slice(0, SIDE), slice(SIDE + LANES, LANES + 2 * SIDE)
        top, bottom = slice(0, RADIUS), slice(RADIUS + rows, rows + 2 * RADIUS)
        for way, part in ((0, top), (1, bottom)):
            if turn in PACKED:
                packed = h_pack[PACKED[turn], way].astype(F32)
                halves = (packed, swap(packed)) if turn == 0 else (swap(packed), packed)
                pad[part, SIDE : SIDE + LANES // 2, :] = halves[0]
                pad[part, SIDE + LANES // 2 : SIDE + LANES, :] = halves[1]
            else:
                pad[part, SIDE : SIDE + LANES, :] = h_row[turn, way].astype(F32)
            pad[part, left, :] = h_corner[turn, 2 * way].astype(F32)[:, EDGE - SIDE :, :]
            pad[part, right, :] = h_corner[turn, 2 * way + 1].astype(F32)[:, :SIDE, :]
        own_rows = slice(RADIUS, RADIUS + rows)
        pad[own_rows, left, :] = h_col[turn, 0].astype(F32)[:, EDGE - SIDE :, :]
        pad[own_rows, right, :] = h_col[turn, 1].astype(F32)[:, :SIDE, :]

    def halo_finish(turn):
        for way in range(8):

            @pl.when(present(way))
            def _():
                halo_copy(turn, way).wait_send()

    def stencil(turn, then):
        pad = pads.at[turn % 2]

        def down(t):
            at = pl.ds(pl.multiple_of(t * SIDE, SIDE), SIDE)
            block = pad[:, at, :]
            across = tap[RADIUS] * block[RADIUS : RADIUS + rows]
            for k in range(1, RADIUS + 1):
                across += tap[RADIUS + k] * (
                    block[RADIUS - k : RADIUS - k + rows] + block[RADIUS + k : RADIUS + k + rows]
                )
            tmp[:, at, :] = across

        def along(i):
            total = tap[RADIUS] * tmp[i, SIDE : SIDE + LANES, :]
            for k in range(1, RADIUS + 1):
                total += tap[RADIUS + k] * (
                    tmp[i, SIDE - k : SIDE - k + LANES, :] + tmp[i, SIDE + k : SIDE + k + LANES, :]
                )
            then(i, total)

        each(LANES // SIDE + 2, down)
        each(rows, along)

    def bins_of(i, size=LANES):
        return pl.ds(pl.multiple_of(i * size, size), size)

    def put(turn, i, value):
        pads[turn % 2, i + RADIUS, SIDE : SIDE + LANES, :] = value
        low = value.astype(BF16)
        if turn not in PACKED:
            hsrc[turn, i] = low
            return
        hsrc[turn, i, 0:EDGE, :] = low[0:EDGE, :]
        hsrc[turn, i, LANES - EDGE :, :] = low[LANES - EDGE :, :]
        front, rear = value[: LANES // 2, :], value[LANES // 2 :, :]
        if turn == 0:
            packed = jnp.where(first, front, swap(rear)).astype(BF16)
        else:
            packed = jnp.where(first, swap(front), rear).astype(BF16)

        @pl.when(i < RADIUS)
        def _():
            pack_src[PACKED[turn], 0, i] = packed

        @pl.when(i >= rows - RADIUS)
        def _():
            pack_src[PACKED[turn], 1, i - (rows - RADIUS)] = packed

    loads = [
        pltpu.make_async_copy(a, b, load_sem.at[i])
        for i, (a, b) in enumerate(
            [
                (send_hbm, orders.at[0]),
                (recv_hbm, orders.at[1]),
                (dec_hbm, wcat.at[pl.ds(0, lats)]),
                (enc_hbm, wcat.at[pl.ds(lats, lats)]),
                (dec_hbm, wtwice.at[pl.ds(0, lats)]),
                (dec_hbm, wtwice.at[pl.ds(lats, lats)]),
                (disc_hbm, discw),
            ]
        )
    ]
    for load in loads[:4]:
        load.start()
    for i in range(rows):
        piece = pl.ds(i * LANES, LANES)
        copy = pltpu.make_async_copy(feat_hbm.at[piece], x.at[piece], feat_sem.at[i])
        copy.start()
    for load in loads[4:]:
        load.start()

    barrier = pltpu.get_barrier_semaphore()

    def greet_row(k, carry):
        other = lax.rem(r + k, n_row)
        pl.semaphore_signal(barrier, inc=1, device_id=(other, c), device_id_type=MESH)
        return carry

    def greet_col(k, carry):
        other = lax.rem(c + k, n_col)
        pl.semaphore_signal(barrier, inc=1, device_id=(r, other), device_id_type=MESH)
        return carry

    lax.fori_loop(1, n_row, greet_row, 0)
    lax.fori_loop(1, n_col, greet_col, 0)

    def build_send():
        def body(a):
            line = orders[0, pl.ds(a, 1), :].astype(F32)
            column = jnp.broadcast_to(line, (LANES, LANES)).T
            for t in range(rows):
                index = (lane + t * LANES).astype(F32)
                send_pick[bins_of(a), t * LANES : (t + 1) * LANES] = jnp.where(
                    column == index, 1.0, 0.0
                ).astype(BF16)

        each(rows, body)

    def build_recv():
        def body(a, carry):
            line = orders[1, pl.ds(a, 1), :].astype(F32)
            column = jnp.broadcast_to(line, (LANES, LANES)).T
            for t in range(rows):
                index = (lane + t * LANES).astype(F32)
                recv_pick[
                    pl.ds(pl.multiple_of(a * LANES, LANES), LANES), t * LANES : (t + 1) * LANES
                ] = jnp.where(column == index, 1.0, 0.0).astype(BF16)
            return carry

        lax.fori_loop(0, rows, body, 0)

    def build_recv_t():
        def body(t, carry):
            index = (lax.broadcasted_iota(jnp.int32, (LANES, 1), 0) + t * LANES).astype(F32)
            for a in range(rows):
                line = orders[1, a : a + 1, :].astype(F32)
                recv_pick_t[
                    pl.ds(pl.multiple_of(t * LANES, LANES), LANES), a * LANES : (a + 1) * LANES
                ] = jnp.where(line == index, 1.0, 0.0).astype(BF16)
            return carry

        lax.fori_loop(0, rows, body, 0)

    def ex_copy(which, k):
        other = lax.rem(me + k, n_dev)
        return pltpu.make_async_remote_copy(
            src_ref=ex_src.at[which, other],
            dst_ref=ex_dst.at[which, me],
            send_sem=as_sem.at[which],
            recv_sem=ar_sem.at[which],
            device_id=(other // n_col, lax.rem(other, n_col)),
            device_id_type=MESH,
        )

    def peers(count, make):
        def body(k, carry):
            make(k).start()
            return carry

        lax.fori_loop(1, count, body, 0)

    def drain(ref, count, send_sem, recv_sem):
        most = ref.at[pl.ds(0, count - 1)]
        pltpu.make_async_copy(most, most, recv_sem).wait()
        pltpu.make_async_copy(most, most, send_sem).wait()

    def ex_start(which):
        peers(n_dev, functools.partial(ex_copy, which))
        ex_dst[which, me] = ex_src[which, me]

    def ex_wait(which):
        drain(ex_dst.at[which], n_dev, as_sem.at[which], ar_sem.at[which])
        return ex_dst[which].reshape(bins, LANES)

    loads[0].wait()
    loads[1].wait()
    build_send()
    for way in range(8):

        @pl.when(jnp.logical_not(present(way)))
        def _():
            for turn in range(ROUNDS):
                if way < 2 and turn in PACKED:
                    empty = h_pack.at[PACKED[turn], way]
                else:
                    empty = halo_buffer(turn, way)
                empty[...] = jnp.zeros_like(empty)

    loads[2].wait()
    loads[3].wait()

    pl.semaphore_wait(barrier, n_row + n_col - 2)

    def greet_meet(k, carry):
        other = lax.rem(c + k, n_col)
        pl.semaphore_signal(meet_sem, inc=1, device_id=(r, other), device_id_type=MESH)
        return carry

    lax.fori_loop(1, n_col, greet_meet, 0)
    def project(i):
        for k in range(rows // CHUNKS):
            at = i * (rows // CHUNKS) + k
            pltpu.make_async_copy(
                feat_hbm.at[bins_of(at)], x.at[bins_of(at)], feat_sem.at[at]
            ).wait()
        acc = dot(x[bins_of(i, chunk), :], wcat[...], 1, 1)
        xp[bins_of(i, chunk), :] = acc
        xp_low[bins_of(i, chunk), :] = acc.astype(BF16)

    each(CHUNKS, project)

    def pick_out(i):
        value = dot(send_pick[bins_of(i, chunk), :], xp_low[...])
        ex_src[0, pl.ds(i * (n_dev // CHUNKS), n_dev // CHUNKS)] = value.astype(BF16).reshape(
            n_dev // CHUNKS, portion, LANES
        )

    each(CHUNKS, pick_out)

    pl.semaphore_wait(meet_sem, n_col - 1)

    ex_start(0)

    each(rows, lambda i: put(0, i, swap(xp_low[bins_of(i), :].astype(F32))))
    halo_start(0)
    build_recv()
    def elu(value):
        return jnp.where(value > 0, value, jnp.exp(jnp.minimum(value, 0.0)) - 1.0)

    def first_latent(i, value):
        lat[i] = value
        emb[i] = elu(value)

    halo_take(0)
    stencil(0, first_latent)

    arrived = ex_wait(0)
    low_in[...] = arrived

    def pick_in(i):
        value = dot(recv_pick[bins_of(i, chunk), :], low_in[...])
        for k in range(rows // CHUNKS):
            at = i * (rows // CHUNKS) + k
            put(1, at, jnp.where(first, emb[at], value[k * LANES : (k + 1) * LANES, :]))

    each(CHUNKS, pick_in)
    halo_start(1)
    build_recv_t()
    gram = dot(wcat[0:lats, :], wcat[0:lats, :], 1, 1)
    gram_high = gram.astype(BF16)
    gram_low = (gram - gram_high.astype(F32)).astype(BF16)
    gram2[...] = jnp.zeros_like(gram2)
    gram2[0:lats, 0:lats] = gram_high
    gram2[lats:, 0:lats] = gram_low

    def first_spread(i, value):
        out = elu(value)
        lat[i] = jnp.where(first, lat[i], value)
        emb[i] = jnp.where(first, emb[i], out)
        put(2, i, out)
        spread[i] = value

    halo_take(1)
    stencil(1, first_spread)
    halo_start(2)

    def after_spread(i):
        value = spread[i]
        here = bins_of(i)
        low = value.astype(BF16).astype(F32)
        summ[i] = jax.nn.sigmoid(value)
        s_low[here, :] = jnp.where(first, low, swap(low)).astype(BF16)
        lt[0:lats, here] = low.T[0:lats, :].astype(BF16)

    each(rows, after_spread)

    back[...] = slope_scale * (
        dot(s_low[...], gram2[...]) - jnp.where(first, xp[...], 0.0)
    )

    def rs1_copy(which, target):
        return pltpu.make_async_remote_copy(
            src_ref=rs1_src.at[which, target],
            dst_ref=rs1_dst.at[which, r],
            send_sem=r1s_sem.at[which],
            recv_sem=r1r_sem.at[which],
            device_id=(target, c),
            device_id_type=MESH,
        )

    def rs1_run(which, product):
        def body(k):
            pair = lax.rem(my_group // 2 + 1 + k, n_pair)
            where = bins_of(pair, 2 * span)
            value = product(where).astype(BF16)
            for j in range(4):
                at = (j // 2) * span + (j % 2) * LANES
                rs1_src[which, 4 * pair + j] = value[:, at : at + width]
            for j in range(4):

                @pl.when(4 * pair + j != r)
                def _():
                    rs1_copy(which, 4 * pair + j).start()

        each(n_pair, body)

    def rs1_finish(which):
        drain(rs1_dst.at[which], n_row, r1s_sem.at[which], r1r_sem.at[which])
        rs1_dst[which, r] = rs1_src[which, r]
        total = rs1_dst[which, 0].astype(F32)
        for k in range(1, n_row):
            total += rs1_dst[which, k].astype(F32)
        rs2_src[which] = total.astype(BF16)

    def rs2_copy(which, k):
        other = lax.rem(c + k, n_col)
        return pltpu.make_async_remote_copy(
            src_ref=rs2_src.at[which],
            dst_ref=rs2_dst.at[which, c],
            send_sem=r2s_sem.at[which],
            recv_sem=r2r_sem.at[which],
            device_id=(r, other),
            device_id_type=MESH,
        )

    def rs2_start(which):
        peers(n_col, functools.partial(rs2_copy, which))
        rs2_dst[which, c] = rs2_src[which]

    def rs2_finish(which):
        drain(rs2_dst.at[which], n_col, r2s_sem.at[which], r2r_sem.at[which])
        total = rs2_dst[which, 0].astype(F32)
        for k in range(1, n_col):
            total += rs2_dst[which, k].astype(F32)
        begin = lax.rem(r, 2) * (width - span // 2)
        gene = lax.broadcasted_iota(jnp.int32, (1, width), 1) - begin
        own_genes = jnp.where((gene >= 0) & (gene < span // 2), total, 0.0)
        for k in range(width // LANES):
            by_gene[k * LANES : (k + 1) * LANES, :] = total[:, k * LANES : (k + 1) * LANES].T
        mine = by_gene[pl.ds(pl.multiple_of(begin + c * per_dev, 8), per_dev), :]
        norm_src[which] = jnp.broadcast_to(jnp.sum(own_genes * own_genes), (8, LANES))
        return mine

    square = dot(lt[0:lats, :], s_low[...])
    square_high = square.astype(BF16).astype(F32)
    square2 = jnp.where(first, square_high, square - square_high).astype(BF16)
    loads[4].wait()
    loads[5].wait()
    rs1_run(
        0,
        lambda where: slope_scale
        * (dot(square2, wtwice[:, where]) - dot(lt[0:lats, :], x[:, where])),
    )

    loads[6].wait()
    wide = jnp.concatenate([discw[...], jnp.zeros_like(discw)], axis=1)
    block = jnp.concatenate([wide, pltpu.roll(wide, lats, 1)], axis=0)
    block_high = block.astype(BF16)
    block_low = (block - block_high.astype(F32)).astype(BF16)
    for u in range(2):
        one = slice(u * LANES, (u + 1) * LANES)
        bd_nt[0:LANES, one] = block_high
        bd_nt[LANES:, one] = block_low
        bd_nn[one, 0:LANES] = block_high
        bd_nn[one, LANES:] = block_low
    for i in range(rows):
        stage[:, i, :] = emb[i].T
    emb_out[...] = stage[0:lats]
    outs[3].start()
    halo_take(2)

    def to_summary(i, value):
        summ[i] = jnp.where(first, summ[i], jax.nn.sigmoid(value))

    stencil(2, to_summary)

    half_sum = jnp.where(
        (lax.broadcasted_iota(jnp.int32, (LANES, LANES), 0) < lats)
        == (lax.broadcasted_iota(jnp.int32, (LANES, LANES), 1) < lats),
        1.0,
        0.0,
    ).astype(BF16)
    half_sum2 = jnp.concatenate([half_sum, half_sum], axis=0)

    step = rows // CHUNKS

    def contrast(i):
        piece = pl.ds(i * step, step)
        here = bins_of(i, chunk)
        summary = summ[piece].reshape(chunk, LANES)
        embedded = emb[piece].reshape(chunk, LANES)
        swapped = swap(embedded)
        summary_2 = split_2(summary)
        wide_q = dot(summary_2, bd_nt[...], 1, 1)
        queries = wide_q[:, :LANES] + wide_q[:, LANES:]
        logit_same = dot(split_2(embedded * queries), half_sum2)
        logit_other = dot(split_2(swapped * queries), half_sum2)
        grad_same = -jax.nn.sigmoid(-logit_same)
        grad_other = jax.nn.sigmoid(logit_other)
        embed_grad = grad_same * queries + swap(grad_other * queries)
        query_grad = grad_same * embedded + grad_other * swapped
        query_grad_2 = split_2(query_grad)
        grads_2[here, :] = query_grad_2
        summ_2[here, :] = summary_2
        wide_s = dot(query_grad_2, bd_nn[...])
        summary_grad = wide_s[:, :LANES] + wide_s[:, LANES:]
        spread_grad = summary_grad * summary * (1.0 - summary)
        spread_grad += back[here, :]
        eg[piece] = embed_grad.reshape(step, LANES, LANES)
        mix[here, :] = jnp.where(lax.rem(lane, lats) < lats // 2, logit_same, logit_other)
        for j in range(step):
            put(3, i * step + j, spread_grad[j * LANES : (j + 1) * LANES, :])

    each(CHUNKS, contrast)
    halo_start(3)

    def disc_step(i, total):
        here = bins_of(i, chunk)
        return total + dot(grads_2[here, :], summ_2[here, :], 0, 0)

    disc_total = lax.fori_loop(
        0, CHUNKS, disc_step, jnp.zeros((2 * LANES, 2 * LANES), F32)
    )
    quarter = (disc_total[:LANES, :LANES] + disc_total[LANES:, :LANES]) + (
        disc_total[:LANES, LANES:] + disc_total[LANES:, LANES:]
    )
    disc_src[...] = quarter[:lats, :] + swap(quarter[lats:, :])

    def part_of(index):
        return pl.ds(pl.multiple_of(index * part, 8), part)

    def disc_1(k):
        other = lax.rem(c + k, n_col)
        return pltpu.make_async_remote_copy(
            src_ref=disc_src.at[part_of(other)],
            dst_ref=disc_a.at[c],
            send_sem=ds_sem.at[0],
            recv_sem=dr_sem.at[0],
            device_id=(r, other),
            device_id_type=MESH,
        )

    disc_a[c] = disc_src[part_of(c), :]
    peers(n_col, disc_1)

    for i in range(rows):
        flipped = mix[i * LANES : (i + 1) * LANES, :].T
        for k in range(4):
            at = k * (lats // 2)
            log_out[k, i : i + 1, :] = flipped[at : at + 1, :]
    outs[4].start()
    rs1_finish(0)
    rs2_start(0)

    halo_take(3)

    def to_latent_grad(i, value):
        z = lat[i]
        slope = jnp.where(z > 0, 1.0, jnp.exp(jnp.minimum(z, 0.0)))
        put(4, i, (eg[i] + value) * slope)

    stencil(3, to_latent_grad)
    halo_start(4)

    drain(disc_a, n_col, ds_sem.at[0], dr_sem.at[0])
    disc_bsrc[...] = jnp.sum(disc_a[...], axis=0)

    def disc_2(k):
        other = lax.rem(r + k, n_row)
        return pltpu.make_async_remote_copy(
            src_ref=disc_bsrc,
            dst_ref=disc_b.at[r],
            send_sem=ds_sem.at[1],
            recv_sem=dr_sem.at[1],
            device_id=(other, c),
            device_id_type=MESH,
        )

    disc_b[r] = disc_bsrc[...]
    peers(n_row, disc_2)
    dec_sum[...] = rs2_finish(0)

    halo_take(4)

    def to_proj_grad(i, value):
        pg_low[bins_of(i), :] = value.astype(BF16)

    stencil(4, to_proj_grad)

    def pick_back(i):
        value = dot(recv_pick_t[bins_of(i, chunk), :], pg_low[...])
        ex_src[1, pl.ds(i * (n_dev // CHUNKS), n_dev // CHUNKS)] = value.astype(BF16).reshape(
            n_dev // CHUNKS, portion, LANES
        )

    each(CHUNKS, pick_back)
    ex_start(1)
    for i in range(rows):
        here = slice(i * LANES, (i + 1) * LANES)
        flipped = pg_low[here, :].astype(F32).T
        stage[:, i, :] = flipped
        own[:, here] = flipped[:lats, :].astype(BF16)
    pg_out[...] = stage[...].astype(BF16)
    outs[5].start()

    drain(disc_b, n_row, ds_sem.at[1], dr_sem.at[1])
    disc_full[c] = jnp.sum(disc_b[...], axis=0)

    def disc_3(k):
        other = lax.rem(c + k, n_col)
        return pltpu.make_async_remote_copy(
            src_ref=disc_full.at[c],
            dst_ref=disc_full.at[c],
            send_sem=ds_sem.at[2],
            recv_sem=dr_sem.at[2],
            device_id=(r, other),
            device_id_type=MESH,
        )

    peers(n_col, disc_3)

    for turn in range(ROUNDS):
        halo_finish(turn)

    lt[0:lats, :] = own[...]
    home = ex_wait(1)
    flipped = jnp.concatenate(
        [home[i * LANES : (i + 1) * LANES, :].astype(F32).T[lats:, :] for i in range(rows)], axis=1
    ).astype(BF16)
    lt[lats:, :] = dot(flipped, send_pick[...]).astype(BF16)

    def encoder_part(where):
        value = dot(lt[...], x[:, where])
        return value[:lats, :] + value[lats:, :]

    rs1_run(1, encoder_part)

    drain(disc_full, n_col, ds_sem.at[2], dr_sem.at[2])
    disc_grad = disc_full[...].reshape(lats, LANES)[:, :lats]
    disc_mean = jnp.sum(disc_grad * disc_grad) / (lats * lats)
    disc_out[...] = disc_grad * lax.rsqrt(disc_mean + 1e-06)
    outs[2].start()

    rs1_finish(1)
    rs2_start(1)
    enc_sum = rs2_finish(1)

    def norm_1(k):
        other = lax.rem(r + k, n_row)
        return pltpu.make_async_remote_copy(
            src_ref=norm_src,
            dst_ref=norm_a.at[r],
            send_sem=ns_sem.at[0],
            recv_sem=nr_sem.at[0],
            device_id=(other, c),
            device_id_type=MESH,
        )

    norm_a[r] = norm_src[...]
    peers(n_row, norm_1)
    drain(norm_a, n_row, ns_sem.at[0], nr_sem.at[0])
    totals = jnp.sum(norm_a[...], axis=0)
    entries = genes * lats
    enc_out[...] = enc_sum * lax.rsqrt(totals[1, 0:1, 0:1] / entries + 1e-06)
    dec_out[...] = dec_sum[...] * lax.rsqrt(totals[0, 0:1, 0:1] / entries + 1e-06)
    outs[0].start()
    outs[1].start()
    for out in outs:
        out.wait()


def hand_on(*refs):
    count = (len(refs) - 2) // 3
    sources, targets, held = (refs[k * count : (k + 1) * count] for k in range(3))
    come, go = refs[3 * count :]
    ins = [pltpu.make_async_copy(sources[i], held[i], come.at[i]) for i in range(count)]
    outs = [pltpu.make_async_copy(held[i], targets[i], go.at[i]) for i in range(count)]
    for copy in ins:
        copy.start()
    for i in range(count):
        ins[i].wait()
        outs[i].start()
    for copy in outs:
        copy.wait()


def per_device(features, enc_weight, dec_weight, disc_weight, send_order, recv_order):
    tile_rows, tile_cols, genes = features.shape
    lats = enc_weight.shape[1]
    bins = tile_rows * tile_cols
    n_row = lax.axis_size("row")
    n_col = lax.axis_size("col")
    n_dev = n_row * n_col
    n_group = n_row // 2
    per_dev = genes // n_dev
    span = genes // n_group
    part = lats // n_col
    portion = bins // n_dev
    field = (tile_rows, LANES, LANES)
    dma = pltpu.SemaphoreType.DMA
    vmem = pltpu.VMEM
    shape = jax.ShapeDtypeStruct
    out_shape = [
        shape((per_dev, lats), F32),
        shape((per_dev, lats), F32),
        shape((lats, lats), F32),
        shape((lats, tile_rows, tile_cols), F32),
        shape((4, tile_rows, tile_cols), F32),
        shape((2 * lats, tile_rows, tile_cols), BF16),
    ]
    scratch = [
        *(vmem(one.shape, one.dtype) for one in out_shape),
        vmem((bins, genes), BF16),
        vmem((lats, lats), F32),
        vmem((2, tile_rows, LANES), jnp.int32),
        vmem((2 * lats, genes), BF16),
        vmem((2 * lats, genes), BF16),
        vmem((LANES, LANES), BF16),
        vmem((2 * LANES, 2 * LANES), BF16),
        vmem((2 * LANES, 2 * LANES), BF16),
        vmem((bins, bins), BF16),
        vmem((bins, bins), BF16),
        vmem((bins, bins), BF16),
        vmem((bins, LANES), F32),
        vmem((bins, LANES), BF16),
        vmem((2, n_dev, portion, LANES), BF16),
        vmem((2, n_dev, portion, LANES), BF16),
        vmem((bins, LANES), BF16),
        vmem((2, tile_rows + 2 * RADIUS, LANES + 2 * SIDE, LANES), F32),
        vmem((tile_rows, LANES + 2 * SIDE, LANES), F32),
        vmem((ROUNDS,) + field, BF16),
        vmem((ROUNDS, 2, RADIUS, LANES, LANES), BF16),
        vmem((ROUNDS, 2, tile_rows, EDGE, LANES), BF16),
        vmem((ROUNDS, 4, RADIUS, EDGE, LANES), BF16),
        vmem((len(PACKED), 2, RADIUS, LANES // 2, LANES), BF16),
        vmem((len(PACKED), 2, RADIUS, LANES // 2, LANES), BF16),
        vmem(field, F32),
        vmem(field, F32),
        vmem(field, F32),
        vmem(field, F32),
        vmem((bins, LANES), BF16),
        vmem((bins, LANES), F32),
        vmem((bins, 2 * LANES), BF16),
        vmem((bins, 2 * LANES), BF16),
        vmem((bins, LANES), F32),
        vmem(field, F32),
        vmem((bins, LANES), BF16),
        vmem((LANES, bins), BF16),
        vmem((lats, bins), BF16),
        vmem((2, n_row, lats, 2 * LANES), BF16),
        vmem((2, n_row, lats, 2 * LANES), BF16),
        vmem((2, lats, 2 * LANES), BF16),
        vmem((2, n_col, lats, 2 * LANES), BF16),
        vmem((lats, LANES), F32),
        vmem((n_col, part, LANES), F32),
        vmem((part, LANES), F32),
        vmem((n_row, part, LANES), F32),
        vmem((n_col, part, LANES), F32),
        vmem((2, 8, LANES), F32),
        vmem((n_row, 2, 8, LANES), F32),
        vmem((2 * LANES, lats), F32),
        vmem((LANES, tile_rows, LANES), F32),
        vmem((per_dev, lats), F32),
        dma((7,)),
        dma((tile_rows,)),
        dma((ROUNDS, 8)),
        dma((ROUNDS, 8)),
        dma((2,)),
        dma((2,)),
        dma((2,)),
        dma((2,)),
        dma((2,)),
        dma((2,)),
        dma((3,)),
        dma((3,)),
        dma((1,)),
        dma((1,)),
        pltpu.SemaphoreType.REGULAR,
        dma((6,)),
    ]
    anywhere = [pl.BlockSpec(memory_space=pl.ANY)] * 6
    results = pl.pallas_call(
        functools.partial(kernel, n_row, n_col),
        out_shape=out_shape,
        in_specs=anywhere,
        out_specs=anywhere,
        scratch_shapes=scratch,
        compiler_params=pltpu.CompilerParams(
            collective_id=0, has_side_effects=True, vmem_limit_bytes=56 * 1024 * 1024
        ),
    )(
        features.reshape(bins, genes),
        enc_weight.T,
        dec_weight.T,
        disc_weight,
        send_order.reshape(tile_rows, LANES),
        recv_order.reshape(tile_rows, LANES),
    )
    *others, grads = pl.pallas_call(
        hand_on,
        out_shape=out_shape,
        in_specs=anywhere,
        out_specs=anywhere,
        scratch_shapes=[*(vmem(one.shape, one.dtype) for one in out_shape), dma((6,)), dma((6,))],
    )(*results)
    return (*others, grads.reshape(2, lats, tile_rows, tile_cols))


def solution(mesh):
    in_specs = (P("row", "col", None), P(), P(), P(), P("row", "col", None), P("row", "col", None))
    out_specs = (
        P(("row", "col"), None),
        P(("row", "col"), None),
        P(),
        P(None, "row", "col"),
        P(None, "row", "col"),
        P(None, None, "row", "col"),
    )
    return jax.shard_map(
        per_device, mesh=mesh, in_specs=in_specs, out_specs=out_specs, check_vma=False
    )
```

```python
import functools
import math

import jax
import jax.numpy as jnp
from jax import lax
from jax.experimental import pallas as pl
from jax.experimental.pallas import tpu as pltpu
from jax.sharding import PartitionSpec as P

RADIUS = 3
RECON_WEIGHT = 10.0
LANES = 128
EDGE = 16
SIDE = 8
MESH = pl.DeviceIdType.MESH
F32 = jnp.float32
BF16 = jnp.bfloat16
DIRECTIONS = ((-1, 0), (1, 0), (0, -1), (0, 1), (-1, -1), (-1, 1), (1, -1), (1, 1))
OPPOSITE = (1, 0, 3, 2, 7, 6, 5, 4)
ROUNDS = 5
PACKED = {0: 0, 2: 1}
CHUNKS = 4


def stencil_taps():
    raw_taps = [math.exp(-offset * offset / 12.0) for offset in range(-RADIUS, RADIUS + 1)]
    tap_total = sum(raw_taps)
    return [raw_value / tap_total for raw_value in raw_taps]


def dot(a, b, ca=1, cb=0):
    return lax.dot_general(a, b, (((ca,), (cb,)), ((), ())), preferred_element_type=F32)


def each(count, body):
    def step(i, carry):
        body(i)
        return carry

    lax.fori_loop(0, count, step, 0)


def when(test):
    if isinstance(test, bool):
        return (lambda body: body()) if test else (lambda body: None)
    return pl.when(test)


def split_2(value):
    high = value.astype(BF16)
    low = (value - high.astype(F32)).astype(BF16)
    return jnp.concatenate([high, low], axis=1)


def kernel(
    n_row,
    n_col,
    feat_hbm,
    enc_hbm,
    dec_hbm,
    disc_hbm,
    send_hbm,
    recv_hbm,
    enc_hbm_out,
    dec_hbm_out,
    disc_hbm_out,
    emb_hbm_out,
    log_hbm_out,
    pg_hbm_out,
    enc_out,
    dec_out,
    disc_out,
    emb_out,
    log_out,
    pg_out,
    x,
    discw,
    orders,
    wcat,
    wtwice,
    gram2,
    bd_nt,
    bd_nn,
    send_pick,
    recv_pick,
    recv_pick_t,
    xp,
    xp_t,
    ex_src,
    ex_dst,
    low_in,
    pads,
    tmp,
    hsrc,
    h_row,
    h_col,
    h_corner,
    pack_src,
    h_pack,
    lat,
    emb,
    spread,
    summ,
    s_low,
    back,
    grads_2,
    summ_2,
    mix,
    eg,
    pg_low,
    lt,
    own,
    rs1_src,
    rs1_dst,
    rs2_src,
    rs2_dst,
    disc_src,
    disc_a,
    disc_bsrc,
    disc_b,
    disc_full,
    norm_src,
    norm_a,
    by_gene,
    stage,
    dec_sum,
    load_sem,
    feat_sem,
    hs_sem,
    hr_sem,
    as_sem,
    ar_sem,
    r1s_sem,
    r1r_sem,
    r2s_sem,
    r2r_sem,
    ds_sem,
    dr_sem,
    ns_sem,
    nr_sem,
    meet_sem,
    out_sem,
):
    n_dev = n_row * n_col
    bins, genes = x.shape
    rows = bins // LANES
    lats = discw.shape[1]
    portion = bins // n_dev
    n_group = n_row // 2
    few = min(4, n_group)
    width = 2 * LANES
    per_dev = genes // n_dev
    span = genes // n_group
    part = lats // n_col
    slope_scale = 2.0 * RECON_WEIGHT / genes
    tap = stencil_taps()
    chunk = bins // CHUNKS

    r = lax.axis_index("row")
    c = lax.axis_index("col")
    me = r * n_col + c
    my_group = r // 2
    lane = lax.broadcasted_iota(jnp.int32, (1, LANES), 1)
    first = lane < lats

    outs = [
        pltpu.make_async_copy(a, b, out_sem.at[i])
        for i, (a, b) in enumerate(
            [
                (enc_out, enc_hbm_out),
                (dec_out, dec_hbm_out),
                (disc_out, disc_hbm_out),
                (emb_out, emb_hbm_out),
                (log_out, log_hbm_out),
                (pg_out, pg_hbm_out),
            ]
        )
    ]

    def bins_of(i, size=LANES):
        return pl.ds(i * size if isinstance(i, int) else pl.multiple_of(i * size, size), size)

    def swap(value):
        return pltpu.roll(value, lats, value.ndim - 1)

    def halo_buffer(turn, way):
        if way < 2:
            return h_row.at[turn, way]
        if way < 4:
            return h_col.at[turn, way - 2]
        return h_corner.at[turn, way - 4]

    def halo_copy(turn, way):
        dr, dc = DIRECTIONS[way]
        row_part = pl.ds(0, RADIUS) if dr < 0 else pl.ds(rows - RADIUS, RADIUS) if dr else pl.ds(0, rows)
        col_part = pl.ds(0, EDGE) if dc < 0 else pl.ds(LANES - EDGE, EDGE) if dc else pl.ds(0, LANES)
        if way < 2 and turn in PACKED:
            source = pack_src.at[PACKED[turn], way]
            target = h_pack.at[PACKED[turn], OPPOSITE[way]]
        else:
            source = hsrc.at[turn, row_part, col_part]
            target = halo_buffer(turn, OPPOSITE[way])
        return pltpu.make_async_remote_copy(
            src_ref=source,
            dst_ref=target,
            send_sem=hs_sem.at[turn, way],
            recv_sem=hr_sem.at[turn, OPPOSITE[way]],
            device_id=(r + dr, c + dc),
            device_id_type=MESH,
        )

    def present(way):
        dr, dc = DIRECTIONS[way]
        tests = []
        if dr < 0:
            tests.append(r > 0)
        if dr > 0:
            tests.append(r < n_row - 1)
        if dc < 0:
            tests.append(c > 0)
        if dc > 0:
            tests.append(c < n_col - 1)
        return functools.reduce(jnp.logical_and, tests)

    def halo_start(turn):
        for way in range(8):

            @pl.when(present(way))
            def _():
                halo_copy(turn, way).start()

    def halo_take(turn):
        pad = pads.at[turn % 2]
        for way in range(8):

            @pl.when(present(way))
            def _():
                halo_copy(turn, OPPOSITE[way]).wait_recv()

        left, right = slice(0, SIDE), slice(SIDE + LANES, LANES + 2 * SIDE)
        top, bottom = slice(0, RADIUS), slice(RADIUS + rows, rows + 2 * RADIUS)
        for way, part in ((0, top), (1, bottom)):
            if turn in PACKED:
                packed = h_pack[PACKED[turn], way].astype(F32)
                halves = (packed, swap(packed)) if turn == 0 else (swap(packed), packed)
                pad[part, SIDE : SIDE + LANES // 2, :] = halves[0]
                pad[part, SIDE + LANES // 2 : SIDE + LANES, :] = halves[1]
            else:
                pad[part, SIDE : SIDE + LANES, :] = h_row[turn, way].astype(F32)
            pad[part, left, :] = h_corner[turn, 2 * way].astype(F32)[:, EDGE - SIDE :, :]
            pad[part, right, :] = h_corner[turn, 2 * way + 1].astype(F32)[:, :SIDE, :]
        own_rows = slice(RADIUS, RADIUS + rows)
        pad[own_rows, left, :] = h_col[turn, 0].astype(F32)[:, EDGE - SIDE :, :]
        pad[own_rows, right, :] = h_col[turn, 1].astype(F32)[:, :SIDE, :]

    def halo_finish(turn):
        for way in range(8):

            @pl.when(present(way))
            def _():
                halo_copy(turn, way).wait_send()

    def stencil(turn, then):
        pad = pads.at[turn % 2]

        def down(t):
            at = pl.ds(pl.multiple_of(t * SIDE, SIDE), SIDE)
            block = pad[:, at, :]
            across = tap[RADIUS] * block[RADIUS : RADIUS + rows]
            for k in range(1, RADIUS + 1):
                across += tap[RADIUS + k] * (
                    block[RADIUS - k : RADIUS - k + rows] + block[RADIUS + k : RADIUS + k + rows]
                )
            tmp[:, at, :] = across

        def along(i):
            total = tap[RADIUS] * tmp[i, SIDE : SIDE + LANES, :]
            for k in range(1, RADIUS + 1):
                total += tap[RADIUS + k] * (
                    tmp[i, SIDE - k : SIDE - k + LANES, :] + tmp[i, SIDE + k : SIDE + k + LANES, :]
                )
            then(i, total)

        each(LANES // SIDE + 2, down)
        each(rows, along)

    def put(turn, i, value):
        pads[turn % 2, i + RADIUS, SIDE : SIDE + LANES, :] = value
        low = value.astype(BF16)
        if turn not in PACKED:
            hsrc[turn, i] = low
            return
        hsrc[turn, i, 0:EDGE, :] = low[0:EDGE, :]
        hsrc[turn, i, LANES - EDGE :, :] = low[LANES - EDGE :, :]
        front, rear = value[: LANES // 2, :], value[LANES // 2 :, :]
        if turn == 0:
            packed = jnp.where(first, front, swap(rear)).astype(BF16)
        else:
            packed = jnp.where(first, swap(front), rear).astype(BF16)

        @when(i < RADIUS)
        def _():
            pack_src[PACKED[turn], 0, i] = packed

        @when(i >= rows - RADIUS)
        def _():
            pack_src[PACKED[turn], 1, i - (rows - RADIUS)] = packed

    loads = [
        pltpu.make_async_copy(a, b, load_sem.at[i])
        for i, (a, b) in enumerate(
            [
                (send_hbm, orders.at[0]),
                (recv_hbm, orders.at[1]),
                (dec_hbm, wcat.at[pl.ds(0, lats)]),
                (enc_hbm, wcat.at[pl.ds(lats, lats)]),
                (dec_hbm, wtwice.at[pl.ds(0, lats)]),
                (dec_hbm, wtwice.at[pl.ds(lats, lats)]),
                (disc_hbm, discw),
            ]
        )
    ]
    for load in loads[:4]:
        load.start()
    for i in range(rows):
        piece = pl.ds(i * LANES, LANES)
        copy = pltpu.make_async_copy(feat_hbm.at[piece], x.at[piece], feat_sem.at[i])
        copy.start()
    for load in loads[4:]:
        load.start()

    barrier = pltpu.get_barrier_semaphore()

    def greet_row(k, carry):
        other = lax.rem(r + k, n_row)
        pl.semaphore_signal(barrier, inc=1, device_id=(other, c), device_id_type=MESH)
        return carry

    def greet_col(k, carry):
        other = lax.rem(c + k, n_col)
        pl.semaphore_signal(barrier, inc=1, device_id=(r, other), device_id_type=MESH)
        return carry

    lax.fori_loop(1, n_row, greet_row, 0)
    lax.fori_loop(1, n_col, greet_col, 0)

    def build_send():
        def body(a):
            line = orders[0, pl.ds(a, 1), :].astype(F32)
            column = jnp.broadcast_to(line, (LANES, LANES)).T
            for t in range(rows):
                index = (lane + t * LANES).astype(F32)
                send_pick[bins_of(a), t * LANES : (t + 1) * LANES] = jnp.where(
                    column == index, 1.0, 0.0
                ).astype(BF16)

        each(rows, body)

    def build_recv():
        def body(a, carry):
            line = orders[1, pl.ds(a, 1), :].astype(F32)
            column = jnp.broadcast_to(line, (LANES, LANES)).T
            for t in range(rows):
                index = (lane + t * LANES).astype(F32)
                recv_pick[
                    pl.ds(pl.multiple_of(a * LANES, LANES), LANES), t * LANES : (t + 1) * LANES
                ] = jnp.where(column == index, 1.0, 0.0).astype(BF16)
            return carry

        lax.fori_loop(0, rows, body, 0)

    def build_recv_t():
        def body(t, carry):
            index = (lax.broadcasted_iota(jnp.int32, (LANES, 1), 0) + t * LANES).astype(F32)
            for a in range(rows):
                line = orders[1, a : a + 1, :].astype(F32)
                recv_pick_t[
                    pl.ds(pl.multiple_of(t * LANES, LANES), LANES), a * LANES : (a + 1) * LANES
                ] = jnp.where(line == index, 1.0, 0.0).astype(BF16)
            return carry

        lax.fori_loop(0, rows, body, 0)

    def ex_copy(which, k):
        other = lax.rem(me + k, n_dev)
        return pltpu.make_async_remote_copy(
            src_ref=ex_src.at[which, other],
            dst_ref=ex_dst.at[which, me],
            send_sem=as_sem.at[which],
            recv_sem=ar_sem.at[which],
            device_id=(other // n_col, lax.rem(other, n_col)),
            device_id_type=MESH,
        )

    def peers(count, make):
        def body(k, carry):
            make(k).start()
            return carry

        lax.fori_loop(1, count, body, 0)

    def drain(ref, count, send_sem, recv_sem):
        most = ref.at[pl.ds(0, count - 1)]
        pltpu.make_async_copy(most, most, recv_sem).wait()
        pltpu.make_async_copy(most, most, send_sem).wait()

    def ex_start(which):
        peers(n_dev, functools.partial(ex_copy, which))
        ex_dst[which, me] = ex_src[which, me]

    def ex_wait(which):
        drain(ex_dst.at[which], n_dev, as_sem.at[which], ar_sem.at[which])
        return ex_dst[which].reshape(bins, LANES)

    loads[0].wait()
    loads[1].wait()
    build_send()
    for way in range(8):

        @pl.when(jnp.logical_not(present(way)))
        def _():
            for turn in range(ROUNDS):
                if way < 2 and turn in PACKED:
                    empty = h_pack.at[PACKED[turn], way]
                else:
                    empty = halo_buffer(turn, way)
                empty[...] = jnp.zeros_like(empty)

    loads[2].wait()
    loads[3].wait()

    pl.semaphore_wait(barrier, n_row + n_col - 2)

    def greet_meet(k, carry):
        other = lax.rem(c + k, n_col)
        pl.semaphore_signal(meet_sem, inc=1, device_id=(r, other), device_id_type=MESH)
        return carry

    lax.fori_loop(1, n_col, greet_meet, 0)
    for k in range(rows):
        pltpu.make_async_copy(feat_hbm.at[bins_of(k)], x.at[bins_of(k)], feat_sem.at[k]).wait()
    flat = dot(wcat[...], x[...], 1, 1)
    xp_t[...] = flat
    picked = dot(flat.astype(BF16), send_pick[...], 1, 1)
    each_dev = LANES // portion
    for i in range(rows):
        block = picked[:, i * LANES : (i + 1) * LANES].T.astype(BF16)
        ex_src[0, i * each_dev : (i + 1) * each_dev] = block.reshape(each_dev, portion, LANES)

    pl.semaphore_wait(meet_sem, n_col - 1)

    ex_start(0)

    for i in range(rows):
        block = xp_t[:, i * LANES : (i + 1) * LANES].T
        xp[bins_of(i), :] = block
        put(0, i, swap(block.astype(BF16).astype(F32)))
    halo_start(0)
    build_recv()
    def elu(value):
        return jnp.where(value > 0, value, jnp.exp(jnp.minimum(value, 0.0)) - 1.0)

    def first_latent(i, value):
        lat[i] = value
        emb[i] = elu(value)

    halo_take(0)
    stencil(0, first_latent)

    arrived = ex_wait(0)
    low_in[...] = arrived

    def pick_in(i):
        value = dot(recv_pick[bins_of(i, chunk), :], low_in[...])
        for k in range(rows // CHUNKS):
            at = i * (rows // CHUNKS) + k
            put(1, at, jnp.where(first, emb[at], value[k * LANES : (k + 1) * LANES, :]))

    each(CHUNKS, pick_in)
    halo_start(1)
    build_recv_t()
    gram = dot(wcat[0:lats, :], wcat[0:lats, :], 1, 1)
    gram_high = gram.astype(BF16)
    gram_low = (gram - gram_high.astype(F32)).astype(BF16)
    gram2[...] = jnp.zeros_like(gram2)
    gram2[0:lats, 0:lats] = gram_high
    gram2[lats:, 0:lats] = gram_low

    def first_spread(i, value):
        out = elu(value)
        lat[i] = jnp.where(first, lat[i], value)
        emb[i] = jnp.where(first, emb[i], out)
        put(2, i, out)
        spread[i] = value

    halo_take(1)
    stencil(1, first_spread)
    halo_start(2)

    def after_spread(i):
        value = spread[i]
        here = bins_of(i)
        low = value.astype(BF16).astype(F32)
        summ[i] = jax.nn.sigmoid(value)
        s_low[here, :] = jnp.where(first, low, swap(low)).astype(BF16)
        lt[0:lats, here] = low.T[0:lats, :].astype(BF16)

    each(rows, after_spread)

    back[...] = slope_scale * (
        dot(s_low[...], gram2[...]) - jnp.where(first, xp[...], 0.0)
    )

    def rs1_copy(which, target):
        return pltpu.make_async_remote_copy(
            src_ref=rs1_src.at[which, target],
            dst_ref=rs1_dst.at[which, r],
            send_sem=r1s_sem.at[which],
            recv_sem=r1r_sem.at[which],
            device_id=(target, c),
            device_id_type=MESH,
        )

    def rs1_run(which, product):
        def body(k):
            part = lax.rem(my_group // few + 1 + k, n_group // few)
            where = bins_of(part, few * span)
            value = product(where).astype(BF16)
            for j in range(2 * few):
                at = (j // 2) * span + (j % 2) * LANES
                rs1_src[which, 2 * few * part + j] = value[:, at : at + width]
            for j in range(2 * few):

                @pl.when(2 * few * part + j != r)
                def _():
                    rs1_copy(which, 2 * few * part + j).start()

        each(n_group // few, body)

    def rs1_finish(which):
        drain(rs1_dst.at[which], n_row, r1s_sem.at[which], r1r_sem.at[which])
        rs1_dst[which, r] = rs1_src[which, r]
        total = rs1_dst[which, 0].astype(F32)
        for k in range(1, n_row):
            total += rs1_dst[which, k].astype(F32)
        rs2_src[which] = total.astype(BF16)

    def rs2_copy(which, k):
        other = lax.rem(c + k, n_col)
        return pltpu.make_async_remote_copy(
            src_ref=rs2_src.at[which],
            dst_ref=rs2_dst.at[which, c],
            send_sem=r2s_sem.at[which],
            recv_sem=r2r_sem.at[which],
            device_id=(r, other),
            device_id_type=MESH,
        )

    def rs2_start(which):
        peers(n_col, functools.partial(rs2_copy, which))
        rs2_dst[which, c] = rs2_src[which]

    def rs2_finish(which):
        drain(rs2_dst.at[which], n_col, r2s_sem.at[which], r2r_sem.at[which])
        total = rs2_dst[which, 0].astype(F32)
        for k in range(1, n_col):
            total += rs2_dst[which, k].astype(F32)
        begin = lax.rem(r, 2) * (width - span // 2)
        gene = lax.broadcasted_iota(jnp.int32, (1, width), 1) - begin
        own_genes = jnp.where((gene >= 0) & (gene < span // 2), total, 0.0)
        for k in range(width // LANES):
            by_gene[k * LANES : (k + 1) * LANES, :] = total[:, k * LANES : (k + 1) * LANES].T
        mine = by_gene[pl.ds(pl.multiple_of(begin + c * per_dev, 8), per_dev), :]
        norm_src[which] = jnp.broadcast_to(jnp.sum(own_genes * own_genes), (8, LANES))
        return mine

    square = dot(lt[0:lats, :], s_low[...])
    square_high = square.astype(BF16).astype(F32)
    square2 = jnp.where(first, square_high, square - square_high).astype(BF16)
    loads[4].wait()
    loads[5].wait()
    rs1_run(
        0,
        lambda where: slope_scale
        * (dot(square2, wtwice[:, where]) - dot(lt[0:lats, :], x[:, where])),
    )

    loads[6].wait()
    wide = jnp.concatenate([discw[...], jnp.zeros_like(discw)], axis=1)
    block = jnp.concatenate([wide, pltpu.roll(wide, lats, 1)], axis=0)
    block_high = block.astype(BF16)
    block_low = (block - block_high.astype(F32)).astype(BF16)
    for u in range(2):
        one = slice(u * LANES, (u + 1) * LANES)
        bd_nt[0:LANES, one] = block_high
        bd_nt[LANES:, one] = block_low
        bd_nn[one, 0:LANES] = block_high
        bd_nn[one, LANES:] = block_low
    for i in range(rows):
        stage[:, i, :] = emb[i].T
    emb_out[...] = stage[0:lats]
    outs[3].start()
    halo_take(2)

    def to_summary(i, value):
        summ[i] = jnp.where(first, summ[i], jax.nn.sigmoid(value))

    stencil(2, to_summary)

    half_sum = jnp.where(
        (lax.broadcasted_iota(jnp.int32, (LANES, LANES), 0) < lats)
        == (lax.broadcasted_iota(jnp.int32, (LANES, LANES), 1) < lats),
        1.0,
        0.0,
    ).astype(BF16)
    half_sum2 = jnp.concatenate([half_sum, half_sum], axis=0)

    step = rows // CHUNKS

    def contrast(i):
        piece = pl.ds(i * step, step)
        here = bins_of(i, chunk)
        summary = summ[piece].reshape(chunk, LANES)
        embedded = emb[piece].reshape(chunk, LANES)
        swapped = swap(embedded)
        summary_2 = split_2(summary)
        wide_q = dot(summary_2, bd_nt[...], 1, 1)
        queries = wide_q[:, :LANES] + wide_q[:, LANES:]
        logit_same = dot(split_2(embedded * queries), half_sum2)
        logit_other = dot(split_2(swapped * queries), half_sum2)
        grad_same = -jax.nn.sigmoid(-logit_same)
        grad_other = jax.nn.sigmoid(logit_other)
        embed_grad = grad_same * queries + swap(grad_other * queries)
        query_grad = grad_same * embedded + grad_other * swapped
        query_grad_2 = split_2(query_grad)
        grads_2[here, :] = query_grad_2
        summ_2[here, :] = summary_2
        wide_s = dot(query_grad_2, bd_nn[...])
        summary_grad = wide_s[:, :LANES] + wide_s[:, LANES:]
        spread_grad = summary_grad * summary * (1.0 - summary)
        spread_grad += back[here, :]
        eg[piece] = embed_grad.reshape(step, LANES, LANES)
        mix[here, :] = jnp.where(lax.rem(lane, lats) < lats // 2, logit_same, logit_other)
        for j in range(step):
            put(3, i * step + j, spread_grad[j * LANES : (j + 1) * LANES, :])

    for i in range(CHUNKS):
        contrast(i)
    halo_start(3)

    def disc_step(i, total):
        here = bins_of(i, chunk)
        return total + dot(grads_2[here, :], summ_2[here, :], 0, 0)

    disc_total = lax.fori_loop(
        0, CHUNKS, disc_step, jnp.zeros((2 * LANES, 2 * LANES), F32)
    )
    quarter = (disc_total[:LANES, :LANES] + disc_total[LANES:, :LANES]) + (
        disc_total[:LANES, LANES:] + disc_total[LANES:, LANES:]
    )
    disc_src[...] = quarter[:lats, :] + swap(quarter[lats:, :])

    def part_of(index):
        return pl.ds(pl.multiple_of(index * part, 8), part)

    def disc_1(k):
        other = lax.rem(c + k, n_col)
        return pltpu.make_async_remote_copy(
            src_ref=disc_src.at[part_of(other)],
            dst_ref=disc_a.at[c],
            send_sem=ds_sem.at[0],
            recv_sem=dr_sem.at[0],
            device_id=(r, other),
            device_id_type=MESH,
        )

    disc_a[c] = disc_src[part_of(c), :]
    peers(n_col, disc_1)

    for i in range(rows):
        flipped = mix[i * LANES : (i + 1) * LANES, :].T
        for k in range(4):
            at = k * (lats // 2)
            log_out[k, i : i + 1, :] = flipped[at : at + 1, :]
    outs[4].start()
    rs1_finish(0)
    rs2_start(0)

    halo_take(3)

    def to_latent_grad(i, value):
        z = lat[i]
        slope = jnp.where(z > 0, 1.0, jnp.exp(jnp.minimum(z, 0.0)))
        put(4, i, (eg[i] + value) * slope)

    stencil(3, to_latent_grad)
    halo_start(4)

    drain(disc_a, n_col, ds_sem.at[0], dr_sem.at[0])
    disc_bsrc[...] = jnp.sum(disc_a[...], axis=0)

    def disc_2(k):
        other = lax.rem(r + k, n_row)
        return pltpu.make_async_remote_copy(
            src_ref=disc_bsrc,
            dst_ref=disc_b.at[r],
            send_sem=ds_sem.at[1],
            recv_sem=dr_sem.at[1],
            device_id=(other, c),
            device_id_type=MESH,
        )

    disc_b[r] = disc_bsrc[...]
    peers(n_row, disc_2)
    dec_sum[...] = rs2_finish(0)

    halo_take(4)

    def to_proj_grad(i, value):
        pg_low[bins_of(i), :] = value.astype(BF16)

    stencil(4, to_proj_grad)

    def pick_back(i):
        value = dot(recv_pick_t[bins_of(i, chunk), :], pg_low[...])
        ex_src[1, pl.ds(i * (n_dev // CHUNKS), n_dev // CHUNKS)] = value.astype(BF16).reshape(
            n_dev // CHUNKS, portion, LANES
        )

    each(CHUNKS, pick_back)
    ex_start(1)
    for i in range(rows):
        here = slice(i * LANES, (i + 1) * LANES)
        flipped = pg_low[here, :].astype(F32).T
        stage[:, i, :] = flipped
        own[:, here] = flipped[:lats, :].astype(BF16)
    pg_out[...] = stage[...].astype(BF16)
    outs[5].start()

    drain(disc_b, n_row, ds_sem.at[1], dr_sem.at[1])
    disc_full[c] = jnp.sum(disc_b[...], axis=0)

    def disc_3(k):
        other = lax.rem(c + k, n_col)
        return pltpu.make_async_remote_copy(
            src_ref=disc_full.at[c],
            dst_ref=disc_full.at[c],
            send_sem=ds_sem.at[2],
            recv_sem=dr_sem.at[2],
            device_id=(r, other),
            device_id_type=MESH,
        )

    peers(n_col, disc_3)

    for turn in range(ROUNDS):
        halo_finish(turn)

    lt[0:lats, :] = own[...]
    home = ex_wait(1)
    flipped = jnp.concatenate(
        [home[i * LANES : (i + 1) * LANES, :].astype(F32).T[lats:, :] for i in range(rows)], axis=1
    ).astype(BF16)
    lt[lats:, :] = dot(flipped, send_pick[...]).astype(BF16)

    def encoder_part(where):
        value = dot(lt[...], x[:, where])
        return value[:lats, :] + value[lats:, :]

    rs1_run(1, encoder_part)

    drain(disc_full, n_col, ds_sem.at[2], dr_sem.at[2])
    disc_grad = disc_full[...].reshape(lats, LANES)[:, :lats]
    disc_mean = jnp.sum(disc_grad * disc_grad) / (lats * lats)
    disc_out[...] = disc_grad * lax.rsqrt(disc_mean + 1e-06)
    outs[2].start()

    rs1_finish(1)
    rs2_start(1)
    enc_sum = rs2_finish(1)

    def norm_1(k):
        other = lax.rem(r + k, n_row)
        return pltpu.make_async_remote_copy(
            src_ref=norm_src,
            dst_ref=norm_a.at[r],
            send_sem=ns_sem.at[0],
            recv_sem=nr_sem.at[0],
            device_id=(other, c),
            device_id_type=MESH,
        )

    norm_a[r] = norm_src[...]
    peers(n_row, norm_1)
    drain(norm_a, n_row, ns_sem.at[0], nr_sem.at[0])
    totals = jnp.sum(norm_a[...], axis=0)
    entries = genes * lats
    enc_out[...] = enc_sum * lax.rsqrt(totals[1, 0:1, 0:1] / entries + 1e-06)
    dec_out[...] = dec_sum[...] * lax.rsqrt(totals[0, 0:1, 0:1] / entries + 1e-06)
    outs[0].start()
    outs[1].start()
    for out in outs:
        out.wait()


def hand_on(*refs):
    count = (len(refs) - 2) // 3
    sources, targets, held = (refs[k * count : (k + 1) * count] for k in range(3))
    come, go = refs[3 * count :]
    ins = [pltpu.make_async_copy(sources[i], held[i], come.at[i]) for i in range(count)]
    outs = [pltpu.make_async_copy(held[i], targets[i], go.at[i]) for i in range(count)]
    for copy in ins:
        copy.start()
    for i in range(count):
        ins[i].wait()
        outs[i].start()
    for copy in outs:
        copy.wait()


def per_device(features, enc_weight, dec_weight, disc_weight, send_order, recv_order):
    tile_rows, tile_cols, genes = features.shape
    lats = enc_weight.shape[1]
    bins = tile_rows * tile_cols
    n_row = lax.axis_size("row")
    n_col = lax.axis_size("col")
    n_dev = n_row * n_col
    n_group = n_row // 2
    per_dev = genes // n_dev
    span = genes // n_group
    part = lats // n_col
    portion = bins // n_dev
    field = (tile_rows, LANES, LANES)
    dma = pltpu.SemaphoreType.DMA
    vmem = pltpu.VMEM
    shape = jax.ShapeDtypeStruct
    out_shape = [
        shape((per_dev, lats), F32),
        shape((per_dev, lats), F32),
        shape((lats, lats), F32),
        shape((lats, tile_rows, tile_cols), F32),
        shape((4, tile_rows, tile_cols), F32),
        shape((2 * lats, tile_rows, tile_cols), BF16),
    ]
    scratch = [
        *(vmem(one.shape, one.dtype) for one in out_shape),
        vmem((bins, genes), BF16),
        vmem((lats, lats), F32),
        vmem((2, tile_rows, LANES), jnp.int32),
        vmem((2 * lats, genes), BF16),
        vmem((2 * lats, genes), BF16),
        vmem((LANES, LANES), BF16),
        vmem((2 * LANES, 2 * LANES), BF16),
        vmem((2 * LANES, 2 * LANES), BF16),
        vmem((bins, bins), BF16),
        vmem((bins, bins), BF16),
        vmem((bins, bins), BF16),
        vmem((bins, LANES), F32),
        vmem((LANES, bins), F32),
        vmem((2, n_dev, portion, LANES), BF16),
        vmem((2, n_dev, portion, LANES), BF16),
        vmem((bins, LANES), BF16),
        vmem((2, tile_rows + 2 * RADIUS, LANES + 2 * SIDE, LANES), F32),
        vmem((tile_rows, LANES + 2 * SIDE, LANES), F32),
        vmem((ROUNDS,) + field, BF16),
        vmem((ROUNDS, 2, RADIUS, LANES, LANES), BF16),
        vmem((ROUNDS, 2, tile_rows, EDGE, LANES), BF16),
        vmem((ROUNDS, 4, RADIUS, EDGE, LANES), BF16),
        vmem((len(PACKED), 2, RADIUS, LANES // 2, LANES), BF16),
        vmem((len(PACKED), 2, RADIUS, LANES // 2, LANES), BF16),
        vmem(field, F32),
        vmem(field, F32),
        vmem(field, F32),
        vmem(field, F32),
        vmem((bins, LANES), BF16),
        vmem((bins, LANES), F32),
        vmem((bins, 2 * LANES), BF16),
        vmem((bins, 2 * LANES), BF16),
        vmem((bins, LANES), F32),
        vmem(field, F32),
        vmem((bins, LANES), BF16),
        vmem((LANES, bins), BF16),
        vmem((lats, bins), BF16),
        vmem((2, n_row, lats, 2 * LANES), BF16),
        vmem((2, n_row, lats, 2 * LANES), BF16),
        vmem((2, lats, 2 * LANES), BF16),
        vmem((2, n_col, lats, 2 * LANES), BF16),
        vmem((lats, LANES), F32),
        vmem((n_col, part, LANES), F32),
        vmem((part, LANES), F32),
        vmem((n_row, part, LANES), F32),
        vmem((n_col, part, LANES), F32),
        vmem((2, 8, LANES), F32),
        vmem((n_row, 2, 8, LANES), F32),
        vmem((2 * LANES, lats), F32),
        vmem((LANES, tile_rows, LANES), F32),
        vmem((per_dev, lats), F32),
        dma((7,)),
        dma((tile_rows,)),
        dma((ROUNDS, 8)),
        dma((ROUNDS, 8)),
        dma((2,)),
        dma((2,)),
        dma((2,)),
        dma((2,)),
        dma((2,)),
        dma((2,)),
        dma((3,)),
        dma((3,)),
        dma((1,)),
        dma((1,)),
        pltpu.SemaphoreType.REGULAR,
        dma((6,)),
    ]
    anywhere = [pl.BlockSpec(memory_space=pl.ANY)] * 6
    results = pl.pallas_call(
        functools.partial(kernel, n_row, n_col),
        out_shape=out_shape,
        in_specs=anywhere,
        out_specs=anywhere,
        scratch_shapes=scratch,
        compiler_params=pltpu.CompilerParams(
            collective_id=0, has_side_effects=True, vmem_limit_bytes=56 * 1024 * 1024
        ),
    )(
        features.reshape(bins, genes),
        enc_weight.T,
        dec_weight.T,
        disc_weight,
        send_order.reshape(tile_rows, LANES),
        recv_order.reshape(tile_rows, LANES),
    )
    *others, grads = pl.pallas_call(
        hand_on,
        out_shape=out_shape,
        in_specs=anywhere,
        out_specs=anywhere,
        scratch_shapes=[*(vmem(one.shape, one.dtype) for one in out_shape), dma((6,)), dma((6,))],
    )(*results)
    return (*others, grads.reshape(2, lats, tile_rows, tile_cols))


def solution(mesh):
    in_specs = (P("row", "col", None), P(), P(), P(), P("row", "col", None), P("row", "col", None))
    out_specs = (
        P(("row", "col"), None),
        P(("row", "col"), None),
        P(),
        P(None, "row", "col"),
        P(None, "row", "col"),
        P(None, None, "row", "col"),
    )
    return jax.shard_map(
        per_device, mesh=mesh, in_specs=in_specs, out_specs=out_specs, check_vma=False
    )
```

```python
import functools
import math

import jax
import jax.numpy as jnp
from jax import lax
from jax.experimental import pallas as pl
from jax.experimental.pallas import tpu as pltpu
from jax.sharding import PartitionSpec as P

RADIUS = 3
RECON_WEIGHT = 10.0
LANES = 128
EDGE = 16
SIDE = 8
MESH = pl.DeviceIdType.MESH
F32 = jnp.float32
BF16 = jnp.bfloat16
DIRECTIONS = ((-1, 0), (1, 0), (0, -1), (0, 1), (-1, -1), (-1, 1), (1, -1), (1, 1))
OPPOSITE = (1, 0, 3, 2, 7, 6, 5, 4)
ROUNDS = 5
PACKED = {0: 0, 2: 1}
CHUNKS = 4


def stencil_taps():
    raw_taps = [math.exp(-offset * offset / 12.0) for offset in range(-RADIUS, RADIUS + 1)]
    tap_total = sum(raw_taps)
    return [raw_value / tap_total for raw_value in raw_taps]


def dot(a, b, ca=1, cb=0):
    return lax.dot_general(a, b, (((ca,), (cb,)), ((), ())), preferred_element_type=F32)


def each(count, body):
    def step(i, carry):
        body(i)
        return carry

    lax.fori_loop(0, count, step, 0)


def when(test):
    if isinstance(test, bool):
        return (lambda body: body()) if test else (lambda body: None)
    return pl.when(test)


def split_2(value):
    high = value.astype(BF16)
    low = (value - high.astype(F32)).astype(BF16)
    return jnp.concatenate([high, low], axis=1)


def kernel(
    n_row,
    n_col,
    feat_hbm,
    enc_hbm,
    dec_hbm,
    disc_hbm,
    send_hbm,
    recv_hbm,
    enc_hbm_out,
    dec_hbm_out,
    disc_hbm_out,
    emb_hbm_out,
    log_hbm_out,
    pg_hbm_out,
    enc_out,
    dec_out,
    disc_out,
    emb_out,
    log_out,
    pg_out,
    x,
    discw,
    orders,
    wcat,
    wtwice,
    gram2,
    bd_nt,
    bd_nn,
    send_pick,
    recv_pick,
    recv_pick_t,
    xp,
    xp_t,
    row_src,
    row_dst,
    col_src,
    col_dst,
    ex_src,
    ex_dst,
    low_in,
    pads,
    tmp,
    hsrc,
    h_row,
    h_col,
    h_corner,
    pack_src,
    h_pack,
    lat,
    emb,
    spread,
    summ,
    s_low,
    back,
    grads_2,
    summ_2,
    mix,
    eg,
    pg_low,
    lt,
    own,
    rs1_src,
    rs1_dst,
    rs2_src,
    rs2_dst,
    disc_src,
    disc_a,
    disc_bsrc,
    disc_b,
    disc_full,
    norm_src,
    norm_a,
    by_gene,
    stage,
    dec_sum,
    load_sem,
    feat_sem,
    hs_sem,
    hr_sem,
    as_sem,
    ar_sem,
    r1s_sem,
    r1r_sem,
    r2s_sem,
    r2r_sem,
    ds_sem,
    dr_sem,
    ns_sem,
    nr_sem,
    meet_sem,
    out_sem,
):
    n_dev = n_row * n_col
    bins, genes = x.shape
    rows = bins // LANES
    lats = discw.shape[1]
    portion = bins // n_dev
    n_group = n_row // 2
    few = min(4, n_group)
    width = 2 * LANES
    per_dev = genes // n_dev
    span = genes // n_group
    part = lats // n_col
    slope_scale = 2.0 * RECON_WEIGHT / genes
    tap = stencil_taps()
    chunk = bins // CHUNKS

    r = lax.axis_index("row")
    c = lax.axis_index("col")
    me = r * n_col + c
    my_group = r // 2
    lane = lax.broadcasted_iota(jnp.int32, (1, LANES), 1)
    first = lane < lats

    outs = [
        pltpu.make_async_copy(a, b, out_sem.at[i])
        for i, (a, b) in enumerate(
            [
                (enc_out, enc_hbm_out),
                (dec_out, dec_hbm_out),
                (disc_out, disc_hbm_out),
                (emb_out, emb_hbm_out),
                (log_out, log_hbm_out),
                (pg_out, pg_hbm_out),
            ]
        )
    ]

    def bins_of(i, size=LANES):
        return pl.ds(i * size if isinstance(i, int) else pl.multiple_of(i * size, size), size)

    def swap(value):
        return pltpu.roll(value, lats, value.ndim - 1)

    def halo_buffer(turn, way):
        if way < 2:
            return h_row.at[turn, way]
        if way < 4:
            return h_col.at[turn, way - 2]
        return h_corner.at[turn, way - 4]

    def halo_copy(turn, way):
        dr, dc = DIRECTIONS[way]
        row_part = pl.ds(0, RADIUS) if dr < 0 else pl.ds(rows - RADIUS, RADIUS) if dr else pl.ds(0, rows)
        col_part = pl.ds(0, EDGE) if dc < 0 else pl.ds(LANES - EDGE, EDGE) if dc else pl.ds(0, LANES)
        if way < 2 and turn in PACKED:
            source = pack_src.at[PACKED[turn], way]
            target = h_pack.at[PACKED[turn], OPPOSITE[way]]
        else:
            source = hsrc.at[turn, row_part, col_part]
            target = halo_buffer(turn, OPPOSITE[way])
        return pltpu.make_async_remote_copy(
            src_ref=source,
            dst_ref=target,
            send_sem=hs_sem.at[turn, way],
            recv_sem=hr_sem.at[turn, OPPOSITE[way]],
            device_id=(r + dr, c + dc),
            device_id_type=MESH,
        )

    def present(way):
        dr, dc = DIRECTIONS[way]
        tests = []
        if dr < 0:
            tests.append(r > 0)
        if dr > 0:
            tests.append(r < n_row - 1)
        if dc < 0:
            tests.append(c > 0)
        if dc > 0:
            tests.append(c < n_col - 1)
        return functools.reduce(jnp.logical_and, tests)

    def halo_start(turn):
        for way in range(8):

            @pl.when(present(way))
            def _():
                halo_copy(turn, way).start()

    def halo_take(turn):
        pad = pads.at[turn % 2]
        for way in range(8):

            @pl.when(present(way))
            def _():
                halo_copy(turn, OPPOSITE[way]).wait_recv()

        left, right = slice(0, SIDE), slice(SIDE + LANES, LANES + 2 * SIDE)
        top, bottom = slice(0, RADIUS), slice(RADIUS + rows, rows + 2 * RADIUS)
        for way, part in ((0, top), (1, bottom)):
            if turn in PACKED:
                packed = h_pack[PACKED[turn], way].astype(F32)
                halves = (packed, swap(packed)) if turn == 0 else (swap(packed), packed)
                pad[part, SIDE : SIDE + LANES // 2, :] = halves[0]
                pad[part, SIDE + LANES // 2 : SIDE + LANES, :] = halves[1]
            else:
                pad[part, SIDE : SIDE + LANES, :] = h_row[turn, way].astype(F32)
            pad[part, left, :] = h_corner[turn, 2 * way].astype(F32)[:, EDGE - SIDE :, :]
            pad[part, right, :] = h_corner[turn, 2 * way + 1].astype(F32)[:, :SIDE, :]
        own_rows = slice(RADIUS, RADIUS + rows)
        pad[own_rows, left, :] = h_col[turn, 0].astype(F32)[:, EDGE - SIDE :, :]
        pad[own_rows, right, :] = h_col[turn, 1].astype(F32)[:, :SIDE, :]

    def halo_finish(turn):
        for way in range(8):

            @pl.when(present(way))
            def _():
                halo_copy(turn, way).wait_send()

    def stencil(turn, then):
        pad = pads.at[turn % 2]

        def down(t):
            at = pl.ds(pl.multiple_of(t * SIDE, SIDE), SIDE)
            block = pad[:, at, :]
            across = tap[RADIUS] * block[RADIUS : RADIUS + rows]
            for k in range(1, RADIUS + 1):
                across += tap[RADIUS + k] * (
                    block[RADIUS - k : RADIUS - k + rows] + block[RADIUS + k : RADIUS + k + rows]
                )
            tmp[:, at, :] = across

        def along(i):
            total = tap[RADIUS] * tmp[i, SIDE : SIDE + LANES, :]
            for k in range(1, RADIUS + 1):
                total += tap[RADIUS + k] * (
                    tmp[i, SIDE - k : SIDE - k + LANES, :] + tmp[i, SIDE + k : SIDE + k + LANES, :]
                )
            then(i, total)

        each(LANES // SIDE + 2, down)
        each(rows, along)

    def put(turn, i, value):
        pads[turn % 2, i + RADIUS, SIDE : SIDE + LANES, :] = value
        low = value.astype(BF16)
        if turn not in PACKED:
            hsrc[turn, i] = low
            return
        hsrc[turn, i, 0:EDGE, :] = low[0:EDGE, :]
        hsrc[turn, i, LANES - EDGE :, :] = low[LANES - EDGE :, :]
        front, rear = value[: LANES // 2, :], value[LANES // 2 :, :]
        if turn == 0:
            packed = jnp.where(first, front, swap(rear)).astype(BF16)
        else:
            packed = jnp.where(first, swap(front), rear).astype(BF16)

        @when(i < RADIUS)
        def _():
            pack_src[PACKED[turn], 0, i] = packed

        @when(i >= rows - RADIUS)
        def _():
            pack_src[PACKED[turn], 1, i - (rows - RADIUS)] = packed

    loads = [
        pltpu.make_async_copy(a, b, load_sem.at[i])
        for i, (a, b) in enumerate(
            [
                (send_hbm, orders.at[0]),
                (recv_hbm, orders.at[1]),
                (dec_hbm, wcat.at[pl.ds(0, lats)]),
                (enc_hbm, wcat.at[pl.ds(lats, lats)]),
                (dec_hbm, wtwice.at[pl.ds(0, lats)]),
                (dec_hbm, wtwice.at[pl.ds(lats, lats)]),
                (disc_hbm, discw),
            ]
        )
    ]
    for load in loads[:4]:
        load.start()
    for i in range(rows):
        piece = pl.ds(i * LANES, LANES)
        copy = pltpu.make_async_copy(feat_hbm.at[piece], x.at[piece], feat_sem.at[i])
        copy.start()
    for load in loads[4:]:
        load.start()

    barrier = pltpu.get_barrier_semaphore()

    def greet_row(k, carry):
        other = lax.rem(r + k, n_row)
        pl.semaphore_signal(barrier, inc=1, device_id=(other, c), device_id_type=MESH)
        return carry

    def greet_col(k, carry):
        other = lax.rem(c + k, n_col)
        pl.semaphore_signal(barrier, inc=1, device_id=(r, other), device_id_type=MESH)
        return carry

    lax.fori_loop(1, n_row, greet_row, 0)
    lax.fori_loop(1, n_col, greet_col, 0)

    def build_send():
        def body(a):
            line = orders[0, pl.ds(a, 1), :].astype(F32)
            column = jnp.broadcast_to(line, (LANES, LANES)).T
            for t in range(rows):
                index = (lane + t * LANES).astype(F32)
                send_pick[bins_of(a), t * LANES : (t + 1) * LANES] = jnp.where(
                    column == index, 1.0, 0.0
                ).astype(BF16)

        each(rows, body)

    def build_recv():
        def body(a, carry):
            line = orders[1, pl.ds(a, 1), :].astype(F32)
            column = jnp.broadcast_to(line, (LANES, LANES)).T
            for t in range(rows):
                index = recv_index(lane + t * LANES)
                recv_pick[
                    pl.ds(pl.multiple_of(a * LANES, LANES), LANES), t * LANES : (t + 1) * LANES
                ] = jnp.where(column == index, 1.0, 0.0).astype(BF16)
            return carry

        lax.fori_loop(0, rows, body, 0)

    def build_recv_t():
        def body(t, carry):
            index = (lax.broadcasted_iota(jnp.int32, (LANES, 1), 0) + t * LANES).astype(F32)
            for a in range(rows):
                line = orders[1, a : a + 1, :].astype(F32)
                recv_pick_t[
                    pl.ds(pl.multiple_of(t * LANES, LANES), LANES), a * LANES : (a + 1) * LANES
                ] = jnp.where(line == index, 1.0, 0.0).astype(BF16)
            return carry

        lax.fori_loop(0, rows, body, 0)

    def regroup(values):
        m = values.shape[0] // 2
        n = values.shape[1] // portion
        low, high = values[:m], values[m:]
        parts = []
        for value in (jnp.where(first, low, swap(high)), jnp.where(first, swap(low), high)):
            for k in range(n):
                block = value[:, k * portion : (k + 1) * portion, :]
                parts.append(block.reshape(m * portion, LANES))
        return parts

    def row_copy(k):
        other = lax.rem(r + k, n_row)
        return pltpu.make_async_remote_copy(
            src_ref=row_src.at[other],
            dst_ref=row_dst.at[r],
            send_sem=as_sem.at[0],
            recv_sem=ar_sem.at[0],
            device_id=(other, c),
            device_id_type=MESH,
        )

    def col_copy(k):
        other = lax.rem(c + k, n_col)
        return pltpu.make_async_remote_copy(
            src_ref=col_src.at[other],
            dst_ref=col_dst.at[c],
            send_sem=as_sem.at[1],
            recv_sem=ar_sem.at[1],
            device_id=(r, other),
            device_id_type=MESH,
        )

    def ex_copy(k):
        other = lax.rem(me + k, n_dev)
        return pltpu.make_async_remote_copy(
            src_ref=ex_src.at[other],
            dst_ref=ex_dst.at[me],
            send_sem=as_sem.at[2],
            recv_sem=ar_sem.at[2],
            device_id=(other // n_col, lax.rem(other, n_col)),
            device_id_type=MESH,
        )

    def peers(count, make):
        def body(k, carry):
            make(k).start()
            return carry

        lax.fori_loop(1, count, body, 0)

    def drain(ref, count, send_sem, recv_sem):
        most = ref.at[pl.ds(0, count - 1)]
        pltpu.make_async_copy(most, most, recv_sem).wait()
        pltpu.make_async_copy(most, most, send_sem).wait()

    def recv_index(position):
        slot = lax.rem(position, portion)
        rest = position // portion
        low_row = lax.rem(rest, n_row // 2)
        rest = rest // (n_row // 2)
        col = lax.rem(rest, n_col)
        row = (rest // n_col) * (n_row // 2) + low_row
        return (((row * n_col) + col) * portion + slot).astype(F32)

    loads[0].wait()
    loads[1].wait()
    build_send()
    for way in range(8):

        @pl.when(jnp.logical_not(present(way)))
        def _():
            for turn in range(ROUNDS):
                if way < 2 and turn in PACKED:
                    empty = h_pack.at[PACKED[turn], way]
                else:
                    empty = halo_buffer(turn, way)
                empty[...] = jnp.zeros_like(empty)

    loads[2].wait()
    loads[3].wait()

    pl.semaphore_wait(barrier, n_row + n_col - 2)

    def greet_meet(k, carry):
        other = lax.rem(c + k, n_col)
        pl.semaphore_signal(meet_sem, inc=1, device_id=(r, other), device_id_type=MESH)
        return carry

    lax.fori_loop(1, n_col, greet_meet, 0)
    for k in range(rows):
        pltpu.make_async_copy(feat_hbm.at[bins_of(k)], x.at[bins_of(k)], feat_sem.at[k]).wait()
    flat = dot(wcat[...], x[...], 1, 1)
    xp_t[...] = flat
    picked = dot(flat.astype(BF16), send_pick[...], 1, 1)
    turned = jnp.concatenate(
        [picked[:, i * LANES : (i + 1) * LANES].T for i in range(rows)], axis=0
    ).reshape(n_row, 2, n_col // 2 * portion, LANES)
    row_src[...] = jnp.where(first, swap(turned[:, 0]), turned[:, 1]).astype(BF16)

    pl.semaphore_wait(meet_sem, n_col - 1)

    peers(n_row, row_copy)
    row_dst[r] = row_src[r]

    for i in range(rows):
        block = xp_t[:, i * LANES : (i + 1) * LANES].T
        xp[bins_of(i), :] = block
        put(0, i, swap(block.astype(BF16).astype(F32)))
    halo_start(0)
    build_recv()
    drain(row_dst, n_row, as_sem.at[0], ar_sem.at[0])
    for k, value in enumerate(regroup(row_dst[...].astype(F32))):
        col_src[k] = value.astype(BF16)
    peers(n_col, col_copy)
    col_dst[c] = col_src[c]

    def elu(value):
        return jnp.where(value > 0, value, jnp.exp(jnp.minimum(value, 0.0)) - 1.0)

    def first_latent(i, value):
        lat[i] = value
        emb[i] = elu(value)

    halo_take(0)
    stencil(0, first_latent)

    drain(col_dst, n_col, as_sem.at[1], ar_sem.at[1])
    low_in[...] = col_dst[...].reshape(bins // 2, LANES)

    def pick_in(i):
        here = bins_of(i, chunk)
        value = swap(dot(recv_pick[here, : bins // 2], low_in[...])) + dot(
            recv_pick[here, bins // 2 :], low_in[...]
        )
        for k in range(rows // CHUNKS):
            at = i * (rows // CHUNKS) + k
            put(1, at, jnp.where(first, emb[at], value[k * LANES : (k + 1) * LANES, :]))

    each(CHUNKS, pick_in)
    halo_start(1)
    build_recv_t()
    gram = dot(wcat[0:lats, :], wcat[0:lats, :], 1, 1)
    gram_high = gram.astype(BF16)
    gram_low = (gram - gram_high.astype(F32)).astype(BF16)
    gram2[...] = jnp.zeros_like(gram2)
    gram2[0:lats, 0:lats] = gram_high
    gram2[lats:, 0:lats] = gram_low

    def first_spread(i, value):
        out = elu(value)
        lat[i] = jnp.where(first, lat[i], value)
        emb[i] = jnp.where(first, emb[i], out)
        put(2, i, out)
        spread[i] = value

    halo_take(1)
    stencil(1, first_spread)
    halo_start(2)

    def after_spread(i):
        value = spread[i]
        here = bins_of(i)
        low = value.astype(BF16).astype(F32)
        summ[i] = jax.nn.sigmoid(value)
        s_low[here, :] = jnp.where(first, low, swap(low)).astype(BF16)
        lt[0:lats, here] = low.T[0:lats, :].astype(BF16)

    each(rows, after_spread)

    back[...] = slope_scale * (
        dot(s_low[...], gram2[...]) - jnp.where(first, xp[...], 0.0)
    )

    def rs1_copy(which, target):
        return pltpu.make_async_remote_copy(
            src_ref=rs1_src.at[which, target],
            dst_ref=rs1_dst.at[which, r],
            send_sem=r1s_sem.at[which],
            recv_sem=r1r_sem.at[which],
            device_id=(target, c),
            device_id_type=MESH,
        )

    def rs1_run(which, product):
        def body(k):
            part = lax.rem(my_group // few + 1 + k, n_group // few)
            where = bins_of(part, few * span)
            value = product(where).astype(BF16)
            for j in range(2 * few):
                at = (j // 2) * span + (j % 2) * LANES
                rs1_src[which, 2 * few * part + j] = value[:, at : at + width]
            for j in range(2 * few):

                @pl.when(2 * few * part + j != r)
                def _():
                    rs1_copy(which, 2 * few * part + j).start()

        each(n_group // few, body)

    def rs1_finish(which):
        drain(rs1_dst.at[which], n_row, r1s_sem.at[which], r1r_sem.at[which])
        rs1_dst[which, r] = rs1_src[which, r]
        total = rs1_dst[which, 0].astype(F32)
        for k in range(1, n_row):
            total += rs1_dst[which, k].astype(F32)
        rs2_src[which] = total.astype(BF16)

    def rs2_copy(which, k):
        other = lax.rem(c + k, n_col)
        return pltpu.make_async_remote_copy(
            src_ref=rs2_src.at[which],
            dst_ref=rs2_dst.at[which, c],
            send_sem=r2s_sem.at[which],
            recv_sem=r2r_sem.at[which],
            device_id=(r, other),
            device_id_type=MESH,
        )

    def rs2_start(which):
        peers(n_col, functools.partial(rs2_copy, which))
        rs2_dst[which, c] = rs2_src[which]

    def rs2_finish(which):
        drain(rs2_dst.at[which], n_col, r2s_sem.at[which], r2r_sem.at[which])
        total = rs2_dst[which, 0].astype(F32)
        for k in range(1, n_col):
            total += rs2_dst[which, k].astype(F32)
        begin = lax.rem(r, 2) * (width - span // 2)
        gene = lax.broadcasted_iota(jnp.int32, (1, width), 1) - begin
        own_genes = jnp.where((gene >= 0) & (gene < span // 2), total, 0.0)
        for k in range(width // LANES):
            by_gene[k * LANES : (k + 1) * LANES, :] = total[:, k * LANES : (k + 1) * LANES].T
        mine = by_gene[pl.ds(pl.multiple_of(begin + c * per_dev, 8), per_dev), :]
        norm_src[which] = jnp.broadcast_to(jnp.sum(own_genes * own_genes), (8, LANES))
        return mine

    loads[6].wait()
    wide = jnp.concatenate([discw[...], jnp.zeros_like(discw)], axis=1)
    block = jnp.concatenate([wide, pltpu.roll(wide, lats, 1)], axis=0)
    block_high = block.astype(BF16)
    block_low = (block - block_high.astype(F32)).astype(BF16)
    for u in range(2):
        one = slice(u * LANES, (u + 1) * LANES)
        bd_nt[0:LANES, one] = block_high
        bd_nt[LANES:, one] = block_low
        bd_nn[one, 0:LANES] = block_high
        bd_nn[one, LANES:] = block_low
    for i in range(rows):
        stage[:, i, :] = emb[i].T
    emb_out[...] = stage[0:lats]
    outs[3].start()
    halo_take(2)

    def to_summary(i, value):
        summ[i] = jnp.where(first, summ[i], jax.nn.sigmoid(value))

    stencil(2, to_summary)

    half_sum = jnp.where(
        (lax.broadcasted_iota(jnp.int32, (LANES, LANES), 0) < lats)
        == (lax.broadcasted_iota(jnp.int32, (LANES, LANES), 1) < lats),
        1.0,
        0.0,
    ).astype(BF16)
    half_sum2 = jnp.concatenate([half_sum, half_sum], axis=0)

    step = rows // CHUNKS

    def contrast(i):
        piece = pl.ds(i * step, step)
        here = bins_of(i, chunk)
        summary = summ[piece].reshape(chunk, LANES)
        embedded = emb[piece].reshape(chunk, LANES)
        swapped = swap(embedded)
        summary_2 = split_2(summary)
        wide_q = dot(summary_2, bd_nt[...], 1, 1)
        queries = wide_q[:, :LANES] + wide_q[:, LANES:]
        logit_same = dot(split_2(embedded * queries), half_sum2)
        logit_other = dot(split_2(swapped * queries), half_sum2)
        grad_same = -jax.nn.sigmoid(-logit_same)
        grad_other = jax.nn.sigmoid(logit_other)
        embed_grad = grad_same * queries + swap(grad_other * queries)
        query_grad = grad_same * embedded + grad_other * swapped
        query_grad_2 = split_2(query_grad)
        grads_2[here, :] = query_grad_2
        summ_2[here, :] = summary_2
        wide_s = dot(query_grad_2, bd_nn[...])
        summary_grad = wide_s[:, :LANES] + wide_s[:, LANES:]
        spread_grad = summary_grad * summary * (1.0 - summary)
        spread_grad += back[here, :]
        eg[piece] = embed_grad.reshape(step, LANES, LANES)
        mix[here, :] = jnp.where(lax.rem(lane, lats) < lats // 2, logit_same, logit_other)
        for j in range(step):
            put(3, i * step + j, spread_grad[j * LANES : (j + 1) * LANES, :])

    for i in range(CHUNKS):
        contrast(i)
    halo_start(3)

    def disc_step(i, total):
        here = bins_of(i, chunk)
        return total + dot(grads_2[here, :], summ_2[here, :], 0, 0)

    disc_total = lax.fori_loop(
        0, CHUNKS, disc_step, jnp.zeros((2 * LANES, 2 * LANES), F32)
    )
    quarter = (disc_total[:LANES, :LANES] + disc_total[LANES:, :LANES]) + (
        disc_total[:LANES, LANES:] + disc_total[LANES:, LANES:]
    )
    disc_src[...] = quarter[:lats, :] + swap(quarter[lats:, :])

    def part_of(index):
        return pl.ds(pl.multiple_of(index * part, 8), part)

    def disc_1(k):
        other = lax.rem(c + k, n_col)
        return pltpu.make_async_remote_copy(
            src_ref=disc_src.at[part_of(other)],
            dst_ref=disc_a.at[c],
            send_sem=ds_sem.at[0],
            recv_sem=dr_sem.at[0],
            device_id=(r, other),
            device_id_type=MESH,
        )

    disc_a[c] = disc_src[part_of(c), :]
    peers(n_col, disc_1)

    for i in range(rows):
        flipped = mix[i * LANES : (i + 1) * LANES, :].T
        for k in range(4):
            at = k * (lats // 2)
            log_out[k, i : i + 1, :] = flipped[at : at + 1, :]
    outs[4].start()
    halo_take(3)

    def to_latent_grad(i, value):
        z = lat[i]
        slope = jnp.where(z > 0, 1.0, jnp.exp(jnp.minimum(z, 0.0)))
        put(4, i, (eg[i] + value) * slope)

    stencil(3, to_latent_grad)
    halo_start(4)

    drain(disc_a, n_col, ds_sem.at[0], dr_sem.at[0])
    disc_bsrc[...] = jnp.sum(disc_a[...], axis=0)

    def disc_2(k):
        other = lax.rem(r + k, n_row)
        return pltpu.make_async_remote_copy(
            src_ref=disc_bsrc,
            dst_ref=disc_b.at[r],
            send_sem=ds_sem.at[1],
            recv_sem=dr_sem.at[1],
            device_id=(other, c),
            device_id_type=MESH,
        )

    disc_b[r] = disc_bsrc[...]
    peers(n_row, disc_2)
    square = dot(lt[0:lats, :], s_low[...])
    square_high = square.astype(BF16).astype(F32)
    square2 = jnp.where(first, square_high, square - square_high).astype(BF16)
    loads[4].wait()
    loads[5].wait()
    rs1_run(
        0,
        lambda where: slope_scale
        * (dot(square2, wtwice[:, where]) - dot(lt[0:lats, :], x[:, where])),
    )

    halo_take(4)

    def to_proj_grad(i, value):
        pg_low[bins_of(i), :] = value.astype(BF16)

    stencil(4, to_proj_grad)

    def pick_back(i):
        value = dot(recv_pick_t[bins_of(i, chunk), :], pg_low[...])
        ex_src[pl.ds(i * (n_dev // CHUNKS), n_dev // CHUNKS)] = value.astype(BF16).reshape(
            n_dev // CHUNKS, portion, LANES
        )

    each(CHUNKS, pick_back)
    peers(n_dev, ex_copy)
    ex_dst[me] = ex_src[me]
    for i in range(rows):
        here = slice(i * LANES, (i + 1) * LANES)
        flipped = pg_low[here, :].astype(F32).T
        stage[:, i, :] = flipped
        own[:, here] = flipped[:lats, :].astype(BF16)
    pg_out[...] = stage[...].astype(BF16)
    outs[5].start()

    rs1_finish(0)
    rs2_start(0)
    drain(disc_b, n_row, ds_sem.at[1], dr_sem.at[1])
    disc_full[c] = jnp.sum(disc_b[...], axis=0)

    def disc_3(k):
        other = lax.rem(c + k, n_col)
        return pltpu.make_async_remote_copy(
            src_ref=disc_full.at[c],
            dst_ref=disc_full.at[c],
            send_sem=ds_sem.at[2],
            recv_sem=dr_sem.at[2],
            device_id=(r, other),
            device_id_type=MESH,
        )

    peers(n_col, disc_3)

    for turn in range(ROUNDS):
        halo_finish(turn)

    lt[0:lats, :] = own[...]
    drain(ex_dst, n_dev, as_sem.at[2], ar_sem.at[2])
    home = ex_dst[...].reshape(bins, LANES)
    flipped = jnp.concatenate(
        [home[i * LANES : (i + 1) * LANES, :].astype(F32).T[lats:, :] for i in range(rows)], axis=1
    ).astype(BF16)
    lt[lats:, :] = dot(flipped, send_pick[...]).astype(BF16)

    def encoder_part(where):
        value = dot(lt[...], x[:, where])
        return value[:lats, :] + value[lats:, :]

    rs1_run(1, encoder_part)

    drain(disc_full, n_col, ds_sem.at[2], dr_sem.at[2])
    disc_grad = disc_full[...].reshape(lats, LANES)[:, :lats]
    disc_mean = jnp.sum(disc_grad * disc_grad) / (lats * lats)
    disc_out[...] = disc_grad * lax.rsqrt(disc_mean + 1e-06)
    outs[2].start()

    dec_sum[...] = rs2_finish(0)
    rs1_finish(1)
    rs2_start(1)
    enc_sum = rs2_finish(1)

    def norm_1(k):
        other = lax.rem(r + k, n_row)
        return pltpu.make_async_remote_copy(
            src_ref=norm_src,
            dst_ref=norm_a.at[r],
            send_sem=ns_sem.at[0],
            recv_sem=nr_sem.at[0],
            device_id=(other, c),
            device_id_type=MESH,
        )

    norm_a[r] = norm_src[...]
    peers(n_row, norm_1)
    drain(norm_a, n_row, ns_sem.at[0], nr_sem.at[0])
    totals = jnp.sum(norm_a[...], axis=0)
    entries = genes * lats
    enc_out[...] = enc_sum * lax.rsqrt(totals[1, 0:1, 0:1] / entries + 1e-06)
    dec_out[...] = dec_sum[...] * lax.rsqrt(totals[0, 0:1, 0:1] / entries + 1e-06)
    outs[0].start()
    outs[1].start()
    for out in outs:
        out.wait()


def hand_on(*refs):
    count = (len(refs) - 2) // 3
    sources, targets, held = (refs[k * count : (k + 1) * count] for k in range(3))
    come, go = refs[3 * count :]
    ins = [pltpu.make_async_copy(sources[i], held[i], come.at[i]) for i in range(count)]
    outs = [pltpu.make_async_copy(held[i], targets[i], go.at[i]) for i in range(count)]
    for copy in ins:
        copy.start()
    for i in range(count):
        ins[i].wait()
        outs[i].start()
    for copy in outs:
        copy.wait()


def per_device(features, enc_weight, dec_weight, disc_weight, send_order, recv_order):
    tile_rows, tile_cols, genes = features.shape
    lats = enc_weight.shape[1]
    bins = tile_rows * tile_cols
    n_row = lax.axis_size("row")
    n_col = lax.axis_size("col")
    n_dev = n_row * n_col
    n_group = n_row // 2
    per_dev = genes // n_dev
    span = genes // n_group
    part = lats // n_col
    portion = bins // n_dev
    field = (tile_rows, LANES, LANES)
    dma = pltpu.SemaphoreType.DMA
    vmem = pltpu.VMEM
    shape = jax.ShapeDtypeStruct
    out_shape = [
        shape((per_dev, lats), F32),
        shape((per_dev, lats), F32),
        shape((lats, lats), F32),
        shape((lats, tile_rows, tile_cols), F32),
        shape((4, tile_rows, tile_cols), F32),
        shape((2 * lats, tile_rows, tile_cols), BF16),
    ]
    scratch = [
        *(vmem(one.shape, one.dtype) for one in out_shape),
        vmem((bins, genes), BF16),
        vmem((lats, lats), F32),
        vmem((2, tile_rows, LANES), jnp.int32),
        vmem((2 * lats, genes), BF16),
        vmem((2 * lats, genes), BF16),
        vmem((LANES, LANES), BF16),
        vmem((2 * LANES, 2 * LANES), BF16),
        vmem((2 * LANES, 2 * LANES), BF16),
        vmem((bins, bins), BF16),
        vmem((bins, bins), BF16),
        vmem((bins, bins), BF16),
        vmem((bins, LANES), F32),
        vmem((LANES, bins), F32),
        vmem((n_row, n_col // 2 * portion, LANES), BF16),
        vmem((n_row, n_col // 2 * portion, LANES), BF16),
        vmem((n_col, n_row // 2 * portion, LANES), BF16),
        vmem((n_col, n_row // 2 * portion, LANES), BF16),
        vmem((n_dev, portion, LANES), BF16),
        vmem((n_dev, portion, LANES), BF16),
        vmem((bins // 2, LANES), BF16),
        vmem((2, tile_rows + 2 * RADIUS, LANES + 2 * SIDE, LANES), F32),
        vmem((tile_rows, LANES + 2 * SIDE, LANES), F32),
        vmem((ROUNDS,) + field, BF16),
        vmem((ROUNDS, 2, RADIUS, LANES, LANES), BF16),
        vmem((ROUNDS, 2, tile_rows, EDGE, LANES), BF16),
        vmem((ROUNDS, 4, RADIUS, EDGE, LANES), BF16),
        vmem((len(PACKED), 2, RADIUS, LANES // 2, LANES), BF16),
        vmem((len(PACKED), 2, RADIUS, LANES // 2, LANES), BF16),
        vmem(field, F32),
        vmem(field, F32),
        vmem(field, F32),
        vmem(field, F32),
        vmem((bins, LANES), BF16),
        vmem((bins, LANES), F32),
        vmem((bins, 2 * LANES), BF16),
        vmem((bins, 2 * LANES), BF16),
        vmem((bins, LANES), F32),
        vmem(field, F32),
        vmem((bins, LANES), BF16),
        vmem((LANES, bins), BF16),
        vmem((lats, bins), BF16),
        vmem((2, n_row, lats, 2 * LANES), BF16),
        vmem((2, n_row, lats, 2 * LANES), BF16),
        vmem((2, lats, 2 * LANES), BF16),
        vmem((2, n_col, lats, 2 * LANES), BF16),
        vmem((lats, LANES), F32),
        vmem((n_col, part, LANES), F32),
        vmem((part, LANES), F32),
        vmem((n_row, part, LANES), F32),
        vmem((n_col, part, LANES), F32),
        vmem((2, 8, LANES), F32),
        vmem((n_row, 2, 8, LANES), F32),
        vmem((2 * LANES, lats), F32),
        vmem((LANES, tile_rows, LANES), F32),
        vmem((per_dev, lats), F32),
        dma((7,)),
        dma((tile_rows,)),
        dma((ROUNDS, 8)),
        dma((ROUNDS, 8)),
        dma((3,)),
        dma((3,)),
        dma((2,)),
        dma((2,)),
        dma((2,)),
        dma((2,)),
        dma((3,)),
        dma((3,)),
        dma((1,)),
        dma((1,)),
        pltpu.SemaphoreType.REGULAR,
        dma((6,)),
    ]
    anywhere = [pl.BlockSpec(memory_space=pl.ANY)] * 6
    results = pl.pallas_call(
        functools.partial(kernel, n_row, n_col),
        out_shape=out_shape,
        in_specs=anywhere,
        out_specs=anywhere,
        scratch_shapes=scratch,
        compiler_params=pltpu.CompilerParams(
            collective_id=0, has_side_effects=True, vmem_limit_bytes=56 * 1024 * 1024
        ),
    )(
        features.reshape(bins, genes),
        enc_weight.T,
        dec_weight.T,
        disc_weight,
        send_order.reshape(tile_rows, LANES),
        recv_order.reshape(tile_rows, LANES),
    )
    *others, grads = pl.pallas_call(
        hand_on,
        out_shape=out_shape,
        in_specs=anywhere,
        out_specs=anywhere,
        scratch_shapes=[*(vmem(one.shape, one.dtype) for one in out_shape), dma((6,)), dma((6,))],
    )(*results)
    return (*others, grads.reshape(2, lats, tile_rows, tile_cols))


def solution(mesh):
    in_specs = (P("row", "col", None), P(), P(), P(), P("row", "col", None), P("row", "col", None))
    out_specs = (
        P(("row", "col"), None),
        P(("row", "col"), None),
        P(),
        P(None, "row", "col"),
        P(None, "row", "col"),
        P(None, None, "row", "col"),
    )
    return jax.shard_map(
        per_device, mesh=mesh, in_specs=in_specs, out_specs=out_specs, check_vma=False
    )
```

```python
import functools
import math

import jax
import jax.numpy as jnp
from jax import lax
from jax.experimental import pallas as pl
from jax.experimental.pallas import tpu as pltpu
from jax.sharding import PartitionSpec as P

RADIUS = 3
RECON_WEIGHT = 10.0
LANES = 128
SIDE = 8
MESH = pl.DeviceIdType.MESH
F32 = jnp.float32
BF16 = jnp.bfloat16
DIRECTIONS = ((-1, 0), (1, 0), (0, -1), (0, 1), (-1, -1), (-1, 1), (1, -1), (1, 1))
OPPOSITE = (1, 0, 3, 2, 7, 6, 5, 4)
ROUNDS = 5
PACKED = {0: 0, 2: 1}
CHUNKS = 4


def stencil_taps():
    raw_taps = [math.exp(-offset * offset / 12.0) for offset in range(-RADIUS, RADIUS + 1)]
    tap_total = sum(raw_taps)
    return [raw_value / tap_total for raw_value in raw_taps]


def dot(a, b, ca=1, cb=0):
    return lax.dot_general(a, b, (((ca,), (cb,)), ((), ())), preferred_element_type=F32)


def each(count, body):
    def step(i, carry):
        body(i)
        return carry

    lax.fori_loop(0, count, step, 0)


def when(test):
    if isinstance(test, bool):
        return (lambda body: body()) if test else (lambda body: None)
    return pl.when(test)


def split_2(value):
    high = value.astype(BF16)
    low = (value - high.astype(F32)).astype(BF16)
    return jnp.concatenate([high, low], axis=1)


def kernel(
    n_row,
    n_col,
    feat_hbm,
    enc_hbm,
    dec_hbm,
    disc_hbm,
    send_hbm,
    recv_hbm,
    enc_hbm_out,
    dec_hbm_out,
    disc_hbm_out,
    emb_hbm_out,
    log_hbm_out,
    pg_hbm_out,
    enc_out,
    dec_out,
    disc_out,
    emb_out,
    log_out,
    pg_out,
    x,
    discw,
    orders,
    wcat,
    wtwice,
    gram2,
    bd_nt,
    bd_nn,
    send_pick,
    recv_pick,
    recv_pick_t,
    xp,
    xp_t,
    row_src,
    row_dst,
    col_src,
    col_dst,
    ex_src,
    ex_dst,
    low_in,
    pads,
    tmp,
    hsrc,
    h_row,
    h_col,
    h_corner,
    pack_src,
    h_pack,
    edge,
    edge_src,
    lat,
    emb,
    spread,
    summ,
    s_low,
    back,
    grads_2,
    summ_2,
    mix,
    eg,
    pg_low,
    lt,
    own,
    rs0_keep,
    rs0_src,
    rs0_dst,
    rs1_src,
    rs1_dst,
    rs2_src,
    rs2_dst,
    disc_src,
    disc_a,
    disc_bsrc,
    disc_b,
    disc_full,
    norm_src,
    norm_a,
    by_gene,
    stage,
    dec_sum,
    load_sem,
    feat_sem,
    hs_sem,
    hr_sem,
    as_sem,
    ar_sem,
    r0s_sem,
    r0r_sem,
    r1s_sem,
    r1r_sem,
    r2s_sem,
    r2r_sem,
    ds_sem,
    dr_sem,
    ns_sem,
    nr_sem,
    meet_sem,
    out_sem,
):
    n_dev = n_row * n_col
    bins, genes = x.shape
    rows = bins // LANES
    lats = discw.shape[1]
    portion = bins // n_dev
    n_group = n_row // 2
    few = min(4, n_group)
    per_dev = genes // n_dev
    span = genes // n_group
    part = lats // n_col
    slope_scale = 2.0 * RECON_WEIGHT / genes
    tap = stencil_taps()
    chunk = bins // CHUNKS

    r = lax.axis_index("row")
    c = lax.axis_index("col")
    me = r * n_col + c
    my_group = r // 2
    lane = lax.broadcasted_iota(jnp.int32, (1, LANES), 1)
    first = lane < lats

    outs = [
        pltpu.make_async_copy(a, b, out_sem.at[i])
        for i, (a, b) in enumerate(
            [
                (enc_out, enc_hbm_out),
                (dec_out, dec_hbm_out),
                (disc_out, disc_hbm_out),
                (emb_out, emb_hbm_out),
                (log_out, log_hbm_out),
                (pg_out, pg_hbm_out),
            ]
        )
    ]

    def bins_of(i, size=LANES):
        return pl.ds(i * size if isinstance(i, int) else pl.multiple_of(i * size, size), size)

    def swap(value):
        return pltpu.roll(value, lats, value.ndim - 1)

    def halo_buffer(turn, way):
        if way < 2:
            return h_row.at[turn, way]
        if way < 4:
            return h_col.at[turn, way - 2]
        return h_corner.at[turn, way - 4]

    def halo_copy(turn, way):
        dr, dc = DIRECTIONS[way]
        if way < 2 and turn in PACKED:
            source = pack_src.at[PACKED[turn], way]
            target = h_pack.at[PACKED[turn], OPPOSITE[way]]
        elif way < 2:
            source = hsrc.at[turn, pl.ds(0 if dr < 0 else rows - RADIUS, RADIUS)]
            target = halo_buffer(turn, OPPOSITE[way])
        else:
            half = rows * SIDE // 2
            source = edge_src.at[turn, 0 if dc < 0 else 1]
            if dr:
                source = source.at[pl.ds(0 if dr < 0 else half, half)]
            target = halo_buffer(turn, OPPOSITE[way])
        return pltpu.make_async_remote_copy(
            src_ref=source,
            dst_ref=target,
            send_sem=hs_sem.at[turn, way],
            recv_sem=hr_sem.at[turn, OPPOSITE[way]],
            device_id=(r + dr, c + dc),
            device_id_type=MESH,
        )

    def present(way):
        dr, dc = DIRECTIONS[way]
        tests = []
        if dr < 0:
            tests.append(r > 0)
        if dr > 0:
            tests.append(r < n_row - 1)
        if dc < 0:
            tests.append(c > 0)
        if dc > 0:
            tests.append(c < n_col - 1)
        return functools.reduce(jnp.logical_and, tests)

    def halo_start(turn):
        edge_src[turn] = edge[...].astype(BF16)
        for way in range(8):

            @pl.when(present(way))
            def _():
                halo_copy(turn, way).start()

    def halo_take(turn):
        pad = pads.at[turn % 2]
        for way in range(8):

            @pl.when(present(way))
            def _():
                halo_copy(turn, OPPOSITE[way]).wait_recv()

        left, right = slice(0, SIDE), slice(SIDE + LANES, LANES + 2 * SIDE)
        top, bottom = slice(0, RADIUS), slice(RADIUS + rows, rows + 2 * RADIUS)
        for way, part in ((0, top), (1, bottom)):
            if turn in PACKED:
                packed = h_pack[PACKED[turn], way].astype(F32)
                halves = (packed, swap(packed)) if turn == 0 else (swap(packed), packed)
                pad[part, SIDE : SIDE + LANES // 2, :] = halves[0]
                pad[part, SIDE + LANES // 2 : SIDE + LANES, :] = halves[1]
            else:
                pad[part, SIDE : SIDE + LANES, :] = h_row[turn, way].astype(F32)
            lines = slice(rows // 2 - RADIUS, rows // 2) if way == 0 else slice(0, RADIUS)
            for k, place in ((0, left), (1, right)):
                corner = h_corner[turn, 2 * way + k].astype(F32).reshape(rows // 2, SIDE, LANES)
                pad[part, place, :] = corner[lines]
        own_rows = slice(RADIUS, RADIUS + rows)
        for k, place in ((0, left), (1, right)):
            pad[own_rows, place, :] = h_col[turn, k].astype(F32).reshape(rows, SIDE, LANES)

    def halo_finish(turn):
        for way in range(8):

            @pl.when(present(way))
            def _():
                halo_copy(turn, way).wait_send()

    def stencil(turn, then):
        pad = pads.at[turn % 2]

        def down(t):
            at = pl.ds(pl.multiple_of(t * SIDE, SIDE), SIDE)
            block = pad[:, at, :]
            across = tap[RADIUS] * block[RADIUS : RADIUS + rows]
            for k in range(1, RADIUS + 1):
                across += tap[RADIUS + k] * (
                    block[RADIUS - k : RADIUS - k + rows] + block[RADIUS + k : RADIUS + k + rows]
                )
            tmp[:, at, :] = across

        def along(i):
            total = tap[RADIUS] * tmp[i, SIDE : SIDE + LANES, :]
            for k in range(1, RADIUS + 1):
                total += tap[RADIUS + k] * (
                    tmp[i, SIDE - k : SIDE - k + LANES, :] + tmp[i, SIDE + k : SIDE + k + LANES, :]
                )
            then(i, total)

        each(LANES // SIDE + 2, down)
        each(rows, along)

    def put(turn, i, value):
        pads[turn % 2, i + RADIUS, SIDE : SIDE + LANES, :] = value
        edge[0, bins_of(i, SIDE), :] = value[0:SIDE, :]
        edge[1, bins_of(i, SIDE), :] = value[LANES - SIDE :, :]
        if turn not in PACKED:
            hsrc[turn, i] = value.astype(BF16)
            return
        front, rear = value[: LANES // 2, :], value[LANES // 2 :, :]
        if turn == 0:
            packed = jnp.where(first, front, swap(rear)).astype(BF16)
        else:
            packed = jnp.where(first, swap(front), rear).astype(BF16)

        @when(i < RADIUS)
        def _():
            pack_src[PACKED[turn], 0, i] = packed

        @when(i >= rows - RADIUS)
        def _():
            pack_src[PACKED[turn], 1, i - (rows - RADIUS)] = packed

    loads = [
        pltpu.make_async_copy(a, b, load_sem.at[i])
        for i, (a, b) in enumerate(
            [
                (send_hbm, orders.at[0]),
                (recv_hbm, orders.at[1]),
                (dec_hbm, wcat.at[pl.ds(0, lats)]),
                (enc_hbm, wcat.at[pl.ds(lats, lats)]),
                (dec_hbm, wtwice.at[pl.ds(0, lats)]),
                (dec_hbm, wtwice.at[pl.ds(lats, lats)]),
                (disc_hbm, discw),
            ]
        )
    ]
    for load in loads[:4]:
        load.start()
    for i in range(rows):
        piece = pl.ds(i * LANES, LANES)
        copy = pltpu.make_async_copy(feat_hbm.at[piece], x.at[piece], feat_sem.at[i])
        copy.start()
    for load in loads[4:]:
        load.start()

    barrier = pltpu.get_barrier_semaphore()

    def greet_row(k, carry):
        other = lax.rem(r + k, n_row)
        pl.semaphore_signal(barrier, inc=1, device_id=(other, c), device_id_type=MESH)
        return carry

    def greet_col(k, carry):
        other = lax.rem(c + k, n_col)
        pl.semaphore_signal(barrier, inc=1, device_id=(r, other), device_id_type=MESH)
        return carry

    lax.fori_loop(1, n_row, greet_row, 0)
    lax.fori_loop(1, n_col, greet_col, 0)

    def build_send():
        def body(a):
            line = orders[0, pl.ds(a, 1), :].astype(F32)
            column = jnp.broadcast_to(line, (LANES, LANES)).T
            for t in range(rows):
                index = (lane + t * LANES).astype(F32)
                send_pick[bins_of(a), t * LANES : (t + 1) * LANES] = jnp.where(
                    column == index, 1.0, 0.0
                ).astype(BF16)

        each(rows, body)

    def build_recv():
        def body(a, carry):
            line = orders[1, pl.ds(a, 1), :].astype(F32)
            column = jnp.broadcast_to(line, (LANES, LANES)).T
            for t in range(rows):
                index = recv_index(lane + t * LANES)
                recv_pick[
                    pl.ds(pl.multiple_of(a * LANES, LANES), LANES), t * LANES : (t + 1) * LANES
                ] = jnp.where(column == index, 1.0, 0.0).astype(BF16)
            return carry

        lax.fori_loop(0, rows, body, 0)

    def build_recv_t():
        def body(t, carry):
            index = (lax.broadcasted_iota(jnp.int32, (LANES, 1), 0) + t * LANES).astype(F32)
            for a in range(rows):
                line = orders[1, a : a + 1, :].astype(F32)
                recv_pick_t[
                    pl.ds(pl.multiple_of(t * LANES, LANES), LANES), a * LANES : (a + 1) * LANES
                ] = jnp.where(line == index, 1.0, 0.0).astype(BF16)
            return carry

        lax.fori_loop(0, rows, body, 0)

    def regroup(values):
        m = values.shape[0] // 2
        n = values.shape[1] // portion
        low, high = values[:m], values[m:]
        parts = []
        for value in (jnp.where(first, low, swap(high)), jnp.where(first, swap(low), high)):
            for k in range(n):
                block = value[:, k * portion : (k + 1) * portion, :]
                parts.append(block.reshape(m * portion, LANES))
        return parts

    def row_copy(k):
        other = lax.rem(r + k, n_row)
        return pltpu.make_async_remote_copy(
            src_ref=row_src.at[other],
            dst_ref=row_dst.at[r],
            send_sem=as_sem.at[0],
            recv_sem=ar_sem.at[0],
            device_id=(other, c),
            device_id_type=MESH,
        )

    def col_copy(k):
        other = lax.rem(c + k, n_col)
        return pltpu.make_async_remote_copy(
            src_ref=col_src.at[other],
            dst_ref=col_dst.at[c],
            send_sem=as_sem.at[1],
            recv_sem=ar_sem.at[1],
            device_id=(r, other),
            device_id_type=MESH,
        )

    def ex_copy(k):
        other = lax.rem(me + k, n_dev)
        return pltpu.make_async_remote_copy(
            src_ref=ex_src.at[other],
            dst_ref=ex_dst.at[me],
            send_sem=as_sem.at[2],
            recv_sem=ar_sem.at[2],
            device_id=(other // n_col, lax.rem(other, n_col)),
            device_id_type=MESH,
        )

    def peers(count, make):
        def body(k, carry):
            make(k).start()
            return carry

        lax.fori_loop(1, count, body, 0)

    def drain(ref, count, send_sem, recv_sem):
        most = ref.at[pl.ds(0, count - 1)]
        pltpu.make_async_copy(most, most, recv_sem).wait()
        pltpu.make_async_copy(most, most, send_sem).wait()

    def recv_index(position):
        slot = lax.rem(position, portion)
        rest = position // portion
        low_row = lax.rem(rest, n_row // 2)
        rest = rest // (n_row // 2)
        col = lax.rem(rest, n_col)
        row = (rest // n_col) * (n_row // 2) + low_row
        return (((row * n_col) + col) * portion + slot).astype(F32)

    loads[0].wait()
    loads[1].wait()
    build_send()
    for way in range(8):

        @pl.when(jnp.logical_not(present(way)))
        def _():
            for turn in range(ROUNDS):
                if way < 2 and turn in PACKED:
                    empty = h_pack.at[PACKED[turn], way]
                else:
                    empty = halo_buffer(turn, way)
                empty[...] = jnp.zeros_like(empty)

    loads[2].wait()
    loads[3].wait()

    pl.semaphore_wait(barrier, n_row + n_col - 2)

    def greet_meet(k, carry):
        other = lax.rem(c + k, n_col)
        pl.semaphore_signal(meet_sem, inc=1, device_id=(r, other), device_id_type=MESH)
        return carry

    lax.fori_loop(1, n_col, greet_meet, 0)
    for k in range(rows):
        pltpu.make_async_copy(feat_hbm.at[bins_of(k)], x.at[bins_of(k)], feat_sem.at[k]).wait()
    flat = dot(wcat[...], x[...], 1, 1)
    xp_t[...] = flat
    picked = dot(flat.astype(BF16), send_pick[...], 1, 1)
    turned = jnp.concatenate(
        [picked[:, i * LANES : (i + 1) * LANES].T for i in range(rows)], axis=0
    ).reshape(n_row, 2, n_col // 2 * portion, LANES)
    row_src[...] = jnp.where(first, swap(turned[:, 0]), turned[:, 1]).astype(BF16)

    pl.semaphore_wait(meet_sem, n_col - 1)

    peers(n_row, row_copy)
    row_dst[r] = row_src[r]

    for i in range(rows):
        block = xp_t[:, i * LANES : (i + 1) * LANES].T
        xp[bins_of(i), :] = block
        put(0, i, swap(block.astype(BF16).astype(F32)))
    halo_start(0)
    build_recv()
    drain(row_dst, n_row, as_sem.at[0], ar_sem.at[0])
    for k, value in enumerate(regroup(row_dst[...].astype(F32))):
        col_src[k] = value.astype(BF16)
    peers(n_col, col_copy)
    col_dst[c] = col_src[c]

    def elu(value):
        return jnp.where(value > 0, value, jnp.exp(jnp.minimum(value, 0.0)) - 1.0)

    def first_latent(i, value):
        lat[i] = value
        emb[i] = elu(value)

    halo_take(0)
    stencil(0, first_latent)

    drain(col_dst, n_col, as_sem.at[1], ar_sem.at[1])
    low_in[...] = col_dst[...].reshape(bins // 2, LANES)

    def pick_in(i):
        here = bins_of(i, chunk)
        value = swap(dot(recv_pick[here, : bins // 2], low_in[...])) + dot(
            recv_pick[here, bins // 2 :], low_in[...]
        )
        for k in range(rows // CHUNKS):
            at = i * (rows // CHUNKS) + k
            put(1, at, jnp.where(first, emb[at], value[k * LANES : (k + 1) * LANES, :]))

    each(CHUNKS, pick_in)
    halo_start(1)
    build_recv_t()
    gram = dot(wcat[0:lats, :], wcat[0:lats, :], 1, 1)
    gram_high = gram.astype(BF16)
    gram_low = (gram - gram_high.astype(F32)).astype(BF16)
    gram2[...] = jnp.zeros_like(gram2)
    gram2[0:lats, 0:lats] = gram_high
    gram2[lats:, 0:lats] = gram_low

    def first_spread(i, value):
        out = elu(value)
        lat[i] = jnp.where(first, lat[i], value)
        emb[i] = jnp.where(first, emb[i], out)
        put(2, i, out)
        spread[i] = value

    halo_take(1)
    stencil(1, first_spread)
    halo_start(2)

    def after_spread(i):
        value = spread[i]
        here = bins_of(i)
        low = value.astype(BF16).astype(F32)
        summ[i] = jax.nn.sigmoid(value)
        s_low[here, :] = jnp.where(first, low, swap(low)).astype(BF16)
        lt[0:lats, here] = low.T[0:lats, :].astype(BF16)

    each(rows, after_spread)

    back[...] = slope_scale * (
        dot(s_low[...], gram2[...]) - jnp.where(first, xp[...], 0.0)
    )

    core = lax.rem(r, 2)
    n_part = n_group // few

    def part_at(k):
        return lax.rem(my_group // few + 1 + k, n_part)

    def rs0_copy(which, k):
        here = pl.ds(part_at(k) * few, few)
        return pltpu.make_async_remote_copy(
            src_ref=rs0_src.at[which, here],
            dst_ref=rs0_dst.at[which, here],
            send_sem=r0s_sem.at[which, k],
            recv_sem=r0r_sem.at[which, k],
            device_id=(r + 1 - 2 * core, c),
            device_id_type=MESH,
        )

    def rs0_run(which, product):
        def body(k):
            part = part_at(k)
            value = product(bins_of(part, few * span))
            for j in range(few):
                at = j * span
                middle = value[:, at + LANES : at + 2 * LANES]
                top, bottom = middle[: lats // 2, :], middle[lats // 2 :, :]
                lower = jnp.concatenate(
                    [value[:, at : at + LANES], jnp.where(first, top, swap(bottom))], axis=0
                )
                upper = jnp.concatenate(
                    [value[:, at + 2 * LANES : at + span], jnp.where(first, swap(top), bottom)],
                    axis=0,
                )
                rs0_keep[which, part * few + j] = jnp.where(core == 0, lower, upper)
                rs0_src[which, part * few + j] = jnp.where(core == 0, upper, lower).astype(BF16)
            rs0_copy(which, k).start()

        each(n_part, body)

    def rs1_start(which):
        def body(k):
            rs0_copy(which, k).wait()
            for j in range(few):
                group = part_at(k) * few + j
                total = rs0_keep[which, group] + rs0_dst[which, group].astype(F32)
                rs1_src[which, group] = total.astype(BF16)

                @pl.when(group != my_group)
                def _():
                    pltpu.make_async_remote_copy(
                        src_ref=rs1_src.at[which, group],
                        dst_ref=rs1_dst.at[which, my_group],
                        send_sem=r1s_sem.at[which],
                        recv_sem=r1r_sem.at[which],
                        device_id=(2 * group + core, c),
                        device_id_type=MESH,
                    ).start()

        each(n_part, body)

    def rs1_finish(which):
        drain(rs1_dst.at[which], n_group, r1s_sem.at[which], r1r_sem.at[which])
        rs1_dst[which, my_group] = rs1_src[which, my_group]
        total = rs1_dst[which, 0].astype(F32)
        for k in range(1, n_group):
            total += rs1_dst[which, k].astype(F32)
        rs2_src[which] = total.astype(BF16)

    def rs2_copy(which, k):
        other = lax.rem(c + k, n_col)
        return pltpu.make_async_remote_copy(
            src_ref=rs2_src.at[which],
            dst_ref=rs2_dst.at[which, c],
            send_sem=r2s_sem.at[which],
            recv_sem=r2r_sem.at[which],
            device_id=(r, other),
            device_id_type=MESH,
        )

    def rs2_start(which):
        peers(n_col, functools.partial(rs2_copy, which))
        rs2_dst[which, c] = rs2_src[which]

    def rs2_finish(which):
        drain(rs2_dst.at[which], n_col, r2s_sem.at[which], r2r_sem.at[which])
        total = rs2_dst[which, 0].astype(F32)
        for k in range(1, n_col):
            total += rs2_dst[which, k].astype(F32)
        norm_src[which] = jnp.broadcast_to(jnp.sum(total * total), (8, LANES))
        pairs = total[lats:, :]
        pairs = jnp.concatenate([pairs, swap(pairs)], axis=0).T
        by_gene[pl.ds(pl.multiple_of(core * lats, lats), LANES), :] = total[:lats, :].T
        by_gene[pl.ds(pl.multiple_of((1 - core) * LANES, LANES), lats), :] = pairs[:lats, :]
        return by_gene[pl.ds(pl.multiple_of(c * per_dev, 8), per_dev), :]

    loads[6].wait()
    wide = jnp.concatenate([discw[...], jnp.zeros_like(discw)], axis=1)
    block = jnp.concatenate([wide, pltpu.roll(wide, lats, 1)], axis=0)
    block_high = block.astype(BF16)
    block_low = (block - block_high.astype(F32)).astype(BF16)
    for u in range(2):
        one = slice(u * LANES, (u + 1) * LANES)
        bd_nt[0:LANES, one] = block_high
        bd_nt[LANES:, one] = block_low
        bd_nn[one, 0:LANES] = block_high
        bd_nn[one, LANES:] = block_low
    for i in range(rows):
        stage[:, i, :] = emb[i].T
    emb_out[...] = stage[0:lats]
    outs[3].start()
    halo_take(2)

    def to_summary(i, value):
        summ[i] = jnp.where(first, summ[i], jax.nn.sigmoid(value))

    stencil(2, to_summary)

    half_sum = jnp.where(
        (lax.broadcasted_iota(jnp.int32, (LANES, LANES), 0) < lats)
        == (lax.broadcasted_iota(jnp.int32, (LANES, LANES), 1) < lats),
        1.0,
        0.0,
    ).astype(BF16)
    half_sum2 = jnp.concatenate([half_sum, half_sum], axis=0)

    step = rows // CHUNKS

    def contrast(i):
        piece = pl.ds(i * step, step)
        here = bins_of(i, chunk)
        summary = summ[piece].reshape(chunk, LANES)
        embedded = emb[piece].reshape(chunk, LANES)
        swapped = swap(embedded)
        summary_2 = split_2(summary)
        wide_q = dot(summary_2, bd_nt[...], 1, 1)
        queries = wide_q[:, :LANES] + wide_q[:, LANES:]
        logit_same = dot(split_2(embedded * queries), half_sum2)
        logit_other = dot(split_2(swapped * queries), half_sum2)
        grad_same = -jax.nn.sigmoid(-logit_same)
        grad_other = jax.nn.sigmoid(logit_other)
        embed_grad = grad_same * queries + swap(grad_other * queries)
        query_grad = grad_same * embedded + grad_other * swapped
        query_grad_2 = split_2(query_grad)
        grads_2[here, :] = query_grad_2
        summ_2[here, :] = summary_2
        wide_s = dot(query_grad_2, bd_nn[...])
        summary_grad = wide_s[:, :LANES] + wide_s[:, LANES:]
        spread_grad = summary_grad * summary * (1.0 - summary)
        spread_grad += back[here, :]
        eg[piece] = embed_grad.reshape(step, LANES, LANES)
        mix[here, :] = jnp.where(lax.rem(lane, lats) < lats // 2, logit_same, logit_other)
        for j in range(step):
            put(3, i * step + j, spread_grad[j * LANES : (j + 1) * LANES, :])

    for i in range(CHUNKS):
        contrast(i)
    halo_start(3)

    def disc_step(i, total):
        here = bins_of(i, chunk)
        return total + dot(grads_2[here, :], summ_2[here, :], 0, 0)

    disc_total = lax.fori_loop(
        0, CHUNKS, disc_step, jnp.zeros((2 * LANES, 2 * LANES), F32)
    )
    quarter = (disc_total[:LANES, :LANES] + disc_total[LANES:, :LANES]) + (
        disc_total[:LANES, LANES:] + disc_total[LANES:, LANES:]
    )
    disc_src[...] = quarter[:lats, :] + swap(quarter[lats:, :])

    def part_of(index):
        return pl.ds(pl.multiple_of(index * part, 8), part)

    def disc_1(k):
        other = lax.rem(c + k, n_col)
        return pltpu.make_async_remote_copy(
            src_ref=disc_src.at[part_of(other)],
            dst_ref=disc_a.at[c],
            send_sem=ds_sem.at[0],
            recv_sem=dr_sem.at[0],
            device_id=(r, other),
            device_id_type=MESH,
        )

    disc_a[c] = disc_src[part_of(c), :]
    peers(n_col, disc_1)

    for i in range(rows):
        flipped = mix[i * LANES : (i + 1) * LANES, :].T
        for k in range(4):
            at = k * (lats // 2)
            log_out[k, i : i + 1, :] = flipped[at : at + 1, :]
    outs[4].start()
    square = dot(lt[0:lats, :], s_low[...])
    square_high = square.astype(BF16).astype(F32)
    square2 = jnp.where(first, square_high, square - square_high).astype(BF16)
    loads[4].wait()
    loads[5].wait()
    rs0_run(
        0,
        lambda where: slope_scale
        * (dot(square2, wtwice[:, where]) - dot(lt[0:lats, :], x[:, where])),
    )

    halo_take(3)

    def to_latent_grad(i, value):
        z = lat[i]
        slope = jnp.where(z > 0, 1.0, jnp.exp(jnp.minimum(z, 0.0)))
        put(4, i, (eg[i] + value) * slope)

    stencil(3, to_latent_grad)
    halo_start(4)

    drain(disc_a, n_col, ds_sem.at[0], dr_sem.at[0])
    disc_bsrc[...] = jnp.sum(disc_a[...], axis=0)

    def disc_2(k):
        other = lax.rem(r + k, n_row)
        return pltpu.make_async_remote_copy(
            src_ref=disc_bsrc,
            dst_ref=disc_b.at[r],
            send_sem=ds_sem.at[1],
            recv_sem=dr_sem.at[1],
            device_id=(other, c),
            device_id_type=MESH,
        )

    disc_b[r] = disc_bsrc[...]
    peers(n_row, disc_2)
    rs1_start(0)
    halo_take(4)

    def to_proj_grad(i, value):
        pg_low[bins_of(i), :] = value.astype(BF16)

    stencil(4, to_proj_grad)

    def pick_back(i):
        value = dot(recv_pick_t[bins_of(i, chunk), :], pg_low[...])
        ex_src[pl.ds(i * (n_dev // CHUNKS), n_dev // CHUNKS)] = value.astype(BF16).reshape(
            n_dev // CHUNKS, portion, LANES
        )

    each(CHUNKS, pick_back)
    peers(n_dev, ex_copy)
    ex_dst[me] = ex_src[me]
    for i in range(rows):
        here = slice(i * LANES, (i + 1) * LANES)
        flipped = pg_low[here, :].astype(F32).T
        stage[:, i, :] = flipped
        own[:, here] = flipped[:lats, :].astype(BF16)
    pg_out[...] = stage[...].astype(BF16)
    outs[5].start()

    rs1_finish(0)
    drain(disc_b, n_row, ds_sem.at[1], dr_sem.at[1])
    disc_full[c] = jnp.sum(disc_b[...], axis=0)

    def disc_3(k):
        other = lax.rem(c + k, n_col)
        return pltpu.make_async_remote_copy(
            src_ref=disc_full.at[c],
            dst_ref=disc_full.at[c],
            send_sem=ds_sem.at[2],
            recv_sem=dr_sem.at[2],
            device_id=(r, other),
            device_id_type=MESH,
        )

    peers(n_col, disc_3)

    for turn in range(ROUNDS):
        halo_finish(turn)

    lt[0:lats, :] = own[...]
    drain(ex_dst, n_dev, as_sem.at[2], ar_sem.at[2])
    rs2_start(0)
    home = ex_dst[...].reshape(bins, LANES)
    flipped = jnp.concatenate(
        [home[i * LANES : (i + 1) * LANES, :].astype(F32).T[lats:, :] for i in range(rows)], axis=1
    ).astype(BF16)
    lt[lats:, :] = dot(flipped, send_pick[...]).astype(BF16)

    def encoder_part(where):
        value = dot(lt[...], x[:, where])
        return value[:lats, :] + value[lats:, :]

    rs0_run(1, encoder_part)
    rs1_start(1)

    drain(disc_full, n_col, ds_sem.at[2], dr_sem.at[2])
    disc_grad = disc_full[...].reshape(lats, LANES)[:, :lats]
    disc_mean = jnp.sum(disc_grad * disc_grad) / (lats * lats)
    disc_out[...] = disc_grad * lax.rsqrt(disc_mean + 1e-06)
    outs[2].start()

    dec_sum[...] = rs2_finish(0)
    rs1_finish(1)
    rs2_start(1)
    enc_sum = rs2_finish(1)

    def norm_1(k):
        other = lax.rem(r + k, n_row)
        return pltpu.make_async_remote_copy(
            src_ref=norm_src,
            dst_ref=norm_a.at[r],
            send_sem=ns_sem.at[0],
            recv_sem=nr_sem.at[0],
            device_id=(other, c),
            device_id_type=MESH,
        )

    norm_a[r] = norm_src[...]
    peers(n_row, norm_1)
    drain(norm_a, n_row, ns_sem.at[0], nr_sem.at[0])
    totals = jnp.sum(norm_a[...], axis=0)
    entries = genes * lats
    enc_out[...] = enc_sum * lax.rsqrt(totals[1, 0:1, 0:1] / entries + 1e-06)
    dec_out[...] = dec_sum[...] * lax.rsqrt(totals[0, 0:1, 0:1] / entries + 1e-06)
    outs[0].start()
    outs[1].start()
    for out in outs:
        out.wait()


def hand_on(*refs):
    count = (len(refs) - 2) // 3
    sources, targets, held = (refs[k * count : (k + 1) * count] for k in range(3))
    come, go = refs[3 * count :]
    ins = [pltpu.make_async_copy(sources[i], held[i], come.at[i]) for i in range(count)]
    outs = [pltpu.make_async_copy(held[i], targets[i], go.at[i]) for i in range(count)]
    for copy in ins:
        copy.start()
    for i in range(count):
        ins[i].wait()
        outs[i].start()
    for copy in outs:
        copy.wait()


def per_device(features, enc_weight, dec_weight, disc_weight, send_order, recv_order):
    tile_rows, tile_cols, genes = features.shape
    lats = enc_weight.shape[1]
    bins = tile_rows * tile_cols
    n_row = lax.axis_size("row")
    n_col = lax.axis_size("col")
    n_dev = n_row * n_col
    n_group = n_row // 2
    per_dev = genes // n_dev
    span = genes // n_group
    part = lats // n_col
    packed = lats + lats // 2
    portion = bins // n_dev
    field = (tile_rows, LANES, LANES)
    dma = pltpu.SemaphoreType.DMA
    vmem = pltpu.VMEM
    shape = jax.ShapeDtypeStruct
    out_shape = [
        shape((per_dev, lats), F32),
        shape((per_dev, lats), F32),
        shape((lats, lats), F32),
        shape((lats, tile_rows, tile_cols), F32),
        shape((4, tile_rows, tile_cols), F32),
        shape((2 * lats, tile_rows, tile_cols), BF16),
    ]
    scratch = [
        *(vmem(one.shape, one.dtype) for one in out_shape),
        vmem((bins, genes), BF16),
        vmem((lats, lats), F32),
        vmem((2, tile_rows, LANES), jnp.int32),
        vmem((2 * lats, genes), BF16),
        vmem((2 * lats, genes), BF16),
        vmem((LANES, LANES), BF16),
        vmem((2 * LANES, 2 * LANES), BF16),
        vmem((2 * LANES, 2 * LANES), BF16),
        vmem((bins, bins), BF16),
        vmem((bins, bins), BF16),
        vmem((bins, bins), BF16),
        vmem((bins, LANES), F32),
        vmem((LANES, bins), F32),
        vmem((n_row, n_col // 2 * portion, LANES), BF16),
        vmem((n_row, n_col // 2 * portion, LANES), BF16),
        vmem((n_col, n_row // 2 * portion, LANES), BF16),
        vmem((n_col, n_row // 2 * portion, LANES), BF16),
        vmem((n_dev, portion, LANES), BF16),
        vmem((n_dev, portion, LANES), BF16),
        vmem((bins // 2, LANES), BF16),
        vmem((2, tile_rows + 2 * RADIUS, LANES + 2 * SIDE, LANES), F32),
        vmem((tile_rows, LANES + 2 * SIDE, LANES), F32),
        vmem((ROUNDS,) + field, BF16),
        vmem((ROUNDS, 2, RADIUS, LANES, LANES), BF16),
        vmem((ROUNDS, 2, tile_rows * SIDE, LANES), BF16),
        vmem((ROUNDS, 4, tile_rows * SIDE // 2, LANES), BF16),
        vmem((len(PACKED), 2, RADIUS, LANES // 2, LANES), BF16),
        vmem((len(PACKED), 2, RADIUS, LANES // 2, LANES), BF16),
        vmem((2, tile_rows * SIDE, LANES), F32),
        vmem((ROUNDS, 2, tile_rows * SIDE, LANES), BF16),
        vmem(field, F32),
        vmem(field, F32),
        vmem(field, F32),
        vmem(field, F32),
        vmem((bins, LANES), BF16),
        vmem((bins, LANES), F32),
        vmem((bins, 2 * LANES), BF16),
        vmem((bins, 2 * LANES), BF16),
        vmem((bins, LANES), F32),
        vmem(field, F32),
        vmem((bins, LANES), BF16),
        vmem((LANES, bins), BF16),
        vmem((lats, bins), BF16),
        vmem((2, n_group, packed, LANES), F32),
        vmem((2, n_group, packed, LANES), BF16),
        vmem((2, n_group, packed, LANES), BF16),
        vmem((2, n_group, packed, LANES), BF16),
        vmem((2, n_group, packed, LANES), BF16),
        vmem((2, packed, LANES), BF16),
        vmem((2, n_col, packed, LANES), BF16),
        vmem((lats, LANES), F32),
        vmem((n_col, part, LANES), F32),
        vmem((part, LANES), F32),
        vmem((n_row, part, LANES), F32),
        vmem((n_col, part, LANES), F32),
        vmem((2, 8, LANES), F32),
        vmem((n_row, 2, 8, LANES), F32),
        vmem((span // 2, lats), F32),
        vmem((LANES, tile_rows, LANES), F32),
        vmem((per_dev, lats), F32),
        dma((7,)),
        dma((tile_rows,)),
        dma((ROUNDS, 8)),
        dma((ROUNDS, 8)),
        dma((3,)),
        dma((3,)),
        dma((2, 2)),
        dma((2, 2)),
        dma((2,)),
        dma((2,)),
        dma((2,)),
        dma((2,)),
        dma((3,)),
        dma((3,)),
        dma((1,)),
        dma((1,)),
        pltpu.SemaphoreType.REGULAR,
        dma((6,)),
    ]
    anywhere = [pl.BlockSpec(memory_space=pl.ANY)] * 6
    results = pl.pallas_call(
        functools.partial(kernel, n_row, n_col),
        out_shape=out_shape,
        in_specs=anywhere,
        out_specs=anywhere,
        scratch_shapes=scratch,
        compiler_params=pltpu.CompilerParams(
            collective_id=0, has_side_effects=True, vmem_limit_bytes=56 * 1024 * 1024
        ),
    )(
        features.reshape(bins, genes),
        enc_weight.T,
        dec_weight.T,
        disc_weight,
        send_order.reshape(tile_rows, LANES),
        recv_order.reshape(tile_rows, LANES),
    )
    *others, grads = pl.pallas_call(
        hand_on,
        out_shape=out_shape,
        in_specs=anywhere,
        out_specs=anywhere,
        scratch_shapes=[*(vmem(one.shape, one.dtype) for one in out_shape), dma((6,)), dma((6,))],
    )(*results)
    return (*others, grads.reshape(2, lats, tile_rows, tile_cols))


def solution(mesh):
    in_specs = (P("row", "col", None), P(), P(), P(), P("row", "col", None), P("row", "col", None))
    out_specs = (
        P(("row", "col"), None),
        P(("row", "col"), None),
        P(),
        P(None, "row", "col"),
        P(None, "row", "col"),
        P(None, None, "row", "col"),
    )
    return jax.shard_map(
        per_device, mesh=mesh, in_specs=in_specs, out_specs=out_specs, check_vma=False
    )
```

```python
import functools
import math

import jax
import jax.numpy as jnp
from jax import lax
from jax.experimental import pallas as pl
from jax.experimental.pallas import tpu as pltpu
from jax.sharding import PartitionSpec as P

RADIUS = 3
RECON_WEIGHT = 10.0
LANES = 128
SIDE = 8
MESH = pl.DeviceIdType.MESH
F32 = jnp.float32
BF16 = jnp.bfloat16
DIRECTIONS = ((-1, 0), (1, 0), (0, -1), (0, 1), (-1, -1), (-1, 1), (1, -1), (1, 1))
OPPOSITE = (1, 0, 3, 2, 7, 6, 5, 4)
ROUNDS = 5
PACKED = {0: 0, 2: 1}
CHUNKS = 4


def stencil_taps():
    raw_taps = [math.exp(-offset * offset / 12.0) for offset in range(-RADIUS, RADIUS + 1)]
    tap_total = sum(raw_taps)
    return [raw_value / tap_total for raw_value in raw_taps]


def dot(a, b, ca=1, cb=0):
    return lax.dot_general(a, b, (((ca,), (cb,)), ((), ())), preferred_element_type=F32)


def each(count, body):
    def step(i, carry):
        body(i)
        return carry

    lax.fori_loop(0, count, step, 0)


def when(test):
    if isinstance(test, bool):
        return (lambda body: body()) if test else (lambda body: None)
    return pl.when(test)


def split_2(value):
    high = value.astype(BF16)
    low = (value - high.astype(F32)).astype(BF16)
    return jnp.concatenate([high, low], axis=1)


def kernel(
    n_row,
    n_col,
    feat_hbm,
    enc_hbm,
    dec_hbm,
    disc_hbm,
    send_hbm,
    recv_hbm,
    enc_hbm_out,
    dec_hbm_out,
    disc_hbm_out,
    emb_hbm_out,
    log_hbm_out,
    pg_hbm_out,
    enc_out,
    dec_out,
    disc_out,
    emb_out,
    log_out,
    pg_out,
    x,
    discw,
    orders,
    wcat,
    wtwice,
    gram2,
    bd_nt,
    bd_nn,
    send_pick,
    recv_pick,
    recv_pick_t,
    xp,
    xp_t,
    ex_src,
    ex_dst,
    low_in,
    pads,
    tmp,
    hsrc,
    h_row,
    h_col,
    h_corner,
    pack_src,
    h_pack,
    edge,
    edge_src,
    lat,
    emb,
    spread,
    summ,
    s_low,
    back,
    grads_2,
    summ_2,
    mix,
    eg,
    pg_low,
    lt,
    own,
    rs0_keep,
    rs0_src,
    rs0_dst,
    rs1_src,
    rs1_dst,
    rs2_src,
    rs2_dst,
    disc_src,
    disc_a,
    disc_bsrc,
    disc_b,
    disc_full,
    norm_src,
    norm_a,
    by_gene,
    stage,
    dec_sum,
    load_sem,
    feat_sem,
    hs_sem,
    hr_sem,
    as_sem,
    ar_sem,
    r0s_sem,
    r0r_sem,
    r1s_sem,
    r1r_sem,
    r2s_sem,
    r2r_sem,
    ds_sem,
    dr_sem,
    ns_sem,
    nr_sem,
    meet_sem,
    out_sem,
):
    n_dev = n_row * n_col
    bins, genes = x.shape
    rows = bins // LANES
    lats = discw.shape[1]
    portion = bins // n_dev
    n_group = n_row // 2
    few = min(4, n_group)
    per_dev = genes // n_dev
    span = genes // n_group
    part = lats // n_col
    slope_scale = 2.0 * RECON_WEIGHT / genes
    tap = stencil_taps()
    chunk = bins // CHUNKS

    r = lax.axis_index("row")
    c = lax.axis_index("col")
    me = r * n_col + c
    my_group = r // 2
    lane = lax.broadcasted_iota(jnp.int32, (1, LANES), 1)
    first = lane < lats

    outs = [
        pltpu.make_async_copy(a, b, out_sem.at[i])
        for i, (a, b) in enumerate(
            [
                (enc_out, enc_hbm_out),
                (dec_out, dec_hbm_out),
                (disc_out, disc_hbm_out),
                (emb_out, emb_hbm_out),
                (log_out, log_hbm_out),
                (pg_out, pg_hbm_out),
            ]
        )
    ]

    def bins_of(i, size=LANES):
        return pl.ds(i * size if isinstance(i, int) else pl.multiple_of(i * size, size), size)

    def swap(value):
        return pltpu.roll(value, lats, value.ndim - 1)

    def halo_buffer(turn, way):
        if way < 2:
            return h_row.at[turn, way]
        if way < 4:
            return h_col.at[turn, way - 2]
        return h_corner.at[turn, way - 4]

    def halo_copy(turn, way):
        dr, dc = DIRECTIONS[way]
        if way < 2 and turn in PACKED:
            source = pack_src.at[PACKED[turn], way]
            target = h_pack.at[PACKED[turn], OPPOSITE[way]]
        elif way < 2:
            source = hsrc.at[turn, pl.ds(0 if dr < 0 else rows - RADIUS, RADIUS)]
            target = halo_buffer(turn, OPPOSITE[way])
        else:
            half = rows * SIDE // 2
            source = edge_src.at[turn, 0 if dc < 0 else 1]
            if dr:
                source = source.at[pl.ds(0 if dr < 0 else half, half)]
            target = halo_buffer(turn, OPPOSITE[way])
        return pltpu.make_async_remote_copy(
            src_ref=source,
            dst_ref=target,
            send_sem=hs_sem.at[turn, way],
            recv_sem=hr_sem.at[turn, OPPOSITE[way]],
            device_id=(r + dr, c + dc),
            device_id_type=MESH,
        )

    def present(way):
        dr, dc = DIRECTIONS[way]
        tests = []
        if dr < 0:
            tests.append(r > 0)
        if dr > 0:
            tests.append(r < n_row - 1)
        if dc < 0:
            tests.append(c > 0)
        if dc > 0:
            tests.append(c < n_col - 1)
        return functools.reduce(jnp.logical_and, tests)

    def halo_start(turn):
        edge_src[turn] = edge[...].astype(BF16)
        for way in range(8):

            @pl.when(present(way))
            def _():
                halo_copy(turn, way).start()

    def halo_take(turn):
        pad = pads.at[turn % 2]
        for way in range(8):

            @pl.when(present(way))
            def _():
                halo_copy(turn, OPPOSITE[way]).wait_recv()

        left, right = slice(0, SIDE), slice(SIDE + LANES, LANES + 2 * SIDE)
        top, bottom = slice(0, RADIUS), slice(RADIUS + rows, rows + 2 * RADIUS)
        for way, part in ((0, top), (1, bottom)):
            if turn in PACKED:
                packed = h_pack[PACKED[turn], way].astype(F32)
                halves = (packed, swap(packed)) if turn == 0 else (swap(packed), packed)
                pad[part, SIDE : SIDE + LANES // 2, :] = halves[0]
                pad[part, SIDE + LANES // 2 : SIDE + LANES, :] = halves[1]
            else:
                pad[part, SIDE : SIDE + LANES, :] = h_row[turn, way].astype(F32)
            lines = slice(rows // 2 - RADIUS, rows // 2) if way == 0 else slice(0, RADIUS)
            for k, place in ((0, left), (1, right)):
                corner = h_corner[turn, 2 * way + k].astype(F32).reshape(rows // 2, SIDE, LANES)
                pad[part, place, :] = corner[lines]
        own_rows = slice(RADIUS, RADIUS + rows)
        for k, place in ((0, left), (1, right)):
            pad[own_rows, place, :] = h_col[turn, k].astype(F32).reshape(rows, SIDE, LANES)

    def halo_finish(turn):
        for way in range(8):

            @pl.when(present(way))
            def _():
                halo_copy(turn, way).wait_send()

    def stencil(turn, then):
        pad = pads.at[turn % 2]

        def down(t):
            at = pl.ds(pl.multiple_of(t * SIDE, SIDE), SIDE)
            block = pad[:, at, :]
            across = tap[RADIUS] * block[RADIUS : RADIUS + rows]
            for k in range(1, RADIUS + 1):
                across += tap[RADIUS + k] * (
                    block[RADIUS - k : RADIUS - k + rows] + block[RADIUS + k : RADIUS + k + rows]
                )
            tmp[:, at, :] = across

        def along(i):
            total = tap[RADIUS] * tmp[i, SIDE : SIDE + LANES, :]
            for k in range(1, RADIUS + 1):
                total += tap[RADIUS + k] * (
                    tmp[i, SIDE - k : SIDE - k + LANES, :] + tmp[i, SIDE + k : SIDE + k + LANES, :]
                )
            then(i, total)

        each(LANES // SIDE + 2, down)
        each(rows, along)

    def put(turn, i, value):
        pads[turn % 2, i + RADIUS, SIDE : SIDE + LANES, :] = value
        edge[0, bins_of(i, SIDE), :] = value[0:SIDE, :]
        edge[1, bins_of(i, SIDE), :] = value[LANES - SIDE :, :]
        if turn not in PACKED:
            hsrc[turn, i] = value.astype(BF16)
            return
        front, rear = value[: LANES // 2, :], value[LANES // 2 :, :]
        if turn == 0:
            packed = jnp.where(first, front, swap(rear)).astype(BF16)
        else:
            packed = jnp.where(first, swap(front), rear).astype(BF16)

        @when(i < RADIUS)
        def _():
            pack_src[PACKED[turn], 0, i] = packed

        @when(i >= rows - RADIUS)
        def _():
            pack_src[PACKED[turn], 1, i - (rows - RADIUS)] = packed

    loads = [
        pltpu.make_async_copy(a, b, load_sem.at[i])
        for i, (a, b) in enumerate(
            [
                (send_hbm, orders.at[0]),
                (recv_hbm, orders.at[1]),
                (dec_hbm, wcat.at[pl.ds(0, lats)]),
                (enc_hbm, wcat.at[pl.ds(lats, lats)]),
                (dec_hbm, wtwice.at[pl.ds(0, lats)]),
                (dec_hbm, wtwice.at[pl.ds(lats, lats)]),
                (disc_hbm, discw),
            ]
        )
    ]
    for load in loads[:4]:
        load.start()
    for i in range(rows):
        piece = pl.ds(i * LANES, LANES)
        copy = pltpu.make_async_copy(feat_hbm.at[piece], x.at[piece], feat_sem.at[i])
        copy.start()
    for load in loads[4:]:
        load.start()

    barrier = pltpu.get_barrier_semaphore()

    def greet_row(k, carry):
        other = lax.rem(r + k, n_row)
        pl.semaphore_signal(barrier, inc=1, device_id=(other, c), device_id_type=MESH)
        return carry

    def greet_col(k, carry):
        other = lax.rem(c + k, n_col)
        pl.semaphore_signal(barrier, inc=1, device_id=(r, other), device_id_type=MESH)
        return carry

    lax.fori_loop(1, n_row, greet_row, 0)
    lax.fori_loop(1, n_col, greet_col, 0)

    def build_send():
        def body(a):
            line = orders[0, pl.ds(a, 1), :].astype(F32)
            column = jnp.broadcast_to(line, (LANES, LANES)).T
            for t in range(rows):
                index = (lane + t * LANES).astype(F32)
                send_pick[bins_of(a), t * LANES : (t + 1) * LANES] = jnp.where(
                    column == index, 1.0, 0.0
                ).astype(BF16)

        each(rows, body)

    def build_recv():
        def body(a, carry):
            line = orders[1, pl.ds(a, 1), :].astype(F32)
            column = jnp.broadcast_to(line, (LANES, LANES)).T
            for t in range(rows):
                index = (lane + t * LANES).astype(F32)
                recv_pick[
                    pl.ds(pl.multiple_of(a * LANES, LANES), LANES), t * LANES : (t + 1) * LANES
                ] = jnp.where(column == index, 1.0, 0.0).astype(BF16)
            return carry

        lax.fori_loop(0, rows, body, 0)

    def build_recv_t():
        def body(t, carry):
            index = (lax.broadcasted_iota(jnp.int32, (LANES, 1), 0) + t * LANES).astype(F32)
            for a in range(rows):
                line = orders[1, a : a + 1, :].astype(F32)
                recv_pick_t[
                    pl.ds(pl.multiple_of(t * LANES, LANES), LANES), a * LANES : (a + 1) * LANES
                ] = jnp.where(line == index, 1.0, 0.0).astype(BF16)
            return carry

        lax.fori_loop(0, rows, body, 0)

    def ex_copy(which, k):
        other = lax.rem(me + k, n_dev)
        return pltpu.make_async_remote_copy(
            src_ref=ex_src.at[which, other],
            dst_ref=ex_dst.at[which, me],
            send_sem=as_sem.at[which],
            recv_sem=ar_sem.at[which],
            device_id=(other // n_col, lax.rem(other, n_col)),
            device_id_type=MESH,
        )

    def peers(count, make):
        def body(k, carry):
            make(k).start()
            return carry

        lax.fori_loop(1, count, body, 0)

    def drain(ref, count, send_sem, recv_sem):
        most = ref.at[pl.ds(0, count - 1)]
        pltpu.make_async_copy(most, most, recv_sem).wait()
        pltpu.make_async_copy(most, most, send_sem).wait()

    def ex_start(which):
        peers(n_dev, functools.partial(ex_copy, which))
        ex_dst[which, me] = ex_src[which, me]

    def ex_wait(which):
        drain(ex_dst.at[which], n_dev, as_sem.at[which], ar_sem.at[which])
        return ex_dst[which].reshape(bins, LANES)

    loads[0].wait()
    loads[1].wait()
    build_send()
    build_recv()
    for way in range(8):

        @pl.when(jnp.logical_not(present(way)))
        def _():
            for turn in range(ROUNDS):
                if way < 2 and turn in PACKED:
                    empty = h_pack.at[PACKED[turn], way]
                else:
                    empty = halo_buffer(turn, way)
                empty[...] = jnp.zeros_like(empty)

    loads[2].wait()
    loads[3].wait()

    pl.semaphore_wait(barrier, n_row + n_col - 2)

    def greet_meet(k, carry):
        other = lax.rem(c + k, n_col)
        pl.semaphore_signal(meet_sem, inc=1, device_id=(r, other), device_id_type=MESH)
        return carry

    lax.fori_loop(1, n_col, greet_meet, 0)
    for k in range(rows):
        pltpu.make_async_copy(feat_hbm.at[bins_of(k)], x.at[bins_of(k)], feat_sem.at[k]).wait()
    flat = dot(wcat[...], x[...], 1, 1)
    xp_t[...] = flat
    picked = dot(flat.astype(BF16), send_pick[...], 1, 1)
    each_dev = LANES // portion
    for i in range(rows):
        block = picked[:, i * LANES : (i + 1) * LANES].T.astype(BF16)
        ex_src[0, i * each_dev : (i + 1) * each_dev] = block.reshape(each_dev, portion, LANES)

    pl.semaphore_wait(meet_sem, n_col - 1)

    for i in range(rows):
        block = xp_t[:, i * LANES : (i + 1) * LANES].T
        xp[bins_of(i), :] = block
        put(0, i, swap(block.astype(BF16).astype(F32)))
    halo_start(0)
    ex_start(0)

    def elu(value):
        return jnp.where(value > 0, value, jnp.exp(jnp.minimum(value, 0.0)) - 1.0)

    def first_latent(i, value):
        lat[i] = value
        emb[i] = elu(value)

    halo_take(0)
    stencil(0, first_latent)

    low_in[...] = ex_wait(0)

    def pick_in(i):
        here = bins_of(i, chunk)
        value = dot(recv_pick[here, :], low_in[...])
        for k in range(rows // CHUNKS):
            at = i * (rows // CHUNKS) + k
            put(1, at, jnp.where(first, emb[at], value[k * LANES : (k + 1) * LANES, :]))

    each(CHUNKS, pick_in)
    halo_start(1)
    build_recv_t()
    gram = dot(wcat[0:lats, :], wcat[0:lats, :], 1, 1)
    gram_high = gram.astype(BF16)
    gram_low = (gram - gram_high.astype(F32)).astype(BF16)
    gram2[...] = jnp.zeros_like(gram2)
    gram2[0:lats, 0:lats] = gram_high
    gram2[lats:, 0:lats] = gram_low

    def first_spread(i, value):
        out = elu(value)
        lat[i] = jnp.where(first, lat[i], value)
        emb[i] = jnp.where(first, emb[i], out)
        put(2, i, out)
        spread[i] = value

    halo_take(1)
    stencil(1, first_spread)
    halo_start(2)

    def after_spread(i):
        value = spread[i]
        here = bins_of(i)
        low = value.astype(BF16).astype(F32)
        summ[i] = jax.nn.sigmoid(value)
        s_low[here, :] = jnp.where(first, low, swap(low)).astype(BF16)
        lt[0:lats, here] = low.T[0:lats, :].astype(BF16)

    each(rows, after_spread)

    back[...] = slope_scale * (
        dot(s_low[...], gram2[...]) - jnp.where(first, xp[...], 0.0)
    )

    core = lax.rem(r, 2)
    n_part = n_group // few

    def part_at(k):
        return lax.rem(my_group // few + 1 + k, n_part)

    def rs0_copy(which, k):
        here = pl.ds(part_at(k) * few, few)
        return pltpu.make_async_remote_copy(
            src_ref=rs0_src.at[which, here],
            dst_ref=rs0_dst.at[which, here],
            send_sem=r0s_sem.at[which, k],
            recv_sem=r0r_sem.at[which, k],
            device_id=(r + 1 - 2 * core, c),
            device_id_type=MESH,
        )

    def rs0_run(which, product):
        def body(k):
            part = part_at(k)
            value = product(bins_of(part, few * span))
            for j in range(few):
                at = j * span
                middle = value[:, at + LANES : at + 2 * LANES]
                top, bottom = middle[: lats // 2, :], middle[lats // 2 :, :]
                lower = jnp.concatenate(
                    [value[:, at : at + LANES], jnp.where(first, top, swap(bottom))], axis=0
                )
                upper = jnp.concatenate(
                    [value[:, at + 2 * LANES : at + span], jnp.where(first, swap(top), bottom)],
                    axis=0,
                )
                rs0_keep[which, part * few + j] = jnp.where(core == 0, lower, upper)
                rs0_src[which, part * few + j] = jnp.where(core == 0, upper, lower).astype(BF16)
            rs0_copy(which, k).start()

        each(n_part, body)

    def rs1_start(which):
        def body(k):
            rs0_copy(which, k).wait()
            for j in range(few):
                group = part_at(k) * few + j
                total = rs0_keep[which, group] + rs0_dst[which, group].astype(F32)
                rs1_src[which, group] = total.astype(BF16)

                @pl.when(group != my_group)
                def _():
                    pltpu.make_async_remote_copy(
                        src_ref=rs1_src.at[which, group],
                        dst_ref=rs1_dst.at[which, my_group],
                        send_sem=r1s_sem.at[which],
                        recv_sem=r1r_sem.at[which],
                        device_id=(2 * group + core, c),
                        device_id_type=MESH,
                    ).start()

        each(n_part, body)

    def rs1_finish(which):
        drain(rs1_dst.at[which], n_group, r1s_sem.at[which], r1r_sem.at[which])
        rs1_dst[which, my_group] = rs1_src[which, my_group]
        total = rs1_dst[which, 0].astype(F32)
        for k in range(1, n_group):
            total += rs1_dst[which, k].astype(F32)
        rs2_src[which] = total.astype(BF16)

    def rs2_copy(which, k):
        other = lax.rem(c + k, n_col)
        return pltpu.make_async_remote_copy(
            src_ref=rs2_src.at[which],
            dst_ref=rs2_dst.at[which, c],
            send_sem=r2s_sem.at[which],
            recv_sem=r2r_sem.at[which],
            device_id=(r, other),
            device_id_type=MESH,
        )

    def rs2_start(which):
        peers(n_col, functools.partial(rs2_copy, which))
        rs2_dst[which, c] = rs2_src[which]

    def rs2_finish(which):
        drain(rs2_dst.at[which], n_col, r2s_sem.at[which], r2r_sem.at[which])
        total = rs2_dst[which, 0].astype(F32)
        for k in range(1, n_col):
            total += rs2_dst[which, k].astype(F32)
        squares = jnp.broadcast_to(jnp.sum(total * total), (1, LANES))
        norm_src[...] = jnp.where(first, norm_src[...], squares) if which else squares
        pairs = total[lats:, :]
        pairs = jnp.concatenate([pairs, swap(pairs)], axis=0).T
        by_gene[pl.ds(pl.multiple_of(core * lats, lats), LANES), :] = total[:lats, :].T
        by_gene[pl.ds(pl.multiple_of((1 - core) * LANES, LANES), lats), :] = pairs[:lats, :]
        return by_gene[pl.ds(pl.multiple_of(c * per_dev, 8), per_dev), :]

    loads[6].wait()
    wide = jnp.concatenate([discw[...], jnp.zeros_like(discw)], axis=1)
    block = jnp.concatenate([wide, pltpu.roll(wide, lats, 1)], axis=0)
    block_high = block.astype(BF16)
    block_low = (block - block_high.astype(F32)).astype(BF16)
    for u in range(2):
        one = slice(u * LANES, (u + 1) * LANES)
        bd_nt[0:LANES, one] = block_high
        bd_nt[LANES:, one] = block_low
        bd_nn[one, 0:LANES] = block_high
        bd_nn[one, LANES:] = block_low
    for i in range(rows):
        stage[:, i, :] = emb[i].T
    emb_out[...] = stage[0:lats]
    outs[3].start()
    halo_take(2)

    def to_summary(i, value):
        summ[i] = jnp.where(first, summ[i], jax.nn.sigmoid(value))

    stencil(2, to_summary)

    half_sum = jnp.where(
        (lax.broadcasted_iota(jnp.int32, (LANES, LANES), 0) < lats)
        == (lax.broadcasted_iota(jnp.int32, (LANES, LANES), 1) < lats),
        1.0,
        0.0,
    ).astype(BF16)
    half_sum2 = jnp.concatenate([half_sum, half_sum], axis=0)

    step = rows // CHUNKS

    def contrast(i):
        piece = pl.ds(i * step, step)
        here = bins_of(i, chunk)
        summary = summ[piece].reshape(chunk, LANES)
        embedded = emb[piece].reshape(chunk, LANES)
        swapped = swap(embedded)
        summary_2 = split_2(summary)
        wide_q = dot(summary_2, bd_nt[...], 1, 1)
        queries = wide_q[:, :LANES] + wide_q[:, LANES:]
        logit_same = dot(split_2(embedded * queries), half_sum2)
        logit_other = dot(split_2(swapped * queries), half_sum2)
        grad_same = -jax.nn.sigmoid(-logit_same)
        grad_other = jax.nn.sigmoid(logit_other)
        embed_grad = grad_same * queries + swap(grad_other * queries)
        query_grad = grad_same * embedded + grad_other * swapped
        query_grad_2 = split_2(query_grad)
        grads_2[here, :] = query_grad_2
        summ_2[here, :] = summary_2
        wide_s = dot(query_grad_2, bd_nn[...])
        summary_grad = wide_s[:, :LANES] + wide_s[:, LANES:]
        spread_grad = summary_grad * summary * (1.0 - summary)
        spread_grad += back[here, :]
        eg[piece] = embed_grad.reshape(step, LANES, LANES)
        mix[here, :] = jnp.where(lax.rem(lane, lats) < lats // 2, logit_same, logit_other)
        for j in range(step):
            put(3, i * step + j, spread_grad[j * LANES : (j + 1) * LANES, :])

    for i in range(CHUNKS):
        contrast(i)
    halo_start(3)

    def disc_step(i, total):
        here = bins_of(i, chunk)
        return total + dot(grads_2[here, :], summ_2[here, :], 0, 0)

    disc_total = lax.fori_loop(
        0, CHUNKS, disc_step, jnp.zeros((2 * LANES, 2 * LANES), F32)
    )
    quarter = (disc_total[:LANES, :LANES] + disc_total[LANES:, :LANES]) + (
        disc_total[:LANES, LANES:] + disc_total[LANES:, LANES:]
    )
    disc_src[...] = quarter[:lats, :] + swap(quarter[lats:, :])

    def part_of(index):
        return pl.ds(pl.multiple_of(index * part, 8), part)

    def disc_1(k):
        other = lax.rem(c + k, n_col)
        return pltpu.make_async_remote_copy(
            src_ref=disc_src.at[part_of(other)],
            dst_ref=disc_a.at[c],
            send_sem=ds_sem.at[0],
            recv_sem=dr_sem.at[0],
            device_id=(r, other),
            device_id_type=MESH,
        )

    disc_a[c] = disc_src[part_of(c), :]
    peers(n_col, disc_1)

    for i in range(rows):
        flipped = mix[i * LANES : (i + 1) * LANES, :].T
        for k in range(4):
            at = k * (lats // 2)
            log_out[k, i : i + 1, :] = flipped[at : at + 1, :]
    outs[4].start()
    square = dot(lt[0:lats, :], s_low[...])
    square_high = square.astype(BF16).astype(F32)
    square2 = jnp.where(first, square_high, square - square_high).astype(BF16)
    loads[4].wait()
    loads[5].wait()
    rs0_run(
        0,
        lambda where: slope_scale
        * (dot(square2, wtwice[:, where]) - dot(lt[0:lats, :], x[:, where])),
    )

    halo_take(3)

    def to_latent_grad(i, value):
        z = lat[i]
        slope = jnp.where(z > 0, 1.0, jnp.exp(jnp.minimum(z, 0.0)))
        put(4, i, (eg[i] + value) * slope)

    stencil(3, to_latent_grad)
    halo_start(4)

    drain(disc_a, n_col, ds_sem.at[0], dr_sem.at[0])
    disc_bsrc[...] = jnp.sum(disc_a[...], axis=0)

    def disc_2(k):
        other = lax.rem(r + k, n_row)
        return pltpu.make_async_remote_copy(
            src_ref=disc_bsrc,
            dst_ref=disc_b.at[r],
            send_sem=ds_sem.at[1],
            recv_sem=dr_sem.at[1],
            device_id=(other, c),
            device_id_type=MESH,
        )

    disc_b[r] = disc_bsrc[...]
    peers(n_row, disc_2)
    halo_take(4)
    rs1_start(0)

    def to_proj_grad(i, value):
        pg_low[bins_of(i), :] = value.astype(BF16)

    stencil(4, to_proj_grad)

    def pick_back(i):
        value = dot(recv_pick_t[bins_of(i, chunk), :], pg_low[...])
        ex_src[1, pl.ds(i * (n_dev // CHUNKS), n_dev // CHUNKS)] = value.astype(BF16).reshape(
            n_dev // CHUNKS, portion, LANES
        )

    each(CHUNKS, pick_back)
    ex_start(1)
    for i in range(rows):
        here = slice(i * LANES, (i + 1) * LANES)
        flipped = pg_low[here, :].astype(F32).T
        stage[:, i, :] = flipped
        own[:, here] = flipped[:lats, :].astype(BF16)
    pg_out[...] = stage[...].astype(BF16)
    outs[5].start()

    rs1_finish(0)
    drain(disc_b, n_row, ds_sem.at[1], dr_sem.at[1])
    disc_full[c] = jnp.sum(disc_b[...], axis=0)

    def disc_3(k):
        other = lax.rem(c + k, n_col)
        return pltpu.make_async_remote_copy(
            src_ref=disc_full.at[c],
            dst_ref=disc_full.at[c],
            send_sem=ds_sem.at[2],
            recv_sem=dr_sem.at[2],
            device_id=(r, other),
            device_id_type=MESH,
        )

    peers(n_col, disc_3)

    for turn in range(ROUNDS):
        halo_finish(turn)

    lt[0:lats, :] = own[...]
    home = ex_wait(1)
    rs2_start(0)
    flipped = jnp.concatenate(
        [home[i * LANES : (i + 1) * LANES, :].astype(F32).T[lats:, :] for i in range(rows)], axis=1
    ).astype(BF16)
    lt[lats:, :] = dot(flipped, send_pick[...]).astype(BF16)

    def encoder_part(where):
        value = dot(lt[...], x[:, where])
        return value[:lats, :] + value[lats:, :]

    rs0_run(1, encoder_part)
    rs1_start(1)

    drain(disc_full, n_col, ds_sem.at[2], dr_sem.at[2])
    disc_grad = disc_full[...].reshape(lats, LANES)[:, :lats]
    disc_mean = jnp.sum(disc_grad * disc_grad) / (lats * lats)
    disc_out[...] = disc_grad * lax.rsqrt(disc_mean + 1e-06)
    outs[2].start()

    dec_sum[...] = rs2_finish(0)
    rs1_finish(1)
    rs2_start(1)
    enc_sum = rs2_finish(1)

    def norm_1(k):
        other = lax.rem(r + k, n_row)
        return pltpu.make_async_remote_copy(
            src_ref=norm_src,
            dst_ref=norm_a.at[r],
            send_sem=ns_sem.at[0],
            recv_sem=nr_sem.at[0],
            device_id=(other, c),
            device_id_type=MESH,
        )

    norm_a[r] = norm_src[...]
    peers(n_row, norm_1)
    drain(norm_a, n_row, ns_sem.at[0], nr_sem.at[0])
    totals = norm_a[0]
    for k in range(1, n_row):
        totals += norm_a[k]
    entries = genes * lats
    enc_out[...] = enc_sum * lax.rsqrt(totals[0:1, lats : lats + 1] / entries + 1e-06)
    dec_out[...] = dec_sum[...] * lax.rsqrt(totals[0:1, 0:1] / entries + 1e-06)
    outs[0].start()
    outs[1].start()
    for out in outs:
        out.wait()


def hand_on(*refs):
    count = (len(refs) - 2) // 3
    sources, targets, held = (refs[k * count : (k + 1) * count] for k in range(3))
    come, go = refs[3 * count :]
    ins = [pltpu.make_async_copy(sources[i], held[i], come.at[i]) for i in range(count)]
    outs = [pltpu.make_async_copy(held[i], targets[i], go.at[i]) for i in range(count)]
    for copy in ins:
        copy.start()
    for i in range(count):
        ins[i].wait()
        outs[i].start()
    for copy in outs:
        copy.wait()


def per_device(features, enc_weight, dec_weight, disc_weight, send_order, recv_order):
    tile_rows, tile_cols, genes = features.shape
    lats = enc_weight.shape[1]
    bins = tile_rows * tile_cols
    n_row = lax.axis_size("row")
    n_col = lax.axis_size("col")
    n_dev = n_row * n_col
    n_group = n_row // 2
    per_dev = genes // n_dev
    span = genes // n_group
    part = lats // n_col
    packed = lats + lats // 2
    portion = bins // n_dev
    field = (tile_rows, LANES, LANES)
    dma = pltpu.SemaphoreType.DMA
    vmem = pltpu.VMEM
    shape = jax.ShapeDtypeStruct
    out_shape = [
        shape((per_dev, lats), F32),
        shape((per_dev, lats), F32),
        shape((lats, lats), F32),
        shape((lats, tile_rows, tile_cols), F32),
        shape((4, tile_rows, tile_cols), F32),
        shape((2 * lats, tile_rows, tile_cols), BF16),
    ]
    scratch = [
        *(vmem(one.shape, one.dtype) for one in out_shape),
        vmem((bins, genes), BF16),
        vmem((lats, lats), F32),
        vmem((2, tile_rows, LANES), jnp.int32),
        vmem((2 * lats, genes), BF16),
        vmem((2 * lats, genes), BF16),
        vmem((LANES, LANES), BF16),
        vmem((2 * LANES, 2 * LANES), BF16),
        vmem((2 * LANES, 2 * LANES), BF16),
        vmem((bins, bins), BF16),
        vmem((bins, bins), BF16),
        vmem((bins, bins), BF16),
        vmem((bins, LANES), F32),
        vmem((LANES, bins), F32),
        vmem((2, n_dev, portion, LANES), BF16),
        vmem((2, n_dev, portion, LANES), BF16),
        vmem((bins, LANES), BF16),
        vmem((2, tile_rows + 2 * RADIUS, LANES + 2 * SIDE, LANES), F32),
        vmem((tile_rows, LANES + 2 * SIDE, LANES), F32),
        vmem((ROUNDS,) + field, BF16),
        vmem((ROUNDS, 2, RADIUS, LANES, LANES), BF16),
        vmem((ROUNDS, 2, tile_rows * SIDE, LANES), BF16),
        vmem((ROUNDS, 4, tile_rows * SIDE // 2, LANES), BF16),
        vmem((len(PACKED), 2, RADIUS, LANES // 2, LANES), BF16),
        vmem((len(PACKED), 2, RADIUS, LANES // 2, LANES), BF16),
        vmem((2, tile_rows * SIDE, LANES), F32),
        vmem((ROUNDS, 2, tile_rows * SIDE, LANES), BF16),
        vmem(field, F32),
        vmem(field, F32),
        vmem(field, F32),
        vmem(field, F32),
        vmem((bins, LANES), BF16),
        vmem((bins, LANES), F32),
        vmem((bins, 2 * LANES), BF16),
        vmem((bins, 2 * LANES), BF16),
        vmem((bins, LANES), F32),
        vmem(field, F32),
        vmem((bins, LANES), BF16),
        vmem((LANES, bins), BF16),
        vmem((lats, bins), BF16),
        vmem((2, n_group, packed, LANES), F32),
        vmem((2, n_group, packed, LANES), BF16),
        vmem((2, n_group, packed, LANES), BF16),
        vmem((2, n_group, packed, LANES), BF16),
        vmem((2, n_group, packed, LANES), BF16),
        vmem((2, packed, LANES), BF16),
        vmem((2, n_col, packed, LANES), BF16),
        vmem((lats, LANES), F32),
        vmem((n_col, part, LANES), F32),
        vmem((part, LANES), F32),
        vmem((n_row, part, LANES), F32),
        vmem((n_col, part, LANES), F32),
        vmem((1, LANES), F32),
        vmem((n_row, 1, LANES), F32),
        vmem((span // 2, lats), F32),
        vmem((LANES, tile_rows, LANES), F32),
        vmem((per_dev, lats), F32),
        dma((7,)),
        dma((tile_rows,)),
        dma((ROUNDS, 8)),
        dma((ROUNDS, 8)),
        dma((2,)),
        dma((2,)),
        dma((2, 2)),
        dma((2, 2)),
        dma((2,)),
        dma((2,)),
        dma((2,)),
        dma((2,)),
        dma((3,)),
        dma((3,)),
        dma((1,)),
        dma((1,)),
        pltpu.SemaphoreType.REGULAR,
        dma((6,)),
    ]
    anywhere = [pl.BlockSpec(memory_space=pl.ANY)] * 6
    results = pl.pallas_call(
        functools.partial(kernel, n_row, n_col),
        out_shape=out_shape,
        in_specs=anywhere,
        out_specs=anywhere,
        scratch_shapes=scratch,
        compiler_params=pltpu.CompilerParams(
            collective_id=0, has_side_effects=True, vmem_limit_bytes=56 * 1024 * 1024
        ),
    )(
        features.reshape(bins, genes),
        enc_weight.T,
        dec_weight.T,
        disc_weight,
        send_order.reshape(tile_rows, LANES),
        recv_order.reshape(tile_rows, LANES),
    )
    *others, grads = pl.pallas_call(
        hand_on,
        out_shape=out_shape,
        in_specs=anywhere,
        out_specs=anywhere,
        scratch_shapes=[*(vmem(one.shape, one.dtype) for one in out_shape), dma((6,)), dma((6,))],
    )(*results)
    return (*others, grads.reshape(2, lats, tile_rows, tile_cols))


def solution(mesh):
    in_specs = (P("row", "col", None), P(), P(), P(), P("row", "col", None), P("row", "col", None))
    out_specs = (
        P(("row", "col"), None),
        P(("row", "col"), None),
        P(),
        P(None, "row", "col"),
        P(None, "row", "col"),
        P(None, None, "row", "col"),
    )
    return jax.shard_map(
        per_device, mesh=mesh, in_specs=in_specs, out_specs=out_specs, check_vma=False
    )
```

```python
import functools
import math

import jax
import jax.numpy as jnp
from jax import lax
from jax.experimental import pallas as pl
from jax.experimental.pallas import tpu as pltpu
from jax.sharding import PartitionSpec as P

RADIUS = 3
RECON_WEIGHT = 10.0
LANES = 128
SIDE = 8
STRIDE = 37
UNROLL = 8
MESH = pl.DeviceIdType.MESH
F32 = jnp.float32
BF16 = jnp.bfloat16
DIRECTIONS = ((-1, 0), (1, 0), (0, -1), (0, 1), (-1, -1), (-1, 1), (1, -1), (1, 1))
OPPOSITE = (1, 0, 3, 2, 7, 6, 5, 4)
ROUNDS = 5
PACKED = {0: 0, 2: 1}
CHUNKS = 4


def stencil_taps():
    raw_taps = [math.exp(-offset * offset / 12.0) for offset in range(-RADIUS, RADIUS + 1)]
    tap_total = sum(raw_taps)
    return [raw_value / tap_total for raw_value in raw_taps]


def dot(a, b, ca=1, cb=0):
    return lax.dot_general(a, b, (((ca,), (cb,)), ((), ())), preferred_element_type=F32)


def each(count, body):
    def step(i, carry):
        body(i)
        return carry

    lax.fori_loop(0, count, step, 0)


def when(test):
    if isinstance(test, bool):
        return (lambda body: body()) if test else (lambda body: None)
    return pl.when(test)


def split_2(value):
    high = value.astype(BF16)
    low = (value - high.astype(F32)).astype(BF16)
    return jnp.concatenate([high, low], axis=1)


def kernel(
    n_row,
    n_col,
    feat_hbm,
    enc_hbm,
    dec_hbm,
    disc_hbm,
    send_hbm,
    recv_hbm,
    enc_hbm_out,
    dec_hbm_out,
    disc_hbm_out,
    emb_hbm_out,
    log_hbm_out,
    pg_hbm_out,
    enc_out,
    dec_out,
    disc_out,
    emb_out,
    log_out,
    pg_out,
    x,
    discw,
    orders,
    wcat,
    wtwice,
    gram2,
    bd_nt,
    bd_nn,
    send_pick,
    recv_pick,
    recv_pick_t,
    xp,
    xp_t,
    ex_src,
    ex_dst,
    low_in,
    pads,
    tmp,
    hsrc,
    h_row,
    h_col,
    h_corner,
    pack_src,
    h_pack,
    edge,
    edge_src,
    lat,
    emb,
    spread,
    summ,
    s_low,
    back,
    grads_2,
    summ_2,
    mix,
    eg,
    pg_low,
    lt,
    own,
    rs0_keep,
    rs0_src,
    rs0_dst,
    rs1_src,
    rs1_dst,
    rs2_src,
    rs2_dst,
    disc_src,
    disc_a,
    disc_bsrc,
    disc_b,
    disc_full,
    norm_src,
    norm_a,
    by_gene,
    stage,
    dec_sum,
    load_sem,
    feat_sem,
    hs_sem,
    hr_sem,
    as_sem,
    ar_sem,
    r0s_sem,
    r0r_sem,
    r1s_sem,
    r1r_sem,
    r2s_sem,
    r2r_sem,
    ds_sem,
    dr_sem,
    ns_sem,
    nr_sem,
    meet_sem,
    out_sem,
):
    n_dev = n_row * n_col
    bins, genes = x.shape
    rows = bins // LANES
    lats = discw.shape[1]
    portion = bins // n_dev
    n_group = n_row // 2
    few = min(4, n_group)
    per_dev = genes // n_dev
    span = genes // n_group
    part = lats // n_col
    slope_scale = 2.0 * RECON_WEIGHT / genes
    tap = stencil_taps()
    chunk = bins // CHUNKS

    r = lax.axis_index("row")
    c = lax.axis_index("col")
    me = r * n_col + c
    my_group = r // 2
    lane = lax.broadcasted_iota(jnp.int32, (1, LANES), 1)
    first = lane < lats

    outs = [
        pltpu.make_async_copy(a, b, out_sem.at[i])
        for i, (a, b) in enumerate(
            [
                (enc_out, enc_hbm_out),
                (dec_out, dec_hbm_out),
                (disc_out, disc_hbm_out),
                (emb_out, emb_hbm_out),
                (log_out, log_hbm_out),
                (pg_out, pg_hbm_out),
            ]
        )
    ]

    def bins_of(i, size=LANES):
        return pl.ds(i * size if isinstance(i, int) else pl.multiple_of(i * size, size), size)

    def swap(value):
        return pltpu.roll(value, lats, value.ndim - 1)

    def halo_buffer(turn, way):
        if way < 2:
            return h_row.at[turn, way]
        if way < 4:
            return h_col.at[turn, way - 2]
        return h_corner.at[turn, way - 4]

    def halo_copy(turn, way):
        dr, dc = DIRECTIONS[way]
        if way < 2 and turn in PACKED:
            source = pack_src.at[PACKED[turn], way]
            target = h_pack.at[PACKED[turn], OPPOSITE[way]]
        elif way < 2:
            source = hsrc.at[turn, pl.ds(0 if dr < 0 else rows - RADIUS, RADIUS)]
            target = halo_buffer(turn, OPPOSITE[way])
        else:
            half = rows * SIDE // 2
            source = edge_src.at[turn, 0 if dc < 0 else 1]
            if dr:
                source = source.at[pl.ds(0 if dr < 0 else half, half)]
            target = halo_buffer(turn, OPPOSITE[way])
        return pltpu.make_async_remote_copy(
            src_ref=source,
            dst_ref=target,
            send_sem=hs_sem.at[turn, way],
            recv_sem=hr_sem.at[turn, OPPOSITE[way]],
            device_id=(r + dr, c + dc),
            device_id_type=MESH,
        )

    def present(way):
        dr, dc = DIRECTIONS[way]
        tests = []
        if dr < 0:
            tests.append(r > 0)
        if dr > 0:
            tests.append(r < n_row - 1)
        if dc < 0:
            tests.append(c > 0)
        if dc > 0:
            tests.append(c < n_col - 1)
        return functools.reduce(jnp.logical_and, tests)

    def halo_start(turn):
        edge_src[turn] = edge[...].astype(BF16)
        for way in range(8):

            @pl.when(present(way))
            def _():
                halo_copy(turn, way).start()

    def halo_take(turn):
        pad = pads.at[turn % 2]
        for way in range(8):

            @pl.when(present(way))
            def _():
                halo_copy(turn, OPPOSITE[way]).wait_recv()

        left, right = slice(0, SIDE), slice(SIDE + LANES, LANES + 2 * SIDE)
        top, bottom = slice(0, RADIUS), slice(RADIUS + rows, rows + 2 * RADIUS)
        for way, part in ((0, top), (1, bottom)):
            if turn in PACKED:
                packed = h_pack[PACKED[turn], way].astype(F32)
                halves = (packed, swap(packed)) if turn == 0 else (swap(packed), packed)
                pad[part, SIDE : SIDE + LANES // 2, :] = halves[0]
                pad[part, SIDE + LANES // 2 : SIDE + LANES, :] = halves[1]
            else:
                pad[part, SIDE : SIDE + LANES, :] = h_row[turn, way].astype(F32)
            lines = slice(rows // 2 - RADIUS, rows // 2) if way == 0 else slice(0, RADIUS)
            for k, place in ((0, left), (1, right)):
                corner = h_corner[turn, 2 * way + k].astype(F32).reshape(rows // 2, SIDE, LANES)
                pad[part, place, :] = corner[lines]
        own_rows = slice(RADIUS, RADIUS + rows)
        for k, place in ((0, left), (1, right)):
            pad[own_rows, place, :] = h_col[turn, k].astype(F32).reshape(rows, SIDE, LANES)

    def halo_finish(turn):
        for way in range(8):

            @pl.when(present(way))
            def _():
                halo_copy(turn, way).wait_send()

    def stencil(turn, then):
        pad = pads.at[turn % 2]

        def down(t):
            at = pl.ds(pl.multiple_of(t * SIDE, SIDE), SIDE)
            block = pad[:, at, :]
            across = tap[RADIUS] * block[RADIUS : RADIUS + rows]
            for k in range(1, RADIUS + 1):
                across += tap[RADIUS + k] * (
                    block[RADIUS - k : RADIUS - k + rows] + block[RADIUS + k : RADIUS + k + rows]
                )
            tmp[:, at, :] = across

        def along(i):
            total = tap[RADIUS] * tmp[i, SIDE : SIDE + LANES, :]
            for k in range(1, RADIUS + 1):
                total += tap[RADIUS + k] * (
                    tmp[i, SIDE - k : SIDE - k + LANES, :] + tmp[i, SIDE + k : SIDE + k + LANES, :]
                )
            then(i, total)

        each(LANES // SIDE + 2, down)
        each(rows, along)

    def put(turn, i, value):
        pads[turn % 2, i + RADIUS, SIDE : SIDE + LANES, :] = value
        edge[0, bins_of(i, SIDE), :] = value[0:SIDE, :]
        edge[1, bins_of(i, SIDE), :] = value[LANES - SIDE :, :]
        if turn not in PACKED:
            hsrc[turn, i] = value.astype(BF16)
            return
        front, rear = value[: LANES // 2, :], value[LANES // 2 :, :]
        if turn == 0:
            packed = jnp.where(first, front, swap(rear)).astype(BF16)
        else:
            packed = jnp.where(first, swap(front), rear).astype(BF16)

        @when(i < RADIUS)
        def _():
            pack_src[PACKED[turn], 0, i] = packed

        @when(i >= rows - RADIUS)
        def _():
            pack_src[PACKED[turn], 1, i - (rows - RADIUS)] = packed

    loads = [
        pltpu.make_async_copy(a, b, load_sem.at[i])
        for i, (a, b) in enumerate(
            [
                (send_hbm, orders.at[0]),
                (recv_hbm, orders.at[1]),
                (dec_hbm, wcat.at[pl.ds(0, lats)]),
                (enc_hbm, wcat.at[pl.ds(lats, lats)]),
                (dec_hbm, wtwice.at[pl.ds(0, lats)]),
                (dec_hbm, wtwice.at[pl.ds(lats, lats)]),
                (disc_hbm, discw),
            ]
        )
    ]
    for load in loads[:4]:
        load.start()
    for i in range(rows):
        piece = pl.ds(i * LANES, LANES)
        copy = pltpu.make_async_copy(feat_hbm.at[piece], x.at[piece], feat_sem.at[i])
        copy.start()
    for load in loads[4:]:
        load.start()

    barrier = pltpu.get_barrier_semaphore()

    def greet_row(k, carry):
        other = lax.rem(r + k, n_row)
        pl.semaphore_signal(barrier, inc=1, device_id=(other, c), device_id_type=MESH)
        return carry

    def greet_col(k, carry):
        other = lax.rem(c + k, n_col)
        pl.semaphore_signal(barrier, inc=1, device_id=(r, other), device_id_type=MESH)
        return carry

    lax.fori_loop(1, n_row, greet_row, 0)
    lax.fori_loop(1, n_col, greet_col, 0)

    def build_send():
        def body(a):
            line = orders[0, pl.ds(a, 1), :].astype(F32)
            column = jnp.broadcast_to(line, (LANES, LANES)).T
            for t in range(rows):
                index = (lane + t * LANES).astype(F32)
                send_pick[bins_of(a), t * LANES : (t + 1) * LANES] = jnp.where(
                    column == index, 1.0, 0.0
                ).astype(BF16)

        each(rows, body)

    def build_recv():
        def body(a, carry):
            line = orders[1, pl.ds(a, 1), :].astype(F32)
            column = jnp.broadcast_to(line, (LANES, LANES)).T
            for t in range(rows):
                index = (lane + t * LANES).astype(F32)
                recv_pick[
                    pl.ds(pl.multiple_of(a * LANES, LANES), LANES), t * LANES : (t + 1) * LANES
                ] = jnp.where(column == index, 1.0, 0.0).astype(BF16)
            return carry

        lax.fori_loop(0, rows, body, 0)

    def build_recv_t():
        def body(t, carry):
            index = (lax.broadcasted_iota(jnp.int32, (LANES, 1), 0) + t * LANES).astype(F32)
            for a in range(rows):
                line = orders[1, a : a + 1, :].astype(F32)
                recv_pick_t[
                    pl.ds(pl.multiple_of(t * LANES, LANES), LANES), a * LANES : (a + 1) * LANES
                ] = jnp.where(line == index, 1.0, 0.0).astype(BF16)
            return carry

        lax.fori_loop(0, rows, body, 0)

    def ex_copy(which, k):
        other = lax.rem(me + k * STRIDE, n_dev)
        return pltpu.make_async_remote_copy(
            src_ref=ex_src.at[which, other],
            dst_ref=ex_dst.at[which, me],
            send_sem=as_sem.at[which],
            recv_sem=ar_sem.at[which],
            device_id=(other // n_col, lax.rem(other, n_col)),
            device_id_type=MESH,
        )

    def peers(count, make):
        def body(k, carry):
            make(k).start()
            return carry

        lax.fori_loop(1, count, body, 0)

    def drain(ref, count, send_sem, recv_sem):
        most = ref.at[pl.ds(0, count - 1)]
        pltpu.make_async_copy(most, most, recv_sem).wait()
        pltpu.make_async_copy(most, most, send_sem).wait()

    def ex_start(which):
        def several(i):
            for k in range(UNROLL):
                ex_copy(which, i * UNROLL + k).start()

        for k in range(1, UNROLL):
            ex_copy(which, k).start()
        each(n_dev // UNROLL - 1, lambda i: several(i + 1))
        ex_dst[which, me] = ex_src[which, me]

    def ex_wait(which):
        drain(ex_dst.at[which], n_dev, as_sem.at[which], ar_sem.at[which])
        return ex_dst[which].reshape(bins, LANES)

    loads[0].wait()
    loads[1].wait()
    build_send()
    build_recv()
    for way in range(8):

        @pl.when(jnp.logical_not(present(way)))
        def _():
            for turn in range(ROUNDS):
                if way < 2 and turn in PACKED:
                    empty = h_pack.at[PACKED[turn], way]
                else:
                    empty = halo_buffer(turn, way)
                empty[...] = jnp.zeros_like(empty)

    loads[2].wait()
    loads[3].wait()

    pl.semaphore_wait(barrier, n_row + n_col - 2)

    def greet_meet(k, carry):
        other = lax.rem(c + k, n_col)
        pl.semaphore_signal(meet_sem, inc=1, device_id=(r, other), device_id_type=MESH)
        return carry

    lax.fori_loop(1, n_col, greet_meet, 0)
    for k in range(rows):
        pltpu.make_async_copy(feat_hbm.at[bins_of(k)], x.at[bins_of(k)], feat_sem.at[k]).wait()
    flat = dot(wcat[...], x[...], 1, 1)
    xp_t[...] = flat
    picked = dot(flat.astype(BF16), send_pick[...], 1, 1)
    each_dev = LANES // portion
    for i in range(rows):
        block = picked[:, i * LANES : (i + 1) * LANES].T.astype(BF16)
        ex_src[0, i * each_dev : (i + 1) * each_dev] = block.reshape(each_dev, portion, LANES)

    pl.semaphore_wait(meet_sem, n_col - 1)

    for i in range(rows):
        block = xp_t[:, i * LANES : (i + 1) * LANES].T
        xp[bins_of(i), :] = block
        put(0, i, swap(block.astype(BF16).astype(F32)))
    halo_start(0)
    ex_start(0)

    def elu(value):
        return jnp.where(value > 0, value, jnp.exp(jnp.minimum(value, 0.0)) - 1.0)

    def first_latent(i, value):
        lat[i] = value
        emb[i] = elu(value)

    halo_take(0)
    stencil(0, first_latent)

    low_in[...] = ex_wait(0)

    def pick_in(i):
        here = bins_of(i, chunk)
        value = dot(recv_pick[here, :], low_in[...])
        for k in range(rows // CHUNKS):
            at = i * (rows // CHUNKS) + k
            put(1, at, jnp.where(first, emb[at], value[k * LANES : (k + 1) * LANES, :]))

    each(CHUNKS, pick_in)
    halo_start(1)
    build_recv_t()
    gram = dot(wcat[0:lats, :], wcat[0:lats, :], 1, 1)
    gram_high = gram.astype(BF16)
    gram_low = (gram - gram_high.astype(F32)).astype(BF16)
    gram2[...] = jnp.zeros_like(gram2)
    gram2[0:lats, 0:lats] = gram_high
    gram2[lats:, 0:lats] = gram_low

    def first_spread(i, value):
        out = elu(value)
        lat[i] = jnp.where(first, lat[i], value)
        emb[i] = jnp.where(first, emb[i], out)
        put(2, i, out)
        spread[i] = value

    halo_take(1)
    stencil(1, first_spread)
    halo_start(2)

    def after_spread(i):
        value = spread[i]
        here = bins_of(i)
        low = value.astype(BF16).astype(F32)
        summ[i] = jax.nn.sigmoid(value)
        s_low[here, :] = jnp.where(first, low, swap(low)).astype(BF16)
        lt[0:lats, here] = low.T[0:lats, :].astype(BF16)

    each(rows, after_spread)

    back[...] = slope_scale * (
        dot(s_low[...], gram2[...]) - jnp.where(first, xp[...], 0.0)
    )

    core = lax.rem(r, 2)
    n_part = n_group // few

    def part_at(k):
        return lax.rem(my_group // few + 1 + k, n_part)

    def rs0_copy(which, k):
        here = pl.ds(part_at(k) * few, few)
        return pltpu.make_async_remote_copy(
            src_ref=rs0_src.at[which, here],
            dst_ref=rs0_dst.at[which, here],
            send_sem=r0s_sem.at[which, k],
            recv_sem=r0r_sem.at[which, k],
            device_id=(r + 1 - 2 * core, c),
            device_id_type=MESH,
        )

    def rs0_run(which, product):
        def body(k):
            part = part_at(k)
            value = product(bins_of(part, few * span))
            for j in range(few):
                at = j * span
                middle = value[:, at + LANES : at + 2 * LANES]
                top, bottom = middle[: lats // 2, :], middle[lats // 2 :, :]
                lower = jnp.concatenate(
                    [value[:, at : at + LANES], jnp.where(first, top, swap(bottom))], axis=0
                )
                upper = jnp.concatenate(
                    [value[:, at + 2 * LANES : at + span], jnp.where(first, swap(top), bottom)],
                    axis=0,
                )
                rs0_keep[which, part * few + j] = jnp.where(core == 0, lower, upper)
                rs0_src[which, part * few + j] = jnp.where(core == 0, upper, lower).astype(BF16)
            rs0_copy(which, k).start()

        each(n_part, body)

    def rs1_start(which):
        def body(k):
            rs0_copy(which, k).wait()
            for j in range(few):
                group = part_at(k) * few + j
                total = rs0_keep[which, group] + rs0_dst[which, group].astype(F32)
                rs1_src[which, group] = total.astype(BF16)

                @pl.when(group != my_group)
                def _():
                    pltpu.make_async_remote_copy(
                        src_ref=rs1_src.at[which, group],
                        dst_ref=rs1_dst.at[which, my_group],
                        send_sem=r1s_sem.at[which],
                        recv_sem=r1r_sem.at[which],
                        device_id=(2 * group + core, c),
                        device_id_type=MESH,
                    ).start()

        each(n_part, body)

    def rs1_finish(which):
        drain(rs1_dst.at[which], n_group, r1s_sem.at[which], r1r_sem.at[which])
        rs1_dst[which, my_group] = rs1_src[which, my_group]
        total = rs1_dst[which, 0].astype(F32)
        for k in range(1, n_group):
            total += rs1_dst[which, k].astype(F32)
        rs2_src[which] = total.astype(BF16)

    def rs2_copy(which, k):
        other = lax.rem(c + k, n_col)
        return pltpu.make_async_remote_copy(
            src_ref=rs2_src.at[which],
            dst_ref=rs2_dst.at[which, c],
            send_sem=r2s_sem.at[which],
            recv_sem=r2r_sem.at[which],
            device_id=(r, other),
            device_id_type=MESH,
        )

    def rs2_start(which):
        peers(n_col, functools.partial(rs2_copy, which))
        rs2_dst[which, c] = rs2_src[which]

    def rs2_finish(which):
        drain(rs2_dst.at[which], n_col, r2s_sem.at[which], r2r_sem.at[which])
        total = rs2_dst[which, 0].astype(F32)
        for k in range(1, n_col):
            total += rs2_dst[which, k].astype(F32)
        squares = jnp.broadcast_to(jnp.sum(total * total), (1, LANES))
        norm_src[...] = jnp.where(first, norm_src[...], squares) if which else squares
        pairs = total[lats:, :]
        pairs = jnp.concatenate([pairs, swap(pairs)], axis=0).T
        by_gene[pl.ds(pl.multiple_of(core * lats, lats), LANES), :] = total[:lats, :].T
        by_gene[pl.ds(pl.multiple_of((1 - core) * LANES, LANES), lats), :] = pairs[:lats, :]
        return by_gene[pl.ds(pl.multiple_of(c * per_dev, 8), per_dev), :]

    loads[6].wait()
    wide = jnp.concatenate([discw[...], jnp.zeros_like(discw)], axis=1)
    block = jnp.concatenate([wide, pltpu.roll(wide, lats, 1)], axis=0)
    block_high = block.astype(BF16)
    block_low = (block - block_high.astype(F32)).astype(BF16)
    for u in range(2):
        one = slice(u * LANES, (u + 1) * LANES)
        bd_nt[0:LANES, one] = block_high
        bd_nt[LANES:, one] = block_low
        bd_nn[one, 0:LANES] = block_high
        bd_nn[one, LANES:] = block_low
    for i in range(rows):
        stage[:, i, :] = emb[i].T
    emb_out[...] = stage[0:lats]
    outs[3].start()
    halo_take(2)

    def to_summary(i, value):
        summ[i] = jnp.where(first, summ[i], jax.nn.sigmoid(value))

    stencil(2, to_summary)

    half_sum = jnp.where(
        (lax.broadcasted_iota(jnp.int32, (LANES, LANES), 0) < lats)
        == (lax.broadcasted_iota(jnp.int32, (LANES, LANES), 1) < lats),
        1.0,
        0.0,
    ).astype(BF16)
    half_sum2 = jnp.concatenate([half_sum, half_sum], axis=0)

    step = rows // CHUNKS

    def contrast(i):
        piece = pl.ds(i * step, step)
        here = bins_of(i, chunk)
        summary = summ[piece].reshape(chunk, LANES)
        embedded = emb[piece].reshape(chunk, LANES)
        swapped = swap(embedded)
        summary_2 = split_2(summary)
        wide_q = dot(summary_2, bd_nt[...], 1, 1)
        queries = wide_q[:, :LANES] + wide_q[:, LANES:]
        logit_same = dot(split_2(embedded * queries), half_sum2)
        logit_other = dot(split_2(swapped * queries), half_sum2)
        grad_same = -jax.nn.sigmoid(-logit_same)
        grad_other = jax.nn.sigmoid(logit_other)
        embed_grad = grad_same * queries + swap(grad_other * queries)
        query_grad = grad_same * embedded + grad_other * swapped
        query_grad_2 = split_2(query_grad)
        grads_2[here, :] = query_grad_2
        summ_2[here, :] = summary_2
        wide_s = dot(query_grad_2, bd_nn[...])
        summary_grad = wide_s[:, :LANES] + wide_s[:, LANES:]
        spread_grad = summary_grad * summary * (1.0 - summary)
        spread_grad += back[here, :]
        eg[piece] = embed_grad.reshape(step, LANES, LANES)
        mix[here, :] = jnp.where(lax.rem(lane, lats) < lats // 2, logit_same, logit_other)
        for j in range(step):
            put(3, i * step + j, spread_grad[j * LANES : (j + 1) * LANES, :])

    for i in range(CHUNKS):
        contrast(i)
    halo_start(3)

    def disc_step(i, total):
        here = bins_of(i, chunk)
        return total + dot(grads_2[here, :], summ_2[here, :], 0, 0)

    disc_total = lax.fori_loop(
        0, CHUNKS, disc_step, jnp.zeros((2 * LANES, 2 * LANES), F32)
    )
    quarter = (disc_total[:LANES, :LANES] + disc_total[LANES:, :LANES]) + (
        disc_total[:LANES, LANES:] + disc_total[LANES:, LANES:]
    )
    disc_src[...] = quarter[:lats, :] + swap(quarter[lats:, :])

    def part_of(index):
        return pl.ds(pl.multiple_of(index * part, 8), part)

    def disc_1(k):
        other = lax.rem(c + k, n_col)
        return pltpu.make_async_remote_copy(
            src_ref=disc_src.at[part_of(other)],
            dst_ref=disc_a.at[c],
            send_sem=ds_sem.at[0],
            recv_sem=dr_sem.at[0],
            device_id=(r, other),
            device_id_type=MESH,
        )

    disc_a[c] = disc_src[part_of(c), :]
    peers(n_col, disc_1)

    for i in range(rows):
        flipped = mix[i * LANES : (i + 1) * LANES, :].T
        for k in range(4):
            at = k * (lats // 2)
            log_out[k, i : i + 1, :] = flipped[at : at + 1, :]
    outs[4].start()
    square = dot(lt[0:lats, :], s_low[...])
    square_high = square.astype(BF16).astype(F32)
    square2 = jnp.where(first, square_high, square - square_high).astype(BF16)
    loads[4].wait()
    loads[5].wait()
    rs0_run(
        0,
        lambda where: slope_scale
        * (dot(square2, wtwice[:, where]) - dot(lt[0:lats, :], x[:, where])),
    )

    halo_take(3)

    def to_latent_grad(i, value):
        z = lat[i]
        slope = jnp.where(z > 0, 1.0, jnp.exp(jnp.minimum(z, 0.0)))
        put(4, i, (eg[i] + value) * slope)

    stencil(3, to_latent_grad)
    halo_start(4)

    drain(disc_a, n_col, ds_sem.at[0], dr_sem.at[0])
    disc_bsrc[...] = jnp.sum(disc_a[...], axis=0)

    def disc_2(k):
        other = lax.rem(r + k, n_row)
        return pltpu.make_async_remote_copy(
            src_ref=disc_bsrc,
            dst_ref=disc_b.at[r],
            send_sem=ds_sem.at[1],
            recv_sem=dr_sem.at[1],
            device_id=(other, c),
            device_id_type=MESH,
        )

    disc_b[r] = disc_bsrc[...]
    peers(n_row, disc_2)
    halo_take(4)
    rs1_start(0)

    def to_proj_grad(i, value):
        pg_low[bins_of(i), :] = value.astype(BF16)

    stencil(4, to_proj_grad)

    def pick_back(i):
        value = dot(recv_pick_t[bins_of(i, chunk), :], pg_low[...])
        ex_src[1, pl.ds(i * (n_dev // CHUNKS), n_dev // CHUNKS)] = value.astype(BF16).reshape(
            n_dev // CHUNKS, portion, LANES
        )

    each(CHUNKS, pick_back)
    ex_start(1)
    for i in range(rows):
        here = slice(i * LANES, (i + 1) * LANES)
        flipped = pg_low[here, :].astype(F32).T
        stage[:, i, :] = flipped
        own[:, here] = flipped[:lats, :].astype(BF16)
    pg_out[...] = stage[...].astype(BF16)
    outs[5].start()

    rs1_finish(0)
    drain(disc_b, n_row, ds_sem.at[1], dr_sem.at[1])
    disc_full[c] = jnp.sum(disc_b[...], axis=0)

    def disc_3(k):
        other = lax.rem(c + k, n_col)
        return pltpu.make_async_remote_copy(
            src_ref=disc_full.at[c],
            dst_ref=disc_full.at[c],
            send_sem=ds_sem.at[2],
            recv_sem=dr_sem.at[2],
            device_id=(r, other),
            device_id_type=MESH,
        )

    peers(n_col, disc_3)

    for turn in range(ROUNDS):
        halo_finish(turn)

    lt[0:lats, :] = own[...]
    home = ex_wait(1)
    rs2_start(0)
    flipped = jnp.concatenate(
        [home[i * LANES : (i + 1) * LANES, :].astype(F32).T[lats:, :] for i in range(rows)], axis=1
    ).astype(BF16)
    lt[lats:, :] = dot(flipped, send_pick[...]).astype(BF16)

    def encoder_part(where):
        value = dot(lt[...], x[:, where])
        return value[:lats, :] + value[lats:, :]

    rs0_run(1, encoder_part)
    rs1_start(1)

    drain(disc_full, n_col, ds_sem.at[2], dr_sem.at[2])
    disc_grad = disc_full[...].reshape(lats, LANES)[:, :lats]
    disc_mean = jnp.sum(disc_grad * disc_grad) / (lats * lats)
    disc_out[...] = disc_grad * lax.rsqrt(disc_mean + 1e-06)
    outs[2].start()

    dec_sum[...] = rs2_finish(0)
    rs1_finish(1)
    rs2_start(1)
    enc_sum = rs2_finish(1)

    def norm_1(k):
        other = lax.rem(r + k, n_row)
        return pltpu.make_async_remote_copy(
            src_ref=norm_src,
            dst_ref=norm_a.at[r],
            send_sem=ns_sem.at[0],
            recv_sem=nr_sem.at[0],
            device_id=(other, c),
            device_id_type=MESH,
        )

    norm_a[r] = norm_src[...]
    peers(n_row, norm_1)
    drain(norm_a, n_row, ns_sem.at[0], nr_sem.at[0])
    totals = norm_a[0]
    for k in range(1, n_row):
        totals += norm_a[k]
    entries = genes * lats
    enc_out[...] = enc_sum * lax.rsqrt(totals[0:1, lats : lats + 1] / entries + 1e-06)
    dec_out[...] = dec_sum[...] * lax.rsqrt(totals[0:1, 0:1] / entries + 1e-06)
    outs[0].start()
    outs[1].start()
    for out in outs:
        out.wait()


def hand_on(*refs):
    count = (len(refs) - 2) // 3
    sources, targets, held = (refs[k * count : (k + 1) * count] for k in range(3))
    come, go = refs[3 * count :]
    ins = [pltpu.make_async_copy(sources[i], held[i], come.at[i]) for i in range(count)]
    outs = [pltpu.make_async_copy(held[i], targets[i], go.at[i]) for i in range(count)]
    for copy in ins:
        copy.start()
    for i in range(count):
        ins[i].wait()
        outs[i].start()
    for copy in outs:
        copy.wait()


def per_device(features, enc_weight, dec_weight, disc_weight, send_order, recv_order):
    tile_rows, tile_cols, genes = features.shape
    lats = enc_weight.shape[1]
    bins = tile_rows * tile_cols
    n_row = lax.axis_size("row")
    n_col = lax.axis_size("col")
    n_dev = n_row * n_col
    n_group = n_row // 2
    per_dev = genes // n_dev
    span = genes // n_group
    part = lats // n_col
    packed = lats + lats // 2
    portion = bins // n_dev
    field = (tile_rows, LANES, LANES)
    dma = pltpu.SemaphoreType.DMA
    vmem = pltpu.VMEM
    shape = jax.ShapeDtypeStruct
    out_shape = [
        shape((per_dev, lats), F32),
        shape((per_dev, lats), F32),
        shape((lats, lats), F32),
        shape((lats, tile_rows, tile_cols), F32),
        shape((4, tile_rows, tile_cols), F32),
        shape((2 * lats, tile_rows, tile_cols), BF16),
    ]
    scratch = [
        *(vmem(one.shape, one.dtype) for one in out_shape),
        vmem((bins, genes), BF16),
        vmem((lats, lats), F32),
        vmem((2, tile_rows, LANES), jnp.int32),
        vmem((2 * lats, genes), BF16),
        vmem((2 * lats, genes), BF16),
        vmem((LANES, LANES), BF16),
        vmem((2 * LANES, 2 * LANES), BF16),
        vmem((2 * LANES, 2 * LANES), BF16),
        vmem((bins, bins), BF16),
        vmem((bins, bins), BF16),
        vmem((bins, bins), BF16),
        vmem((bins, LANES), F32),
        vmem((LANES, bins), F32),
        vmem((2, n_dev, portion, LANES), BF16),
        vmem((2, n_dev, portion, LANES), BF16),
        vmem((bins, LANES), BF16),
        vmem((2, tile_rows + 2 * RADIUS, LANES + 2 * SIDE, LANES), F32),
        vmem((tile_rows, LANES + 2 * SIDE, LANES), F32),
        vmem((ROUNDS,) + field, BF16),
        vmem((ROUNDS, 2, RADIUS, LANES, LANES), BF16),
        vmem((ROUNDS, 2, tile_rows * SIDE, LANES), BF16),
        vmem((ROUNDS, 4, tile_rows * SIDE // 2, LANES), BF16),
        vmem((len(PACKED), 2, RADIUS, LANES // 2, LANES), BF16),
        vmem((len(PACKED), 2, RADIUS, LANES // 2, LANES), BF16),
        vmem((2, tile_rows * SIDE, LANES), F32),
        vmem((ROUNDS, 2, tile_rows * SIDE, LANES), BF16),
        vmem(field, F32),
        vmem(field, F32),
        vmem(field, F32),
        vmem(field, F32),
        vmem((bins, LANES), BF16),
        vmem((bins, LANES), F32),
        vmem((bins, 2 * LANES), BF16),
        vmem((bins, 2 * LANES), BF16),
        vmem((bins, LANES), F32),
        vmem(field, F32),
        vmem((bins, LANES), BF16),
        vmem((LANES, bins), BF16),
        vmem((lats, bins), BF16),
        vmem((2, n_group, packed, LANES), F32),
        vmem((2, n_group, packed, LANES), BF16),
        vmem((2, n_group, packed, LANES), BF16),
        vmem((2, n_group, packed, LANES), BF16),
        vmem((2, n_group, packed, LANES), BF16),
        vmem((2, packed, LANES), BF16),
        vmem((2, n_col, packed, LANES), BF16),
        vmem((lats, LANES), F32),
        vmem((n_col, part, LANES), F32),
        vmem((part, LANES), F32),
        vmem((n_row, part, LANES), F32),
        vmem((n_col, part, LANES), F32),
        vmem((1, LANES), F32),
        vmem((n_row, 1, LANES), F32),
        vmem((span // 2, lats), F32),
        vmem((LANES, tile_rows, LANES), F32),
        vmem((per_dev, lats), F32),
        dma((7,)),
        dma((tile_rows,)),
        dma((ROUNDS, 8)),
        dma((ROUNDS, 8)),
        dma((2,)),
        dma((2,)),
        dma((2, 2)),
        dma((2, 2)),
        dma((2,)),
        dma((2,)),
        dma((2,)),
        dma((2,)),
        dma((3,)),
        dma((3,)),
        dma((1,)),
        dma((1,)),
        pltpu.SemaphoreType.REGULAR,
        dma((6,)),
    ]
    anywhere = [pl.BlockSpec(memory_space=pl.ANY)] * 6
    results = pl.pallas_call(
        functools.partial(kernel, n_row, n_col),
        out_shape=out_shape,
        in_specs=anywhere,
        out_specs=anywhere,
        scratch_shapes=scratch,
        compiler_params=pltpu.CompilerParams(
            collective_id=0, has_side_effects=True, vmem_limit_bytes=56 * 1024 * 1024
        ),
    )(
        features.reshape(bins, genes),
        enc_weight.T,
        dec_weight.T,
        disc_weight,
        send_order.reshape(tile_rows, LANES),
        recv_order.reshape(tile_rows, LANES),
    )
    *others, grads = pl.pallas_call(
        hand_on,
        out_shape=out_shape,
        in_specs=anywhere,
        out_specs=anywhere,
        scratch_shapes=[*(vmem(one.shape, one.dtype) for one in out_shape), dma((6,)), dma((6,))],
    )(*results)
    return (*others, grads.reshape(2, lats, tile_rows, tile_cols))


def solution(mesh):
    in_specs = (P("row", "col", None), P(), P(), P(), P("row", "col", None), P("row", "col", None))
    out_specs = (
        P(("row", "col"), None),
        P(("row", "col"), None),
        P(),
        P(None, "row", "col"),
        P(None, "row", "col"),
        P(None, None, "row", "col"),
    )
    return jax.shard_map(
        per_device, mesh=mesh, in_specs=in_specs, out_specs=out_specs, check_vma=False
    )
```

```python
import functools
import math

import jax
import jax.numpy as jnp
from jax import lax
from jax.experimental import pallas as pl
from jax.experimental.pallas import tpu as pltpu
from jax.sharding import PartitionSpec as P

RADIUS = 3
RECON_WEIGHT = 10.0
LANES = 128
SIDE = 8
STRIDE = 37
UNROLL = 8
MESH = pl.DeviceIdType.MESH
F32 = jnp.float32
BF16 = jnp.bfloat16
DIRECTIONS = ((-1, 0), (1, 0), (0, -1), (0, 1), (-1, -1), (-1, 1), (1, -1), (1, 1))
OPPOSITE = (1, 0, 3, 2, 7, 6, 5, 4)
ROUNDS = 5
PACKED = {0: 0, 2: 1}
CHUNKS = 4


def stencil_taps():
    raw_taps = [math.exp(-offset * offset / 12.0) for offset in range(-RADIUS, RADIUS + 1)]
    tap_total = sum(raw_taps)
    return [raw_value / tap_total for raw_value in raw_taps]


def dot(a, b, ca=1, cb=0):
    return lax.dot_general(a, b, (((ca,), (cb,)), ((), ())), preferred_element_type=F32)


def each(count, body):
    def step(i, carry):
        body(i)
        return carry

    lax.fori_loop(0, count, step, 0)


def when(test):
    if isinstance(test, bool):
        return (lambda body: body()) if test else (lambda body: None)
    return pl.when(test)


def split_2(value):
    high = value.astype(BF16)
    low = (value - high.astype(F32)).astype(BF16)
    return jnp.concatenate([high, low], axis=1)


def kernel(
    n_row,
    n_col,
    feat_hbm,
    enc_hbm,
    dec_hbm,
    disc_hbm,
    send_hbm,
    recv_hbm,
    enc_hbm_out,
    dec_hbm_out,
    disc_hbm_out,
    emb_hbm_out,
    log_hbm_out,
    pg_hbm_out,
    enc_out,
    dec_out,
    disc_out,
    emb_out,
    log_out,
    pg_out,
    x,
    discw,
    orders,
    wcat,
    wtwice,
    gram2,
    bd_nt,
    bd_nn,
    send_pick,
    recv_pick,
    recv_pick_t,
    xp,
    xp_t,
    ex_src,
    ex_dst,
    low_in,
    pads,
    tmp,
    hsrc,
    h_row,
    h_col,
    h_corner,
    pack_src,
    h_pack,
    edge,
    edge_src,
    lat,
    emb,
    spread,
    summ,
    s_low,
    back,
    grads_2,
    summ_2,
    mix,
    eg,
    pg_low,
    lt,
    own,
    rs0_keep,
    rs0_src,
    rs0_dst,
    rs1_src,
    rs1_dst,
    rs2_src,
    rs2_dst,
    disc_src,
    disc_a,
    disc_bsrc,
    disc_b,
    disc_full,
    norm_src,
    norm_a,
    by_gene,
    stage,
    dec_sum,
    load_sem,
    feat_sem,
    hs_sem,
    hr_sem,
    as_sem,
    ar_sem,
    r0s_sem,
    r0r_sem,
    r1s_sem,
    r1r_sem,
    r2s_sem,
    r2r_sem,
    ds_sem,
    dr_sem,
    ns_sem,
    nr_sem,
    meet_sem,
    out_sem,
):
    n_dev = n_row * n_col
    bins, genes = x.shape
    rows = bins // LANES
    lats = discw.shape[1]
    portion = bins // n_dev
    n_group = n_row // 2
    few = min(4, n_group)
    per_dev = genes // n_dev
    span = genes // n_group
    part = lats // n_col
    slope_scale = 2.0 * RECON_WEIGHT / genes
    tap = stencil_taps()
    chunk = bins // CHUNKS

    r = lax.axis_index("row")
    c = lax.axis_index("col")
    me = r * n_col + c
    my_group = r // 2
    lane = lax.broadcasted_iota(jnp.int32, (1, LANES), 1)
    first = lane < lats

    outs = [
        pltpu.make_async_copy(a, b, out_sem.at[i])
        for i, (a, b) in enumerate(
            [
                (enc_out, enc_hbm_out),
                (dec_out, dec_hbm_out),
                (disc_out, disc_hbm_out),
                (emb_out, emb_hbm_out),
                (log_out, log_hbm_out),
                (pg_out, pg_hbm_out),
            ]
        )
    ]

    def bins_of(i, size=LANES):
        return pl.ds(i * size if isinstance(i, int) else pl.multiple_of(i * size, size), size)

    def swap(value):
        return pltpu.roll(value, lats, value.ndim - 1)

    def halo_buffer(turn, way):
        if way < 2:
            return h_row.at[turn, way]
        if way < 4:
            return h_col.at[turn, way - 2]
        return h_corner.at[turn, way - 4]

    def halo_copy(turn, way):
        dr, dc = DIRECTIONS[way]
        if way < 2 and turn in PACKED:
            source = pack_src.at[PACKED[turn], way]
            target = h_pack.at[PACKED[turn], OPPOSITE[way]]
        elif way < 2:
            source = hsrc.at[turn, pl.ds(0 if dr < 0 else rows - RADIUS, RADIUS)]
            target = halo_buffer(turn, OPPOSITE[way])
        else:
            half = rows * SIDE // 2
            source = edge_src.at[turn, 0 if dc < 0 else 1]
            if dr:
                source = source.at[pl.ds(0 if dr < 0 else half, half)]
            target = halo_buffer(turn, OPPOSITE[way])
        return pltpu.make_async_remote_copy(
            src_ref=source,
            dst_ref=target,
            send_sem=hs_sem.at[turn, way],
            recv_sem=hr_sem.at[turn, OPPOSITE[way]],
            device_id=(r + dr, c + dc),
            device_id_type=MESH,
        )

    def present(way):
        dr, dc = DIRECTIONS[way]
        tests = []
        if dr < 0:
            tests.append(r > 0)
        if dr > 0:
            tests.append(r < n_row - 1)
        if dc < 0:
            tests.append(c > 0)
        if dc > 0:
            tests.append(c < n_col - 1)
        return functools.reduce(jnp.logical_and, tests)

    def halo_start(turn):
        edge_src[turn] = edge[...].astype(BF16)
        for way in range(8):

            @pl.when(present(way))
            def _():
                halo_copy(turn, way).start()

    def halo_take(turn):
        pad = pads.at[turn % 2]
        for way in range(8):

            @pl.when(present(way))
            def _():
                halo_copy(turn, OPPOSITE[way]).wait_recv()

        left, right = slice(0, SIDE), slice(SIDE + LANES, LANES + 2 * SIDE)
        top, bottom = slice(0, RADIUS), slice(RADIUS + rows, rows + 2 * RADIUS)
        for way, part in ((0, top), (1, bottom)):
            if turn in PACKED:
                packed = h_pack[PACKED[turn], way].astype(F32)
                halves = (packed, swap(packed)) if turn == 0 else (swap(packed), packed)
                pad[part, SIDE : SIDE + LANES // 2, :] = halves[0]
                pad[part, SIDE + LANES // 2 : SIDE + LANES, :] = halves[1]
            else:
                pad[part, SIDE : SIDE + LANES, :] = h_row[turn, way].astype(F32)
            lines = slice(rows // 2 - RADIUS, rows // 2) if way == 0 else slice(0, RADIUS)
            for k, place in ((0, left), (1, right)):
                corner = h_corner[turn, 2 * way + k].astype(F32).reshape(rows // 2, SIDE, LANES)
                pad[part, place, :] = corner[lines]
        own_rows = slice(RADIUS, RADIUS + rows)
        for k, place in ((0, left), (1, right)):
            pad[own_rows, place, :] = h_col[turn, k].astype(F32).reshape(rows, SIDE, LANES)

    def halo_finish(turn):
        for way in range(8):

            @pl.when(present(way))
            def _():
                halo_copy(turn, way).wait_send()

    def stencil(turn, then):
        pad = pads.at[turn % 2]

        def down(t):
            at = pl.ds(pl.multiple_of(t * SIDE, SIDE), SIDE)
            block = pad[:, at, :]
            across = tap[RADIUS] * block[RADIUS : RADIUS + rows]
            for k in range(1, RADIUS + 1):
                across += tap[RADIUS + k] * (
                    block[RADIUS - k : RADIUS - k + rows] + block[RADIUS + k : RADIUS + k + rows]
                )
            tmp[:, at, :] = across

        def along(i):
            total = tap[RADIUS] * tmp[i, SIDE : SIDE + LANES, :]
            for k in range(1, RADIUS + 1):
                total += tap[RADIUS + k] * (
                    tmp[i, SIDE - k : SIDE - k + LANES, :] + tmp[i, SIDE + k : SIDE + k + LANES, :]
                )
            then(i, total)

        each(LANES // SIDE + 2, down)
        each(rows, along)

    def put(turn, i, value):
        pads[turn % 2, i + RADIUS, SIDE : SIDE + LANES, :] = value
        edge[0, bins_of(i, SIDE), :] = value[0:SIDE, :]
        edge[1, bins_of(i, SIDE), :] = value[LANES - SIDE :, :]
        if turn not in PACKED:
            hsrc[turn, i] = value.astype(BF16)
            return
        front, rear = value[: LANES // 2, :], value[LANES // 2 :, :]
        if turn == 0:
            packed = jnp.where(first, front, swap(rear)).astype(BF16)
        else:
            packed = jnp.where(first, swap(front), rear).astype(BF16)

        @when(i < RADIUS)
        def _():
            pack_src[PACKED[turn], 0, i] = packed

        @when(i >= rows - RADIUS)
        def _():
            pack_src[PACKED[turn], 1, i - (rows - RADIUS)] = packed

    loads = [
        pltpu.make_async_copy(a, b, load_sem.at[i])
        for i, (a, b) in enumerate(
            [
                (send_hbm, orders.at[0]),
                (recv_hbm, orders.at[1]),
                (dec_hbm, wcat.at[pl.ds(0, lats)]),
                (enc_hbm, wcat.at[pl.ds(lats, lats)]),
                (dec_hbm, wtwice.at[pl.ds(0, lats)]),
                (dec_hbm, wtwice.at[pl.ds(lats, lats)]),
                (disc_hbm, discw),
            ]
        )
    ]
    for load in loads[:4]:
        load.start()
    for i in range(rows):
        piece = pl.ds(i * LANES, LANES)
        copy = pltpu.make_async_copy(feat_hbm.at[piece], x.at[piece], feat_sem.at[i])
        copy.start()
    for load in loads[4:]:
        load.start()

    barrier = pltpu.get_barrier_semaphore()

    def greet_row(k, carry):
        other = lax.rem(r + k, n_row)
        pl.semaphore_signal(barrier, inc=1, device_id=(other, c), device_id_type=MESH)
        return carry

    def greet_col(k, carry):
        other = lax.rem(c + k, n_col)
        pl.semaphore_signal(barrier, inc=1, device_id=(r, other), device_id_type=MESH)
        return carry

    lax.fori_loop(1, n_row, greet_row, 0)
    lax.fori_loop(1, n_col, greet_col, 0)

    def build_send():
        def body(a):
            line = orders[0, pl.ds(a, 1), :].astype(F32)
            column = jnp.broadcast_to(line, (LANES, LANES)).T
            for t in range(rows):
                index = (lane + t * LANES).astype(F32)
                send_pick[bins_of(a), t * LANES : (t + 1) * LANES] = jnp.where(
                    column == index, 1.0, 0.0
                ).astype(BF16)

        each(rows, body)

    def build_recv():
        def body(a, carry):
            line = orders[1, pl.ds(a, 1), :].astype(F32)
            column = jnp.broadcast_to(line, (LANES, LANES)).T
            for t in range(rows):
                index = (lane + t * LANES).astype(F32)
                recv_pick[
                    pl.ds(pl.multiple_of(a * LANES, LANES), LANES), t * LANES : (t + 1) * LANES
                ] = jnp.where(column == index, 1.0, 0.0).astype(BF16)
            return carry

        lax.fori_loop(0, rows, body, 0)

    def build_recv_t():
        def body(t, carry):
            index = (lax.broadcasted_iota(jnp.int32, (LANES, 1), 0) + t * LANES).astype(F32)
            for a in range(rows):
                line = orders[1, a : a + 1, :].astype(F32)
                recv_pick_t[
                    pl.ds(pl.multiple_of(t * LANES, LANES), LANES), a * LANES : (a + 1) * LANES
                ] = jnp.where(line == index, 1.0, 0.0).astype(BF16)
            return carry

        lax.fori_loop(0, rows, body, 0)

    def ex_copy(which, k):
        other = lax.rem(me + k * STRIDE, n_dev)
        return pltpu.make_async_remote_copy(
            src_ref=ex_src.at[which, other],
            dst_ref=ex_dst.at[which, me],
            send_sem=as_sem.at[which],
            recv_sem=ar_sem.at[which],
            device_id=(other // n_col, lax.rem(other, n_col)),
            device_id_type=MESH,
        )

    def peers(count, make):
        def body(k, carry):
            make(k).start()
            return carry

        lax.fori_loop(1, count, body, 0)

    def drain(ref, count, send_sem, recv_sem):
        most = ref.at[pl.ds(0, count - 1)]
        pltpu.make_async_copy(most, most, recv_sem).wait()
        pltpu.make_async_copy(most, most, send_sem).wait()

    def ex_pack(values):
        values = values.reshape(-1, portion, LANES)
        half = portion // 2
        return jnp.where(first, swap(values[:, :half, :]), values[:, half:, :]).astype(BF16)

    def ex_start(which):
        def several(i):
            for k in range(UNROLL):
                ex_copy(which, i * UNROLL + k).start()

        for k in range(1, UNROLL):
            ex_copy(which, k).start()
        each(n_dev // UNROLL - 1, lambda i: several(i + 1))
        ex_dst[which, me] = ex_src[which, me]

    def ex_wait(which):
        drain(ex_dst.at[which], n_dev, as_sem.at[which], ar_sem.at[which])
        values = ex_dst[which].astype(F32)
        values = jnp.concatenate([swap(values), values], axis=1)
        return values.reshape(bins, LANES).astype(BF16)

    loads[0].wait()
    loads[1].wait()
    build_send()
    build_recv()
    for way in range(8):

        @pl.when(jnp.logical_not(present(way)))
        def _():
            for turn in range(ROUNDS):
                if way < 2 and turn in PACKED:
                    empty = h_pack.at[PACKED[turn], way]
                else:
                    empty = halo_buffer(turn, way)
                empty[...] = jnp.zeros_like(empty)

    loads[2].wait()
    loads[3].wait()

    pl.semaphore_wait(barrier, n_row + n_col - 2)

    def greet_meet(k, carry):
        other = lax.rem(c + k, n_col)
        pl.semaphore_signal(meet_sem, inc=1, device_id=(r, other), device_id_type=MESH)
        return carry

    lax.fori_loop(1, n_col, greet_meet, 0)
    for k in range(rows):
        pltpu.make_async_copy(feat_hbm.at[bins_of(k)], x.at[bins_of(k)], feat_sem.at[k]).wait()
    flat = dot(wcat[...], x[...], 1, 1)
    xp_t[...] = flat
    picked = dot(flat.astype(BF16), send_pick[...], 1, 1)
    each_dev = LANES // portion
    for i in range(rows):
        block = picked[:, i * LANES : (i + 1) * LANES].T
        ex_src[0, i * each_dev : (i + 1) * each_dev] = ex_pack(block)

    pl.semaphore_wait(meet_sem, n_col - 1)

    for i in range(rows):
        block = xp_t[:, i * LANES : (i + 1) * LANES].T
        xp[bins_of(i), :] = block
        put(0, i, swap(block.astype(BF16).astype(F32)))
    halo_start(0)
    ex_start(0)

    def elu(value):
        return jnp.where(value > 0, value, jnp.exp(jnp.minimum(value, 0.0)) - 1.0)

    def first_latent(i, value):
        lat[i] = value
        emb[i] = elu(value)

    halo_take(0)
    stencil(0, first_latent)

    low_in[...] = ex_wait(0)

    def pick_in(i):
        here = bins_of(i, chunk)
        value = dot(recv_pick[here, :], low_in[...])
        for k in range(rows // CHUNKS):
            at = i * (rows // CHUNKS) + k
            put(1, at, jnp.where(first, emb[at], value[k * LANES : (k + 1) * LANES, :]))

    each(CHUNKS, pick_in)
    halo_start(1)
    build_recv_t()
    gram = dot(wcat[0:lats, :], wcat[0:lats, :], 1, 1)
    gram_high = gram.astype(BF16)
    gram_low = (gram - gram_high.astype(F32)).astype(BF16)
    gram2[...] = jnp.zeros_like(gram2)
    gram2[0:lats, 0:lats] = gram_high
    gram2[lats:, 0:lats] = gram_low

    def first_spread(i, value):
        out = elu(value)
        lat[i] = jnp.where(first, lat[i], value)
        emb[i] = jnp.where(first, emb[i], out)
        put(2, i, out)
        spread[i] = value

    halo_take(1)
    stencil(1, first_spread)
    halo_start(2)

    def after_spread(i):
        value = spread[i]
        here = bins_of(i)
        low = value.astype(BF16).astype(F32)
        summ[i] = jax.nn.sigmoid(value)
        s_low[here, :] = jnp.where(first, low, swap(low)).astype(BF16)
        lt[0:lats, here] = low.T[0:lats, :].astype(BF16)

    each(rows, after_spread)

    back[...] = slope_scale * (
        dot(s_low[...], gram2[...]) - jnp.where(first, xp[...], 0.0)
    )

    core = lax.rem(r, 2)
    n_part = n_group // few

    def part_at(k):
        return lax.rem(my_group // few + 1 + k, n_part)

    def rs0_copy(which, k):
        here = pl.ds(part_at(k) * few, few)
        return pltpu.make_async_remote_copy(
            src_ref=rs0_src.at[which, here],
            dst_ref=rs0_dst.at[which, here],
            send_sem=r0s_sem.at[which, k],
            recv_sem=r0r_sem.at[which, k],
            device_id=(r + 1 - 2 * core, c),
            device_id_type=MESH,
        )

    def rs0_run(which, product):
        def body(k):
            part = part_at(k)
            value = product(bins_of(part, few * span))
            for j in range(few):
                at = j * span
                middle = value[:, at + LANES : at + 2 * LANES]
                top, bottom = middle[: lats // 2, :], middle[lats // 2 :, :]
                lower = jnp.concatenate(
                    [value[:, at : at + LANES], jnp.where(first, top, swap(bottom))], axis=0
                )
                upper = jnp.concatenate(
                    [value[:, at + 2 * LANES : at + span], jnp.where(first, swap(top), bottom)],
                    axis=0,
                )
                rs0_keep[which, part * few + j] = jnp.where(core == 0, lower, upper)
                rs0_src[which, part * few + j] = jnp.where(core == 0, upper, lower).astype(BF16)
            rs0_copy(which, k).start()

        each(n_part, body)

    def rs1_start(which):
        def body(k):
            rs0_copy(which, k).wait()
            for j in range(few):
                group = part_at(k) * few + j
                total = rs0_keep[which, group] + rs0_dst[which, group].astype(F32)
                rs1_src[which, group] = total.astype(BF16)

                @pl.when(group != my_group)
                def _():
                    pltpu.make_async_remote_copy(
                        src_ref=rs1_src.at[which, group],
                        dst_ref=rs1_dst.at[which, my_group],
                        send_sem=r1s_sem.at[which],
                        recv_sem=r1r_sem.at[which],
                        device_id=(2 * group + core, c),
                        device_id_type=MESH,
                    ).start()

        each(n_part, body)

    def rs1_finish(which):
        drain(rs1_dst.at[which], n_group, r1s_sem.at[which], r1r_sem.at[which])
        rs1_dst[which, my_group] = rs1_src[which, my_group]
        total = rs1_dst[which, 0].astype(F32)
        for k in range(1, n_group):
            total += rs1_dst[which, k].astype(F32)
        rs2_src[which] = total.astype(BF16)

    def rs2_copy(which, k):
        other = lax.rem(c + k, n_col)
        return pltpu.make_async_remote_copy(
            src_ref=rs2_src.at[which],
            dst_ref=rs2_dst.at[which, c],
            send_sem=r2s_sem.at[which],
            recv_sem=r2r_sem.at[which],
            device_id=(r, other),
            device_id_type=MESH,
        )

    def rs2_start(which):
        peers(n_col, functools.partial(rs2_copy, which))
        rs2_dst[which, c] = rs2_src[which]

    def rs2_finish(which):
        drain(rs2_dst.at[which], n_col, r2s_sem.at[which], r2r_sem.at[which])
        total = rs2_dst[which, 0].astype(F32)
        for k in range(1, n_col):
            total += rs2_dst[which, k].astype(F32)
        squares = jnp.broadcast_to(jnp.sum(total * total), (1, LANES))
        norm_src[...] = jnp.where(first, norm_src[...], squares) if which else squares
        pairs = total[lats:, :]
        pairs = jnp.concatenate([pairs, swap(pairs)], axis=0).T
        by_gene[pl.ds(pl.multiple_of(core * lats, lats), LANES), :] = total[:lats, :].T
        by_gene[pl.ds(pl.multiple_of((1 - core) * LANES, LANES), lats), :] = pairs[:lats, :]
        return by_gene[pl.ds(pl.multiple_of(c * per_dev, 8), per_dev), :]

    loads[6].wait()
    wide = jnp.concatenate([discw[...], jnp.zeros_like(discw)], axis=1)
    block = jnp.concatenate([wide, pltpu.roll(wide, lats, 1)], axis=0)
    block_high = block.astype(BF16)
    block_low = (block - block_high.astype(F32)).astype(BF16)
    for u in range(2):
        one = slice(u * LANES, (u + 1) * LANES)
        bd_nt[0:LANES, one] = block_high
        bd_nt[LANES:, one] = block_low
        bd_nn[one, 0:LANES] = block_high
        bd_nn[one, LANES:] = block_low
    for i in range(rows):
        stage[:, i, :] = emb[i].T
    emb_out[...] = stage[0:lats]
    outs[3].start()
    halo_take(2)

    def to_summary(i, value):
        summ[i] = jnp.where(first, summ[i], jax.nn.sigmoid(value))

    stencil(2, to_summary)

    half_sum = jnp.where(
        (lax.broadcasted_iota(jnp.int32, (LANES, LANES), 0) < lats)
        == (lax.broadcasted_iota(jnp.int32, (LANES, LANES), 1) < lats),
        1.0,
        0.0,
    ).astype(BF16)
    half_sum2 = jnp.concatenate([half_sum, half_sum], axis=0)

    step = rows // CHUNKS

    def contrast(i):
        piece = pl.ds(i * step, step)
        here = bins_of(i, chunk)
        summary = summ[piece].reshape(chunk, LANES)
        embedded = emb[piece].reshape(chunk, LANES)
        swapped = swap(embedded)
        summary_2 = split_2(summary)
        wide_q = dot(summary_2, bd_nt[...], 1, 1)
        queries = wide_q[:, :LANES] + wide_q[:, LANES:]
        logit_same = dot(split_2(embedded * queries), half_sum2)
        logit_other = dot(split_2(swapped * queries), half_sum2)
        grad_same = -jax.nn.sigmoid(-logit_same)
        grad_other = jax.nn.sigmoid(logit_other)
        embed_grad = grad_same * queries + swap(grad_other * queries)
        query_grad = grad_same * embedded + grad_other * swapped
        query_grad_2 = split_2(query_grad)
        grads_2[here, :] = query_grad_2
        summ_2[here, :] = summary_2
        wide_s = dot(query_grad_2, bd_nn[...])
        summary_grad = wide_s[:, :LANES] + wide_s[:, LANES:]
        spread_grad = summary_grad * summary * (1.0 - summary)
        spread_grad += back[here, :]
        eg[piece] = embed_grad.reshape(step, LANES, LANES)
        mix[here, :] = jnp.where(lax.rem(lane, lats) < lats // 2, logit_same, logit_other)
        for j in range(step):
            put(3, i * step + j, spread_grad[j * LANES : (j + 1) * LANES, :])

    for i in range(CHUNKS):
        contrast(i)
    halo_start(3)

    def disc_step(i, total):
        here = bins_of(i, chunk)
        return total + dot(grads_2[here, :], summ_2[here, :], 0, 0)

    disc_total = lax.fori_loop(
        0, CHUNKS, disc_step, jnp.zeros((2 * LANES, 2 * LANES), F32)
    )
    quarter = (disc_total[:LANES, :LANES] + disc_total[LANES:, :LANES]) + (
        disc_total[:LANES, LANES:] + disc_total[LANES:, LANES:]
    )
    disc_src[...] = quarter[:lats, :] + swap(quarter[lats:, :])

    def part_of(index):
        return pl.ds(pl.multiple_of(index * part, 8), part)

    def disc_1(k):
        other = lax.rem(c + k, n_col)
        return pltpu.make_async_remote_copy(
            src_ref=disc_src.at[part_of(other)],
            dst_ref=disc_a.at[c],
            send_sem=ds_sem.at[0],
            recv_sem=dr_sem.at[0],
            device_id=(r, other),
            device_id_type=MESH,
        )

    disc_a[c] = disc_src[part_of(c), :]
    peers(n_col, disc_1)

    for i in range(rows):
        flipped = mix[i * LANES : (i + 1) * LANES, :].T
        for k in range(4):
            at = k * (lats // 2)
            log_out[k, i : i + 1, :] = flipped[at : at + 1, :]
    outs[4].start()
    square = dot(lt[0:lats, :], s_low[...])
    square_high = square.astype(BF16).astype(F32)
    square2 = jnp.where(first, square_high, square - square_high).astype(BF16)
    loads[4].wait()
    loads[5].wait()
    rs0_run(
        0,
        lambda where: slope_scale
        * (dot(square2, wtwice[:, where]) - dot(lt[0:lats, :], x[:, where])),
    )

    halo_take(3)

    def to_latent_grad(i, value):
        z = lat[i]
        slope = jnp.where(z > 0, 1.0, jnp.exp(jnp.minimum(z, 0.0)))
        put(4, i, (eg[i] + value) * slope)

    stencil(3, to_latent_grad)
    halo_start(4)

    drain(disc_a, n_col, ds_sem.at[0], dr_sem.at[0])
    disc_bsrc[...] = jnp.sum(disc_a[...], axis=0)

    def disc_2(k):
        other = lax.rem(r + k, n_row)
        return pltpu.make_async_remote_copy(
            src_ref=disc_bsrc,
            dst_ref=disc_b.at[r],
            send_sem=ds_sem.at[1],
            recv_sem=dr_sem.at[1],
            device_id=(other, c),
            device_id_type=MESH,
        )

    disc_b[r] = disc_bsrc[...]
    peers(n_row, disc_2)
    halo_take(4)
    rs1_start(0)

    def to_proj_grad(i, value):
        pg_low[bins_of(i), :] = value.astype(BF16)

    stencil(4, to_proj_grad)

    def pick_back(i):
        value = dot(recv_pick_t[bins_of(i, chunk), :], pg_low[...])
        ex_src[1, pl.ds(i * (n_dev // CHUNKS), n_dev // CHUNKS)] = ex_pack(value)

    each(CHUNKS, pick_back)
    ex_start(1)
    for i in range(rows):
        here = slice(i * LANES, (i + 1) * LANES)
        flipped = pg_low[here, :].astype(F32).T
        stage[:, i, :] = flipped
        own[:, here] = flipped[:lats, :].astype(BF16)
    pg_out[...] = stage[...].astype(BF16)
    outs[5].start()

    rs1_finish(0)
    drain(disc_b, n_row, ds_sem.at[1], dr_sem.at[1])
    disc_full[c] = jnp.sum(disc_b[...], axis=0)

    def disc_3(k):
        other = lax.rem(c + k, n_col)
        return pltpu.make_async_remote_copy(
            src_ref=disc_full.at[c],
            dst_ref=disc_full.at[c],
            send_sem=ds_sem.at[2],
            recv_sem=dr_sem.at[2],
            device_id=(r, other),
            device_id_type=MESH,
        )

    peers(n_col, disc_3)

    for turn in range(ROUNDS):
        halo_finish(turn)

    lt[0:lats, :] = own[...]
    home = ex_wait(1)
    rs2_start(0)
    flipped = jnp.concatenate(
        [home[i * LANES : (i + 1) * LANES, :].astype(F32).T[lats:, :] for i in range(rows)], axis=1
    ).astype(BF16)
    lt[lats:, :] = dot(flipped, send_pick[...]).astype(BF16)

    def encoder_part(where):
        value = dot(lt[...], x[:, where])
        return value[:lats, :] + value[lats:, :]

    rs0_run(1, encoder_part)
    rs1_start(1)

    drain(disc_full, n_col, ds_sem.at[2], dr_sem.at[2])
    disc_grad = disc_full[...].reshape(lats, LANES)[:, :lats]
    disc_mean = jnp.sum(disc_grad * disc_grad) / (lats * lats)
    disc_out[...] = disc_grad * lax.rsqrt(disc_mean + 1e-06)
    outs[2].start()

    dec_sum[...] = rs2_finish(0)
    rs1_finish(1)
    rs2_start(1)
    enc_sum = rs2_finish(1)

    def norm_1(k):
        other = lax.rem(r + k, n_row)
        return pltpu.make_async_remote_copy(
            src_ref=norm_src,
            dst_ref=norm_a.at[r],
            send_sem=ns_sem.at[0],
            recv_sem=nr_sem.at[0],
            device_id=(other, c),
            device_id_type=MESH,
        )

    norm_a[r] = norm_src[...]
    peers(n_row, norm_1)
    drain(norm_a, n_row, ns_sem.at[0], nr_sem.at[0])
    totals = norm_a[0]
    for k in range(1, n_row):
        totals += norm_a[k]
    entries = genes * lats
    enc_out[...] = enc_sum * lax.rsqrt(totals[0:1, lats : lats + 1] / entries + 1e-06)
    dec_out[...] = dec_sum[...] * lax.rsqrt(totals[0:1, 0:1] / entries + 1e-06)
    outs[0].start()
    outs[1].start()
    for out in outs:
        out.wait()


def hand_on(*refs):
    count = (len(refs) - 2) // 3
    sources, targets, held = (refs[k * count : (k + 1) * count] for k in range(3))
    come, go = refs[3 * count :]
    ins = [pltpu.make_async_copy(sources[i], held[i], come.at[i]) for i in range(count)]
    outs = [pltpu.make_async_copy(held[i], targets[i], go.at[i]) for i in range(count)]
    for copy in ins:
        copy.start()
    for i in range(count):
        ins[i].wait()
        outs[i].start()
    for copy in outs:
        copy.wait()


def per_device(features, enc_weight, dec_weight, disc_weight, send_order, recv_order):
    tile_rows, tile_cols, genes = features.shape
    lats = enc_weight.shape[1]
    bins = tile_rows * tile_cols
    n_row = lax.axis_size("row")
    n_col = lax.axis_size("col")
    n_dev = n_row * n_col
    n_group = n_row // 2
    per_dev = genes // n_dev
    span = genes // n_group
    part = lats // n_col
    packed = lats + lats // 2
    portion = bins // n_dev
    field = (tile_rows, LANES, LANES)
    dma = pltpu.SemaphoreType.DMA
    vmem = pltpu.VMEM
    shape = jax.ShapeDtypeStruct
    out_shape = [
        shape((per_dev, lats), F32),
        shape((per_dev, lats), F32),
        shape((lats, lats), F32),
        shape((lats, tile_rows, tile_cols), F32),
        shape((4, tile_rows, tile_cols), F32),
        shape((2 * lats, tile_rows, tile_cols), BF16),
    ]
    scratch = [
        *(vmem(one.shape, one.dtype) for one in out_shape),
        vmem((bins, genes), BF16),
        vmem((lats, lats), F32),
        vmem((2, tile_rows, LANES), jnp.int32),
        vmem((2 * lats, genes), BF16),
        vmem((2 * lats, genes), BF16),
        vmem((LANES, LANES), BF16),
        vmem((2 * LANES, 2 * LANES), BF16),
        vmem((2 * LANES, 2 * LANES), BF16),
        vmem((bins, bins), BF16),
        vmem((bins, bins), BF16),
        vmem((bins, bins), BF16),
        vmem((bins, LANES), F32),
        vmem((LANES, bins), F32),
        vmem((2, n_dev, portion // 2, LANES), BF16),
        vmem((2, n_dev, portion // 2, LANES), BF16),
        vmem((bins, LANES), BF16),
        vmem((2, tile_rows + 2 * RADIUS, LANES + 2 * SIDE, LANES), F32),
        vmem((tile_rows, LANES + 2 * SIDE, LANES), F32),
        vmem((ROUNDS,) + field, BF16),
        vmem((ROUNDS, 2, RADIUS, LANES, LANES), BF16),
        vmem((ROUNDS, 2, tile_rows * SIDE, LANES), BF16),
        vmem((ROUNDS, 4, tile_rows * SIDE // 2, LANES), BF16),
        vmem((len(PACKED), 2, RADIUS, LANES // 2, LANES), BF16),
        vmem((len(PACKED), 2, RADIUS, LANES // 2, LANES), BF16),
        vmem((2, tile_rows * SIDE, LANES), F32),
        vmem((ROUNDS, 2, tile_rows * SIDE, LANES), BF16),
        vmem(field, F32),
        vmem(field, F32),
        vmem(field, F32),
        vmem(field, F32),
        vmem((bins, LANES), BF16),
        vmem((bins, LANES), F32),
        vmem((bins, 2 * LANES), BF16),
        vmem((bins, 2 * LANES), BF16),
        vmem((bins, LANES), F32),
        vmem(field, F32),
        vmem((bins, LANES), BF16),
        vmem((LANES, bins), BF16),
        vmem((lats, bins), BF16),
        vmem((2, n_group, packed, LANES), F32),
        vmem((2, n_group, packed, LANES), BF16),
        vmem((2, n_group, packed, LANES), BF16),
        vmem((2, n_group, packed, LANES), BF16),
        vmem((2, n_group, packed, LANES), BF16),
        vmem((2, packed, LANES), BF16),
        vmem((2, n_col, packed, LANES), BF16),
        vmem((lats, LANES), F32),
        vmem((n_col, part, LANES), F32),
        vmem((part, LANES), F32),
        vmem((n_row, part, LANES), F32),
        vmem((n_col, part, LANES), F32),
        vmem((1, LANES), F32),
        vmem((n_row, 1, LANES), F32),
        vmem((span // 2, lats), F32),
        vmem((LANES, tile_rows, LANES), F32),
        vmem((per_dev, lats), F32),
        dma((7,)),
        dma((tile_rows,)),
        dma((ROUNDS, 8)),
        dma((ROUNDS, 8)),
        dma((2,)),
        dma((2,)),
        dma((2, 2)),
        dma((2, 2)),
        dma((2,)),
        dma((2,)),
        dma((2,)),
        dma((2,)),
        dma((3,)),
        dma((3,)),
        dma((1,)),
        dma((1,)),
        pltpu.SemaphoreType.REGULAR,
        dma((6,)),
    ]
    anywhere = [pl.BlockSpec(memory_space=pl.ANY)] * 6
    results = pl.pallas_call(
        functools.partial(kernel, n_row, n_col),
        out_shape=out_shape,
        in_specs=anywhere,
        out_specs=anywhere,
        scratch_shapes=scratch,
        compiler_params=pltpu.CompilerParams(
            collective_id=0, has_side_effects=True, vmem_limit_bytes=56 * 1024 * 1024
        ),
    )(
        features.reshape(bins, genes),
        enc_weight.T,
        dec_weight.T,
        disc_weight,
        send_order.reshape(tile_rows, LANES),
        recv_order.reshape(tile_rows, LANES),
    )
    *others, grads = pl.pallas_call(
        hand_on,
        out_shape=out_shape,
        in_specs=anywhere,
        out_specs=anywhere,
        scratch_shapes=[*(vmem(one.shape, one.dtype) for one in out_shape), dma((6,)), dma((6,))],
    )(*results)
    return (*others, grads.reshape(2, lats, tile_rows, tile_cols))


def solution(mesh):
    in_specs = (P("row", "col", None), P(), P(), P(), P("row", "col", None), P("row", "col", None))
    out_specs = (
        P(("row", "col"), None),
        P(("row", "col"), None),
        P(),
        P(None, "row", "col"),
        P(None, "row", "col"),
        P(None, None, "row", "col"),
    )
    return jax.shard_map(
        per_device, mesh=mesh, in_specs=in_specs, out_specs=out_specs, check_vma=False
    )
```

```python
import functools
import math

import jax
import jax.numpy as jnp
from jax import lax
from jax.experimental import pallas as pl
from jax.experimental.pallas import tpu as pltpu
from jax.sharding import PartitionSpec as P

RADIUS = 3
RECON_WEIGHT = 10.0
LANES = 128
SIDE = 8
STRIDE = 37
UNROLL = 8
MESH = pl.DeviceIdType.MESH
F32 = jnp.float32
BF16 = jnp.bfloat16
DIRECTIONS = ((-1, 0), (1, 0), (0, -1), (0, 1), (-1, -1), (-1, 1), (1, -1), (1, 1))
OPPOSITE = (1, 0, 3, 2, 7, 6, 5, 4)
ROUNDS = 5
PACKED = {0: 0, 2: 1}
CHUNKS = 4


def stencil_taps():
    raw_taps = [math.exp(-offset * offset / 12.0) for offset in range(-RADIUS, RADIUS + 1)]
    tap_total = sum(raw_taps)
    return [raw_value / tap_total for raw_value in raw_taps]


def dot(a, b, ca=1, cb=0):
    return lax.dot_general(a, b, (((ca,), (cb,)), ((), ())), preferred_element_type=F32)


def each(count, body):
    def step(i, carry):
        body(i)
        return carry

    lax.fori_loop(0, count, step, 0)


def when(test):
    if isinstance(test, bool):
        return (lambda body: body()) if test else (lambda body: None)
    return pl.when(test)


def split_2(value):
    high = value.astype(BF16)
    low = (value - high.astype(F32)).astype(BF16)
    return jnp.concatenate([high, low], axis=1)


def kernel(
    n_row,
    n_col,
    feat_hbm,
    enc_hbm,
    dec_hbm,
    disc_hbm,
    send_hbm,
    recv_hbm,
    enc_hbm_out,
    dec_hbm_out,
    disc_hbm_out,
    emb_hbm_out,
    log_hbm_out,
    pg_hbm_out,
    enc_out,
    dec_out,
    disc_out,
    emb_out,
    log_out,
    pg_out,
    x,
    discw,
    orders,
    wcat,
    wtwice,
    gram2,
    bd_nt,
    bd_nn,
    send_pick,
    recv_pick,
    recv_pick_t,
    xp,
    xp_t,
    ex_src,
    ex_dst,
    low_in,
    pads,
    tmp,
    hsrc,
    h_row,
    h_col,
    h_corner,
    pack_src,
    h_pack,
    edge,
    edge_src,
    lat,
    emb,
    spread,
    summ,
    s_low,
    back,
    grads_2,
    summ_2,
    mix,
    eg,
    pg_low,
    lt,
    own,
    rs0_keep,
    rs0_src,
    rs0_dst,
    rs1_src,
    rs1_dst,
    rs2_src,
    rs2_dst,
    disc_src,
    disc_a,
    disc_bsrc,
    disc_b,
    disc_full,
    norm_src,
    norm_a,
    by_gene,
    stage,
    dec_sum,
    load_sem,
    feat_sem,
    hs_sem,
    hr_sem,
    as_sem,
    ar_sem,
    r0s_sem,
    r0r_sem,
    r1s_sem,
    r1r_sem,
    r2s_sem,
    r2r_sem,
    ds_sem,
    dr_sem,
    ns_sem,
    nr_sem,
    meet_sem,
    out_sem,
):
    n_dev = n_row * n_col
    bins, genes = x.shape
    rows = bins // LANES
    lats = discw.shape[1]
    portion = bins // n_dev
    n_group = n_row // 2
    few = min(4, n_group)
    per_dev = genes // n_dev
    span = genes // n_group
    part = lats // n_col
    slope_scale = 2.0 * RECON_WEIGHT / genes
    tap = stencil_taps()
    chunk = bins // CHUNKS

    r = lax.axis_index("row")
    c = lax.axis_index("col")
    me = r * n_col + c
    my_group = r // 2
    lane = lax.broadcasted_iota(jnp.int32, (1, LANES), 1)
    first = lane < lats

    outs = [
        pltpu.make_async_copy(a, b, out_sem.at[i])
        for i, (a, b) in enumerate(
            [
                (enc_out, enc_hbm_out),
                (dec_out, dec_hbm_out),
                (disc_out, disc_hbm_out),
                (emb_out, emb_hbm_out),
                (log_out, log_hbm_out),
                (pg_out, pg_hbm_out),
            ]
        )
    ]

    def bins_of(i, size=LANES):
        return pl.ds(i * size if isinstance(i, int) else pl.multiple_of(i * size, size), size)

    def swap(value):
        return pltpu.roll(value, lats, value.ndim - 1)

    def halo_buffer(turn, way):
        if way < 2:
            return h_row.at[turn, way]
        if way < 4:
            return h_col.at[turn, way - 2]
        return h_corner.at[turn, way - 4]

    def halo_copy(turn, way):
        dr, dc = DIRECTIONS[way]
        if way < 2 and turn in PACKED:
            source = pack_src.at[PACKED[turn], way]
            target = h_pack.at[PACKED[turn], OPPOSITE[way]]
        elif way < 2:
            source = hsrc.at[turn, pl.ds(0 if dr < 0 else rows - RADIUS, RADIUS)]
            target = halo_buffer(turn, OPPOSITE[way])
        else:
            half = rows * SIDE // 2
            source = edge_src.at[turn, 0 if dc < 0 else 1]
            if dr:
                source = source.at[pl.ds(0 if dr < 0 else half, half)]
            target = halo_buffer(turn, OPPOSITE[way])
        return pltpu.make_async_remote_copy(
            src_ref=source,
            dst_ref=target,
            send_sem=hs_sem.at[turn, way],
            recv_sem=hr_sem.at[turn, OPPOSITE[way]],
            device_id=(r + dr, c + dc),
            device_id_type=MESH,
        )

    def present(way):
        dr, dc = DIRECTIONS[way]
        tests = []
        if dr < 0:
            tests.append(r > 0)
        if dr > 0:
            tests.append(r < n_row - 1)
        if dc < 0:
            tests.append(c > 0)
        if dc > 0:
            tests.append(c < n_col - 1)
        return functools.reduce(jnp.logical_and, tests)

    def halo_start(turn):
        edge_src[turn] = edge[...].astype(BF16)
        for way in range(8):

            @pl.when(present(way))
            def _():
                halo_copy(turn, way).start()

    def halo_take(turn):
        pad = pads.at[turn % 2]
        for way in range(8):

            @pl.when(present(way))
            def _():
                halo_copy(turn, OPPOSITE[way]).wait_recv()

        left, right = slice(0, SIDE), slice(SIDE + LANES, LANES + 2 * SIDE)
        top, bottom = slice(0, RADIUS), slice(RADIUS + rows, rows + 2 * RADIUS)
        for way, part in ((0, top), (1, bottom)):
            if turn in PACKED:
                packed = h_pack[PACKED[turn], way].astype(F32)
                halves = (packed, swap(packed)) if turn == 0 else (swap(packed), packed)
                pad[part, SIDE : SIDE + LANES // 2, :] = halves[0]
                pad[part, SIDE + LANES // 2 : SIDE + LANES, :] = halves[1]
            else:
                pad[part, SIDE : SIDE + LANES, :] = h_row[turn, way].astype(F32)
            lines = slice(rows // 2 - RADIUS, rows // 2) if way == 0 else slice(0, RADIUS)
            for k, place in ((0, left), (1, right)):
                corner = h_corner[turn, 2 * way + k].astype(F32).reshape(rows // 2, SIDE, LANES)
                pad[part, place, :] = corner[lines]
        own_rows = slice(RADIUS, RADIUS + rows)
        for k, place in ((0, left), (1, right)):
            pad[own_rows, place, :] = h_col[turn, k].astype(F32).reshape(rows, SIDE, LANES)

    def halo_finish(turn):
        for way in range(8):

            @pl.when(present(way))
            def _():
                halo_copy(turn, way).wait_send()

    def stencil(turn, then):
        pad = pads.at[turn % 2]

        def down(t):
            at = pl.ds(pl.multiple_of(t * SIDE, SIDE), SIDE)
            block = pad[:, at, :]
            across = tap[RADIUS] * block[RADIUS : RADIUS + rows]
            for k in range(1, RADIUS + 1):
                across += tap[RADIUS + k] * (
                    block[RADIUS - k : RADIUS - k + rows] + block[RADIUS + k : RADIUS + k + rows]
                )
            tmp[:, at, :] = across

        def along(i):
            total = tap[RADIUS] * tmp[i, SIDE : SIDE + LANES, :]
            for k in range(1, RADIUS + 1):
                total += tap[RADIUS + k] * (
                    tmp[i, SIDE - k : SIDE - k + LANES, :] + tmp[i, SIDE + k : SIDE + k + LANES, :]
                )
            then(i, total)

        each(LANES // SIDE + 2, down)
        each(rows, along)

    def put(turn, i, value):
        pads[turn % 2, i + RADIUS, SIDE : SIDE + LANES, :] = value
        edge[0, bins_of(i, SIDE), :] = value[0:SIDE, :]
        edge[1, bins_of(i, SIDE), :] = value[LANES - SIDE :, :]
        if turn not in PACKED:
            hsrc[turn, i] = value.astype(BF16)
            return
        front, rear = value[: LANES // 2, :], value[LANES // 2 :, :]
        if turn == 0:
            packed = jnp.where(first, front, swap(rear)).astype(BF16)
        else:
            packed = jnp.where(first, swap(front), rear).astype(BF16)

        @when(i < RADIUS)
        def _():
            pack_src[PACKED[turn], 0, i] = packed

        @when(i >= rows - RADIUS)
        def _():
            pack_src[PACKED[turn], 1, i - (rows - RADIUS)] = packed

    loads = [
        pltpu.make_async_copy(a, b, load_sem.at[i])
        for i, (a, b) in enumerate(
            [
                (send_hbm, orders.at[0]),
                (recv_hbm, orders.at[1]),
                (dec_hbm, wcat.at[pl.ds(0, lats)]),
                (enc_hbm, wcat.at[pl.ds(lats, lats)]),
                (dec_hbm, wtwice.at[pl.ds(0, lats)]),
                (dec_hbm, wtwice.at[pl.ds(lats, lats)]),
                (disc_hbm, discw),
            ]
        )
    ]
    for load in loads[:4]:
        load.start()
    for i in range(rows):
        piece = pl.ds(i * LANES, LANES)
        copy = pltpu.make_async_copy(feat_hbm.at[piece], x.at[piece], feat_sem.at[i])
        copy.start()
    for load in loads[4:]:
        load.start()

    barrier = pltpu.get_barrier_semaphore()

    def greet_row(k, carry):
        other = lax.rem(r + k, n_row)
        pl.semaphore_signal(barrier, inc=1, device_id=(other, c), device_id_type=MESH)
        return carry

    def greet_col(k, carry):
        other = lax.rem(c + k, n_col)
        pl.semaphore_signal(barrier, inc=1, device_id=(r, other), device_id_type=MESH)
        return carry

    lax.fori_loop(1, n_row, greet_row, 0)
    lax.fori_loop(1, n_col, greet_col, 0)

    def build_send():
        def body(a):
            line = orders[0, pl.ds(a, 1), :].astype(F32)
            column = jnp.broadcast_to(line, (LANES, LANES)).T
            for t in range(rows):
                index = (lane + t * LANES).astype(F32)
                send_pick[bins_of(a), t * LANES : (t + 1) * LANES] = jnp.where(
                    column == index, 1.0, 0.0
                ).astype(BF16)

        each(rows, body)

    def build_recv():
        def body(a, carry):
            line = orders[1, pl.ds(a, 1), :].astype(F32)
            column = jnp.broadcast_to(line, (LANES, LANES)).T
            for t in range(rows):
                index = (lane + t * LANES).astype(F32)
                recv_pick[
                    pl.ds(pl.multiple_of(a * LANES, LANES), LANES), t * LANES : (t + 1) * LANES
                ] = jnp.where(column == index, 1.0, 0.0).astype(BF16)
            return carry

        lax.fori_loop(0, rows, body, 0)

    def build_recv_t():
        def body(t, carry):
            index = (lax.broadcasted_iota(jnp.int32, (LANES, 1), 0) + t * LANES).astype(F32)
            for a in range(rows):
                line = orders[1, a : a + 1, :].astype(F32)
                recv_pick_t[
                    pl.ds(pl.multiple_of(t * LANES, LANES), LANES), a * LANES : (a + 1) * LANES
                ] = jnp.where(line == index, 1.0, 0.0).astype(BF16)
            return carry

        lax.fori_loop(0, rows, body, 0)

    def ex_copy(which, k):
        other = lax.rem(me + k * STRIDE, n_dev)
        return pltpu.make_async_remote_copy(
            src_ref=ex_src.at[which, other],
            dst_ref=ex_dst.at[which, me],
            send_sem=as_sem.at[which],
            recv_sem=ar_sem.at[which],
            device_id=(other // n_col, lax.rem(other, n_col)),
            device_id_type=MESH,
        )

    def peers(count, make):
        def body(k, carry):
            make(k).start()
            return carry

        lax.fori_loop(1, count, body, 0)

    def drain(ref, count, send_sem, recv_sem):
        most = ref.at[pl.ds(0, count - 1)]
        pltpu.make_async_copy(most, most, recv_sem).wait()
        pltpu.make_async_copy(most, most, send_sem).wait()

    def ex_pack(values):
        values = values.reshape(-1, portion, LANES)
        half = portion // 2
        return jnp.where(first, swap(values[:, :half, :]), values[:, half:, :]).astype(BF16)

    def ex_start(which):
        def several(i):
            for k in range(UNROLL):
                ex_copy(which, i * UNROLL + k).start()

        for k in range(1, UNROLL):
            ex_copy(which, k).start()
        each(n_dev // UNROLL - 1, lambda i: several(i + 1))
        ex_dst[which, me] = ex_src[which, me]

    def ex_wait(which):
        drain(ex_dst.at[which], n_dev, as_sem.at[which], ar_sem.at[which])
        values = ex_dst[which].astype(F32)
        values = jnp.concatenate([swap(values), values], axis=1)
        return values.reshape(bins, LANES).astype(BF16)

    loads[0].wait()
    loads[1].wait()
    build_send()
    build_recv()
    for way in range(8):

        @pl.when(jnp.logical_not(present(way)))
        def _():
            for turn in range(ROUNDS):
                if way < 2 and turn in PACKED:
                    empty = h_pack.at[PACKED[turn], way]
                else:
                    empty = halo_buffer(turn, way)
                empty[...] = jnp.zeros_like(empty)

    loads[2].wait()
    loads[3].wait()

    pl.semaphore_wait(barrier, n_row + n_col - 2)

    def greet_meet(k, carry):
        other = lax.rem(c + k, n_col)
        pl.semaphore_signal(meet_sem, inc=1, device_id=(r, other), device_id_type=MESH)
        return carry

    lax.fori_loop(1, n_col, greet_meet, 0)
    for k in range(rows):
        pltpu.make_async_copy(feat_hbm.at[bins_of(k)], x.at[bins_of(k)], feat_sem.at[k]).wait()
    flat = dot(wcat[...], x[...], 1, 1)
    xp_t[...] = flat
    picked = dot(flat.astype(BF16), send_pick[...], 1, 1)
    each_dev = LANES // portion
    for i in range(rows):
        block = picked[:, i * LANES : (i + 1) * LANES].T
        ex_src[0, i * each_dev : (i + 1) * each_dev] = ex_pack(block)

    pl.semaphore_wait(meet_sem, n_col - 1)

    for i in range(rows):
        block = xp_t[:, i * LANES : (i + 1) * LANES].T
        xp[bins_of(i), :] = block
        put(0, i, swap(block.astype(BF16).astype(F32)))
    halo_start(0)
    ex_start(0)

    def elu(value):
        return jnp.where(value > 0, value, jnp.exp(jnp.minimum(value, 0.0)) - 1.0)

    def first_latent(i, value):
        lat[i] = value
        emb[i] = elu(value)

    halo_take(0)
    stencil(0, first_latent)

    low_in[...] = ex_wait(0)

    def pick_in(i):
        here = bins_of(i, chunk)
        value = dot(recv_pick[here, :], low_in[...])
        for k in range(rows // CHUNKS):
            at = i * (rows // CHUNKS) + k
            put(1, at, jnp.where(first, emb[at], value[k * LANES : (k + 1) * LANES, :]))

    each(CHUNKS, pick_in)
    halo_start(1)
    build_recv_t()
    gram = dot(wcat[0:lats, :], wcat[0:lats, :], 1, 1)
    gram_high = gram.astype(BF16)
    gram_low = (gram - gram_high.astype(F32)).astype(BF16)
    gram2[...] = jnp.zeros_like(gram2)
    gram2[0:lats, 0:lats] = gram_high
    gram2[lats:, 0:lats] = gram_low

    def first_spread(i, value):
        out = elu(value)
        lat[i] = jnp.where(first, lat[i], value)
        emb[i] = jnp.where(first, emb[i], out)
        put(2, i, out)
        spread[i] = value

    halo_take(1)
    stencil(1, first_spread)
    halo_start(2)

    def after_spread(i):
        value = spread[i]
        here = bins_of(i)
        low = value.astype(BF16).astype(F32)
        summ[i] = jax.nn.sigmoid(value)
        s_low[here, :] = jnp.where(first, low, swap(low)).astype(BF16)
        lt[0:lats, here] = low.T[0:lats, :].astype(BF16)

    each(rows, after_spread)

    back[...] = slope_scale * (
        dot(s_low[...], gram2[...]) - jnp.where(first, xp[...], 0.0)
    )

    core = lax.rem(r, 2)
    n_part = n_group // few

    def part_at(k):
        return lax.rem(my_group // few + 1 + k, n_part)

    def rs0_copy(which, k):
        here = pl.ds(part_at(k) * few, few)
        return pltpu.make_async_remote_copy(
            src_ref=rs0_src.at[which, here],
            dst_ref=rs0_dst.at[which, here],
            send_sem=r0s_sem.at[which, k],
            recv_sem=r0r_sem.at[which, k],
            device_id=(r + 1 - 2 * core, c),
            device_id_type=MESH,
        )

    def rs0_run(which, product):
        def body(k):
            part = part_at(k)
            value = product(bins_of(part, few * span))
            for j in range(few):
                at = j * span
                middle = value[:, at + LANES : at + 2 * LANES]
                top, bottom = middle[: lats // 2, :], middle[lats // 2 :, :]
                lower = jnp.concatenate(
                    [value[:, at : at + LANES], jnp.where(first, top, swap(bottom))], axis=0
                )
                upper = jnp.concatenate(
                    [value[:, at + 2 * LANES : at + span], jnp.where(first, swap(top), bottom)],
                    axis=0,
                )
                rs0_keep[which, part * few + j] = jnp.where(core == 0, lower, upper)
                rs0_src[which, part * few + j] = jnp.where(core == 0, upper, lower).astype(BF16)
            rs0_copy(which, k).start()

        each(n_part, body)

    def rs1_start(which):
        def body(k):
            rs0_copy(which, k).wait()
            for j in range(few):
                group = part_at(k) * few + j
                total = rs0_keep[which, group] + rs0_dst[which, group].astype(F32)
                rs1_src[which, group] = total.astype(BF16)

                @pl.when(group != my_group)
                def _():
                    pltpu.make_async_remote_copy(
                        src_ref=rs1_src.at[which, group],
                        dst_ref=rs1_dst.at[which, my_group],
                        send_sem=r1s_sem.at[which],
                        recv_sem=r1r_sem.at[which],
                        device_id=(2 * group + core, c),
                        device_id_type=MESH,
                    ).start()

        each(n_part, body)

    def rs1_finish(which):
        drain(rs1_dst.at[which], n_group, r1s_sem.at[which], r1r_sem.at[which])
        rs1_dst[which, my_group] = rs1_src[which, my_group]
        total = rs1_dst[which, 0].astype(F32)
        for k in range(1, n_group):
            total += rs1_dst[which, k].astype(F32)
        rs2_src[which] = total.astype(BF16)

    def rs2_copy(which, k):
        other = lax.rem(c + k, n_col)
        return pltpu.make_async_remote_copy(
            src_ref=rs2_src.at[which],
            dst_ref=rs2_dst.at[which, c],
            send_sem=r2s_sem.at[which],
            recv_sem=r2r_sem.at[which],
            device_id=(r, other),
            device_id_type=MESH,
        )

    def rs2_start(which):
        peers(n_col, functools.partial(rs2_copy, which))
        rs2_dst[which, c] = rs2_src[which]

    def rs2_finish(which):
        drain(rs2_dst.at[which], n_col, r2s_sem.at[which], r2r_sem.at[which])
        total = rs2_dst[which, 0].astype(F32)
        for k in range(1, n_col):
            total += rs2_dst[which, k].astype(F32)
        squares = jnp.broadcast_to(jnp.sum(total * total), (1, LANES))
        norm_src[...] = jnp.where(first, norm_src[...], squares) if which else squares
        pairs = total[lats:, :]
        pairs = jnp.concatenate([pairs, swap(pairs)], axis=0).T
        by_gene[pl.ds(pl.multiple_of(core * lats, lats), LANES), :] = total[:lats, :].T
        by_gene[pl.ds(pl.multiple_of((1 - core) * LANES, LANES), lats), :] = pairs[:lats, :]
        return by_gene[pl.ds(pl.multiple_of(c * per_dev, 8), per_dev), :]

    loads[6].wait()
    wide = jnp.concatenate([discw[...], jnp.zeros_like(discw)], axis=1)
    block = jnp.concatenate([wide, pltpu.roll(wide, lats, 1)], axis=0)
    block_high = block.astype(BF16)
    block_low = (block - block_high.astype(F32)).astype(BF16)
    for u in range(2):
        one = slice(u * LANES, (u + 1) * LANES)
        bd_nt[0:LANES, one] = block_high
        bd_nt[LANES:, one] = block_low
        bd_nn[one, 0:LANES] = block_high
        bd_nn[one, LANES:] = block_low
    for i in range(rows):
        stage[:, i, :] = emb[i].T
    emb_out[...] = stage[0:lats]
    outs[3].start()
    halo_take(2)

    def to_summary(i, value):
        summ[i] = jnp.where(first, summ[i], jax.nn.sigmoid(value))

    stencil(2, to_summary)

    half_sum = jnp.where(
        (lax.broadcasted_iota(jnp.int32, (LANES, LANES), 0) < lats)
        == (lax.broadcasted_iota(jnp.int32, (LANES, LANES), 1) < lats),
        1.0,
        0.0,
    ).astype(BF16)
    half_sum2 = jnp.concatenate([half_sum, half_sum], axis=0)

    step = rows // CHUNKS

    def contrast(i):
        piece = pl.ds(i * step, step)
        here = bins_of(i, chunk)
        summary = summ[piece].reshape(chunk, LANES)
        embedded = emb[piece].reshape(chunk, LANES)
        swapped = swap(embedded)
        summary_2 = split_2(summary)
        wide_q = dot(summary_2, bd_nt[...], 1, 1)
        queries = wide_q[:, :LANES] + wide_q[:, LANES:]
        logit_same = dot(split_2(embedded * queries), half_sum2)
        logit_other = dot(split_2(swapped * queries), half_sum2)
        grad_same = -jax.nn.sigmoid(-logit_same)
        grad_other = jax.nn.sigmoid(logit_other)
        embed_grad = grad_same * queries + swap(grad_other * queries)
        query_grad = grad_same * embedded + grad_other * swapped
        query_grad_2 = split_2(query_grad)
        grads_2[here, :] = query_grad_2
        summ_2[here, :] = summary_2
        wide_s = dot(query_grad_2, bd_nn[...])
        summary_grad = wide_s[:, :LANES] + wide_s[:, LANES:]
        spread_grad = summary_grad * summary * (1.0 - summary)
        spread_grad += back[here, :]
        eg[piece] = embed_grad.reshape(step, LANES, LANES)
        mix[here, :] = jnp.where(lax.rem(lane, lats) < lats // 2, logit_same, logit_other)
        for j in range(step):
            put(3, i * step + j, spread_grad[j * LANES : (j + 1) * LANES, :])

    for i in range(CHUNKS):
        contrast(i)
    halo_start(3)

    for i in range(rows):
        flipped = mix[i * LANES : (i + 1) * LANES, :].T
        for k in range(4):
            at = k * (lats // 2)
            log_out[k, i : i + 1, :] = flipped[at : at + 1, :]
    outs[4].start()
    square = dot(lt[0:lats, :], s_low[...])
    square_high = square.astype(BF16).astype(F32)
    square2 = jnp.where(first, square_high, square - square_high).astype(BF16)
    loads[4].wait()
    loads[5].wait()
    rs0_run(
        0,
        lambda where: slope_scale
        * (dot(square2, wtwice[:, where]) - dot(lt[0:lats, :], x[:, where])),
    )

    halo_take(3)

    def to_latent_grad(i, value):
        z = lat[i]
        slope = jnp.where(z > 0, 1.0, jnp.exp(jnp.minimum(z, 0.0)))
        put(4, i, (eg[i] + value) * slope)

    stencil(3, to_latent_grad)
    halo_start(4)

    def disc_step(i, total):
        here = bins_of(i, chunk)
        return total + dot(grads_2[here, :], summ_2[here, :], 0, 0)

    disc_total = lax.fori_loop(
        0, CHUNKS, disc_step, jnp.zeros((2 * LANES, 2 * LANES), F32)
    )
    quarter = (disc_total[:LANES, :LANES] + disc_total[LANES:, :LANES]) + (
        disc_total[:LANES, LANES:] + disc_total[LANES:, LANES:]
    )
    disc_src[...] = quarter[:lats, :] + swap(quarter[lats:, :])

    def part_of(index):
        return pl.ds(pl.multiple_of(index * part, 8), part)

    def disc_1(k):
        other = lax.rem(c + k, n_col)
        return pltpu.make_async_remote_copy(
            src_ref=disc_src.at[part_of(other)],
            dst_ref=disc_a.at[c],
            send_sem=ds_sem.at[0],
            recv_sem=dr_sem.at[0],
            device_id=(r, other),
            device_id_type=MESH,
        )

    disc_a[c] = disc_src[part_of(c), :]
    peers(n_col, disc_1)

    halo_take(4)
    rs1_start(0)

    def to_proj_grad(i, value):
        pg_low[bins_of(i), :] = value.astype(BF16)

    stencil(4, to_proj_grad)

    def pick_back(i):
        value = dot(recv_pick_t[bins_of(i, chunk), :], pg_low[...])
        ex_src[1, pl.ds(i * (n_dev // CHUNKS), n_dev // CHUNKS)] = ex_pack(value)

    each(CHUNKS, pick_back)
    ex_start(1)
    for i in range(rows):
        here = slice(i * LANES, (i + 1) * LANES)
        flipped = pg_low[here, :].astype(F32).T
        stage[:, i, :] = flipped
        own[:, here] = flipped[:lats, :].astype(BF16)
    pg_out[...] = stage[...].astype(BF16)
    outs[5].start()

    rs1_finish(0)
    drain(disc_a, n_col, ds_sem.at[0], dr_sem.at[0])
    disc_bsrc[...] = jnp.sum(disc_a[...], axis=0)

    def disc_2(k):
        other = lax.rem(r + k, n_row)
        return pltpu.make_async_remote_copy(
            src_ref=disc_bsrc,
            dst_ref=disc_b.at[r],
            send_sem=ds_sem.at[1],
            recv_sem=dr_sem.at[1],
            device_id=(other, c),
            device_id_type=MESH,
        )

    disc_b[r] = disc_bsrc[...]
    peers(n_row, disc_2)
    for turn in range(ROUNDS):
        halo_finish(turn)

    lt[0:lats, :] = own[...]
    home = ex_wait(1)
    rs2_start(0)
    flipped = jnp.concatenate(
        [home[i * LANES : (i + 1) * LANES, :].astype(F32).T[lats:, :] for i in range(rows)], axis=1
    ).astype(BF16)
    lt[lats:, :] = dot(flipped, send_pick[...]).astype(BF16)

    def encoder_part(where):
        value = dot(lt[...], x[:, where])
        return value[:lats, :] + value[lats:, :]

    rs0_run(1, encoder_part)
    rs1_start(1)

    drain(disc_b, n_row, ds_sem.at[1], dr_sem.at[1])
    disc_full[c] = jnp.sum(disc_b[...], axis=0)

    def disc_3(k):
        other = lax.rem(c + k, n_col)
        return pltpu.make_async_remote_copy(
            src_ref=disc_full.at[c],
            dst_ref=disc_full.at[c],
            send_sem=ds_sem.at[2],
            recv_sem=dr_sem.at[2],
            device_id=(r, other),
            device_id_type=MESH,
        )

    peers(n_col, disc_3)

    dec_sum[...] = rs2_finish(0)
    rs1_finish(1)
    rs2_start(1)
    drain(disc_full, n_col, ds_sem.at[2], dr_sem.at[2])
    disc_grad = disc_full[...].reshape(lats, LANES)[:, :lats]
    disc_mean = jnp.sum(disc_grad * disc_grad) / (lats * lats)
    disc_out[...] = disc_grad * lax.rsqrt(disc_mean + 1e-06)
    outs[2].start()

    enc_sum = rs2_finish(1)

    def norm_1(k):
        other = lax.rem(r + k, n_row)
        return pltpu.make_async_remote_copy(
            src_ref=norm_src,
            dst_ref=norm_a.at[r],
            send_sem=ns_sem.at[0],
            recv_sem=nr_sem.at[0],
            device_id=(other, c),
            device_id_type=MESH,
        )

    norm_a[r] = norm_src[...]
    peers(n_row, norm_1)
    drain(norm_a, n_row, ns_sem.at[0], nr_sem.at[0])
    totals = norm_a[0]
    for k in range(1, n_row):
        totals += norm_a[k]
    entries = genes * lats
    enc_out[...] = enc_sum * lax.rsqrt(totals[0:1, lats : lats + 1] / entries + 1e-06)
    dec_out[...] = dec_sum[...] * lax.rsqrt(totals[0:1, 0:1] / entries + 1e-06)
    outs[0].start()
    outs[1].start()
    for out in outs:
        out.wait()


def hand_on(*refs):
    count = (len(refs) - 2) // 3
    sources, targets, held = (refs[k * count : (k + 1) * count] for k in range(3))
    come, go = refs[3 * count :]
    ins = [pltpu.make_async_copy(sources[i], held[i], come.at[i]) for i in range(count)]
    outs = [pltpu.make_async_copy(held[i], targets[i], go.at[i]) for i in range(count)]
    for copy in ins:
        copy.start()
    for i in range(count):
        ins[i].wait()
        outs[i].start()
    for copy in outs:
        copy.wait()


def per_device(features, enc_weight, dec_weight, disc_weight, send_order, recv_order):
    tile_rows, tile_cols, genes = features.shape
    lats = enc_weight.shape[1]
    bins = tile_rows * tile_cols
    n_row = lax.axis_size("row")
    n_col = lax.axis_size("col")
    n_dev = n_row * n_col
    n_group = n_row // 2
    per_dev = genes // n_dev
    span = genes // n_group
    part = lats // n_col
    packed = lats + lats // 2
    portion = bins // n_dev
    field = (tile_rows, LANES, LANES)
    dma = pltpu.SemaphoreType.DMA
    vmem = pltpu.VMEM
    shape = jax.ShapeDtypeStruct
    out_shape = [
        shape((per_dev, lats), F32),
        shape((per_dev, lats), F32),
        shape((lats, lats), F32),
        shape((lats, tile_rows, tile_cols), F32),
        shape((4, tile_rows, tile_cols), F32),
        shape((2 * lats, tile_rows, tile_cols), BF16),
    ]
    scratch = [
        *(vmem(one.shape, one.dtype) for one in out_shape),
        vmem((bins, genes), BF16),
        vmem((lats, lats), F32),
        vmem((2, tile_rows, LANES), jnp.int32),
        vmem((2 * lats, genes), BF16),
        vmem((2 * lats, genes), BF16),
        vmem((LANES, LANES), BF16),
        vmem((2 * LANES, 2 * LANES), BF16),
        vmem((2 * LANES, 2 * LANES), BF16),
        vmem((bins, bins), BF16),
        vmem((bins, bins), BF16),
        vmem((bins, bins), BF16),
        vmem((bins, LANES), F32),
        vmem((LANES, bins), F32),
        vmem((2, n_dev, portion // 2, LANES), BF16),
        vmem((2, n_dev, portion // 2, LANES), BF16),
        vmem((bins, LANES), BF16),
        vmem((2, tile_rows + 2 * RADIUS, LANES + 2 * SIDE, LANES), F32),
        vmem((tile_rows, LANES + 2 * SIDE, LANES), F32),
        vmem((ROUNDS,) + field, BF16),
        vmem((ROUNDS, 2, RADIUS, LANES, LANES), BF16),
        vmem((ROUNDS, 2, tile_rows * SIDE, LANES), BF16),
        vmem((ROUNDS, 4, tile_rows * SIDE // 2, LANES), BF16),
        vmem((len(PACKED), 2, RADIUS, LANES // 2, LANES), BF16),
        vmem((len(PACKED), 2, RADIUS, LANES // 2, LANES), BF16),
        vmem((2, tile_rows * SIDE, LANES), F32),
        vmem((ROUNDS, 2, tile_rows * SIDE, LANES), BF16),
        vmem(field, F32),
        vmem(field, F32),
        vmem(field, F32),
        vmem(field, F32),
        vmem((bins, LANES), BF16),
        vmem((bins, LANES), F32),
        vmem((bins, 2 * LANES), BF16),
        vmem((bins, 2 * LANES), BF16),
        vmem((bins, LANES), F32),
        vmem(field, F32),
        vmem((bins, LANES), BF16),
        vmem((LANES, bins), BF16),
        vmem((lats, bins), BF16),
        vmem((2, n_group, packed, LANES), F32),
        vmem((2, n_group, packed, LANES), BF16),
        vmem((2, n_group, packed, LANES), BF16),
        vmem((2, n_group, packed, LANES), BF16),
        vmem((2, n_group, packed, LANES), BF16),
        vmem((2, packed, LANES), BF16),
        vmem((2, n_col, packed, LANES), BF16),
        vmem((lats, LANES), F32),
        vmem((n_col, part, LANES), F32),
        vmem((part, LANES), F32),
        vmem((n_row, part, LANES), F32),
        vmem((n_col, part, LANES), F32),
        vmem((1, LANES), F32),
        vmem((n_row, 1, LANES), F32),
        vmem((span // 2, lats), F32),
        vmem((LANES, tile_rows, LANES), F32),
        vmem((per_dev, lats), F32),
        dma((7,)),
        dma((tile_rows,)),
        dma((ROUNDS, 8)),
        dma((ROUNDS, 8)),
        dma((2,)),
        dma((2,)),
        dma((2, 2)),
        dma((2, 2)),
        dma((2,)),
        dma((2,)),
        dma((2,)),
        dma((2,)),
        dma((3,)),
        dma((3,)),
        dma((1,)),
        dma((1,)),
        pltpu.SemaphoreType.REGULAR,
        dma((6,)),
    ]
    anywhere = [pl.BlockSpec(memory_space=pl.ANY)] * 6
    results = pl.pallas_call(
        functools.partial(kernel, n_row, n_col),
        out_shape=out_shape,
        in_specs=anywhere,
        out_specs=anywhere,
        scratch_shapes=scratch,
        compiler_params=pltpu.CompilerParams(
            collective_id=0, has_side_effects=True, vmem_limit_bytes=56 * 1024 * 1024
        ),
    )(
        features.reshape(bins, genes),
        enc_weight.T,
        dec_weight.T,
        disc_weight,
        send_order.reshape(tile_rows, LANES),
        recv_order.reshape(tile_rows, LANES),
    )
    *others, grads = pl.pallas_call(
        hand_on,
        out_shape=out_shape,
        in_specs=anywhere,
        out_specs=anywhere,
        scratch_shapes=[*(vmem(one.shape, one.dtype) for one in out_shape), dma((6,)), dma((6,))],
    )(*results)
    return (*others, grads.reshape(2, lats, tile_rows, tile_cols))


def solution(mesh):
    in_specs = (P("row", "col", None), P(), P(), P(), P("row", "col", None), P("row", "col", None))
    out_specs = (
        P(("row", "col"), None),
        P(("row", "col"), None),
        P(),
        P(None, "row", "col"),
        P(None, "row", "col"),
        P(None, None, "row", "col"),
    )
    return jax.shard_map(
        per_device, mesh=mesh, in_specs=in_specs, out_specs=out_specs, check_vma=False
    )
```
